128 devices in a mesh: rows: 32 (over z, x, core), half: 4 (over y).
Axes of the slice: x: 4, y: 4, z: 4, core: 2. Of those that a mesh axis runs over, the one named last changes fastest.
Arguments:
- pair: bfloat16 [1024, 1024, 128], P('rows', 'half'), may hold values from -6 to 6
- pair_mask: int32 [1024, 1024], P('rows', 'half'), may hold values from 0 to 1, as said below
- gains: float32 [3, 128], replicated, may hold values from 0.1 to 1.9
- w_tri: bfloat16 [128, 640], replicated, may hold values from -0.5 to 0.5
- w_tri_out: bfloat16 [128, 128], replicated, may hold values from -0.5 to 0.5
- w_att: bfloat16 [128, 512], replicated, may hold values from -0.5 to 0.5
- w_bias: bfloat16 [128, 4], replicated, may hold values from -0.5 to 0.5
- w_att_out: bfloat16 [128, 128], replicated, may hold values from -0.5 to 0.5
Outputs:
- updated: bfloat16 [1024, 1024, 128], P('rows', 'half')
The draws below stay inside these ranges and needn't reach their ends.
Inputs may be any that keep to these rules, and one draw needn't show every extreme that they name: The last tokens of the crop are padding, between 102 and 2 * (102) of them: pair_mask[i, k] is 0 wherever token i or token k is padding. Other pairs may be 0 as well.
All inputs are finite; a program needn't handle non-finite values.
Results may differ from the reference program's by a relative error of at most 0.012.
Values may be sent and summed in bfloat16 or wider, within the bound.
No kernel may reach another device: no remote copies, remote signals or barrier semaphores. Data moves between devices by JAX's collectives and lax.ppermute only.
A program may use at most 128 MiB of HBM per device.

```python
import jax
import jax.numpy as jnp
from jax import lax

C = 128
HEADS = 4
HEAD_DIM = 32
N = 1024


def draw_pair_mask(key, part):
    key = jax.random.fold_in(key, 11)
    pad_key, drop_key = jax.random.split(key)
    padded = N // 10 + jax.random.randint(pad_key, (), 0, N // 10 + 1)
    token = (jnp.arange(N) < N - padded).astype(jnp.int32)
    kept = (jax.random.randint(drop_key, (N, N), 0, 8) < 7).astype(jnp.int32)
    return token[:, None] * token[None, :] * kept


def levels(key, shape, cuts, least, high):
    level = 1.0
    for dim, parts in cuts:
        steps = jax.random.uniform(jax.random.fold_in(jax.random.fold_in(key, 6), dim), (parts,), jnp.float32, least / len(cuts), high / len(cuts))
        level = level * jnp.repeat(jnp.exp(steps), shape[dim] // parts).reshape((-1,) + (1,) * (len(shape) - 1 - dim))
    return level


def scatter_about(rng, shape, scale, most, shards=(), dtype=jnp.bfloat16):
    loudness = levels(rng, shape, shards, -0.22, 0.18) if shards else 1.0
    values = jax.random.normal(rng, shape, jnp.float32) * scale * loudness
    return jnp.minimum(jnp.maximum(values, -most), most).astype(dtype)


def setup_inputs(seed: int = 0) -> dict:
    key_of = jax.random.split(jax.random.key(seed), 9)
    pair = scatter_about(key_of[0], (N, N, C), 1.0, 6.0, ((0, 32), (1, 4)))
    pair_mask = draw_pair_mask(jax.random.fold_in(key_of[8], 71), 0)
    gains = jnp.clip(1.0 + 0.18 * jax.random.normal(key_of[2], (3, C), jnp.float32), 0.1, 1.9)
    w_tri = scatter_about(key_of[3], (C, 5 * C), C ** -0.5, 0.5)
    w_tri_out = scatter_about(key_of[4], (C, C), C ** -0.5, 0.5)
    w_att = scatter_about(key_of[5], (C, 4 * C), C ** -0.5, 0.5)
    w_bias = scatter_about(key_of[6], (C, HEADS), C ** -0.5, 0.5)
    w_att_out = scatter_about(key_of[7], (C, C), C ** -0.5, 0.5)
    return {"pair": pair, "pair_mask": pair_mask, "gains": gains, "w_tri": w_tri, "w_tri_out": w_tri_out, "w_att": w_att, "w_bias": w_bias, "w_att_out": w_att_out}


def layer_norm(value, gain, axis):
    center = value - lax.optimization_barrier(jnp.mean(value, axis=axis, keepdims=True))
    spread = lax.optimization_barrier(jnp.mean(center * center, axis=axis, keepdims=True))
    return center * lax.rsqrt(spread + 1e-05) * gain

def reference(pair, pair_mask, gains, w_tri, w_tri_out, w_att, w_bias, w_att_out):

    def tri_inputs(items):
        pair_row, mask_row = items
        normed = layer_norm(pair_row.astype(jnp.float32), gains[0], -1).astype(jnp.bfloat16)
        mixed = jnp.dot(normed, w_tri, preferred_element_type=jnp.float32)
        weight_mask = mask_row.astype(jnp.float32)[:, None]
        left = (weight_mask * jax.nn.sigmoid(mixed[:, C:2 * C]) * mixed[:, :C]).astype(jnp.bfloat16)
        right = (weight_mask * jax.nn.sigmoid(mixed[:, 3 * C:4 * C]) * mixed[:, 2 * C:3 * C]).astype(jnp.bfloat16)
        return (left, right, jax.nn.sigmoid(mixed[:, 4 * C:]))
    left, right, gate_field = lax.map(tri_inputs, (pair, pair_mask))
    left_channels = jnp.transpose(left, (2, 0, 1))
    right_channels = jnp.transpose(right, (2, 0, 1))

    def channel_product(items):
        left_one, right_one = items
        return jnp.dot(left_one, right_one.T, preferred_element_type=jnp.float32).astype(jnp.bfloat16)
    product = jnp.transpose(lax.map(channel_product, (left_channels, right_channels)), (1, 2, 0))

    def tri_output(items):
        pair_row, product_row, gate_row = items
        normed = layer_norm(product_row.astype(jnp.float32), gains[1], -1).astype(jnp.bfloat16)
        update = jnp.dot(normed, w_tri_out, preferred_element_type=jnp.float32)
        return (pair_row.astype(jnp.float32) + gate_row * update).astype(jnp.bfloat16)
    after_mult = lax.map(tri_output, (pair, product, gate_field))

    def att_inputs(row):
        normed = layer_norm(row.astype(jnp.float32), gains[2], -1).astype(jnp.bfloat16)
        mixed = jnp.dot(normed, w_att, preferred_element_type=jnp.float32).astype(jnp.bfloat16)
        biased = jnp.dot(normed, w_bias, preferred_element_type=jnp.float32).astype(jnp.bfloat16)
        return (mixed, biased)
    projected, bias = lax.map(att_inputs, after_mult)
    bias_heads = jnp.transpose(bias, (2, 0, 1)).astype(jnp.float32)
    scale = HEAD_DIM ** (-0.5)

    def attend(items):
        base_row, mixed_row, mask_row = items
        queries = mixed_row[:, :C].reshape(N, HEADS, HEAD_DIM).astype(jnp.float32)
        keys = mixed_row[:, C:2 * C].reshape(N, HEADS, HEAD_DIM).astype(jnp.float32)
        values = mixed_row[:, 2 * C:3 * C].reshape(N, HEADS, HEAD_DIM).astype(jnp.float32)
        gates = mixed_row[:, 3 * C:].astype(jnp.float32)
        scores = jnp.einsum('jhd,khd->hjk', queries, keys) * scale + bias_heads
        scores = jnp.where(mask_row[None, None, :] > 0, scores, -1000000000.0)
        peak = lax.optimization_barrier(jnp.max(scores, axis=-1, keepdims=True))
        expo = jnp.exp(scores - peak)
        total = lax.optimization_barrier(jnp.sum(expo, axis=-1))
        rounded = lax.optimization_barrier(expo.astype(jnp.bfloat16))
        attended = jnp.einsum('hjk,khd->jhd', rounded.astype(jnp.float32), values)
        attended = attended / jnp.transpose(total)[:, :, None]
        gated = (attended.reshape(N, C) * jax.nn.sigmoid(gates)).astype(jnp.bfloat16)
        output = jnp.dot(gated, w_att_out, preferred_element_type=jnp.float32)
        return (base_row.astype(jnp.float32) + output).astype(jnp.bfloat16)
    return lax.map(attend, (after_mult, projected, pair_mask))
```

```python
import functools

import jax
import jax.numpy as jnp
from jax import lax
from jax.experimental import pallas as pl
from jax.experimental.pallas import tpu as pltpu
from jax.sharding import PartitionSpec as P

LOG2E = 1.4426950408889634
NEG = -1e30
SAFE = 100.0
AXES = ("rows", "half")
VMEM = pl.BlockSpec(memory_space=pltpu.VMEM)


def dot_nn(a, b):
    return lax.dot_general(a, b, (((1,), (0,)), ((), ())), preferred_element_type=jnp.float32)


def dot_nt(a, b):
    return lax.dot_general(a, b, (((1,), (1,)), ((), ())), preferred_element_type=jnp.float32)


def dot_tn(a, b):
    return lax.dot_general(a, b, (((0,), (0,)), ((), ())), preferred_element_type=jnp.float32)


def layer_norm(value, gain, axis):
    center = value - jnp.mean(value, axis=axis, keepdims=True)
    spread = jnp.mean(center * center, axis=axis, keepdims=True)
    return center * lax.rsqrt(spread + 1e-05) * gain


def edges_kernel(pair_ref, mask_ref, gain_ref, wt_ref, out_ref, scr):
    group, cols, width = pair_ref.shape
    gain = gain_ref[0:1, :]

    def row(i, carry):
        x = pair_ref[i].astype(jnp.float32)
        normed = layer_norm(x, gain, -1).astype(jnp.bfloat16)
        mixed = dot_nt(wt_ref[...], normed)
        m = mask_ref[pl.ds(i, 1), :]
        left = m * jax.nn.sigmoid(mixed[width : 2 * width]) * mixed[:width]
        right = m * jax.nn.sigmoid(mixed[3 * width :]) * mixed[2 * width : 3 * width]
        for e, edge in enumerate((left, right)):
            for s in range(cols // 128):
                scr[e, s, pl.ds(i, width, stride=group), :] = edge[:, s * 128 : (s + 1) * 128]
        return carry

    lax.fori_loop(0, group, row, 0, unroll=2)
    for e in range(2):
        for s in range(cols // 128):
            out_ref[:, e, :, s * 128 : (s + 1) * 128] = (
                scr[e, s].reshape(width, group, 128).astype(jnp.bfloat16)
            )


def edges(pair, mask, gains, wt, group=16):
    rows, cols, width = pair.shape
    return pl.pallas_call(
        edges_kernel,
        grid=(rows // group,),
        out_shape=jax.ShapeDtypeStruct((width, 2, rows, cols), jnp.bfloat16),
        in_specs=[
            pl.BlockSpec((group, cols, width), lambda i: (i, 0, 0)),
            pl.BlockSpec((group, cols), lambda i: (i, 0)),
            VMEM,
            VMEM,
        ],
        out_specs=pl.BlockSpec((width, 2, group, cols), lambda i: (0, 0, i, 0)),
        scratch_shapes=[pltpu.VMEM((2, cols // 128, width * group, 128), jnp.float32)],
        compiler_params=pltpu.CompilerParams(vmem_limit_bytes=48 << 20),
    )(pair, mask, gains, wt)


def product_kernel(lr_ref, out_ref):
    blocks, halves, _, rows, cols = lr_ref.shape
    step = 256 // rows

    def tile(t, carry):
        acc = None
        for h in range(halves):
            left = lr_ref[pl.ds(t * step, step), h, 0].reshape(step * rows, cols)
            right = lr_ref[:, h, 1].reshape(blocks * rows, cols)
            part = dot_nt(left, right)
            acc = part if acc is None else acc + part
        for h in range(halves):
            out_ref[pl.ds(t * step, step), h] = (
                acc[:, h * cols : (h + 1) * cols].reshape(step, rows, cols).astype(jnp.bfloat16)
            )
        return carry

    lax.fori_loop(0, blocks // step, tile, 0)


def product(lr):
    blocks, halves, _, rows, cols = lr.shape
    return pl.pallas_call(
        product_kernel,
        out_shape=jax.ShapeDtypeStruct((blocks, halves, rows, cols), jnp.bfloat16),
        in_specs=[VMEM],
        out_specs=VMEM,
        compiler_params=pltpu.CompilerParams(vmem_limit_bytes=48 << 20),
    )(lr)


def output_kernel(prod_ref, pair_ref, mask_ref, gain_ref, gcol_ref, w4_ref, wo_ref, wb_ref, out_ref, bias_ref, scr):
    width, rows, cols = prod_ref.shape
    heads = bias_ref.shape[1]
    for s in range(cols // 128):
        for c in range(0, width, 16):
            part = prod_ref[c : c + 16, :, s * 128 : (s + 1) * 128].astype(jnp.float32)
            scr[s, c * rows : (c + 16) * rows, :] = part.reshape(16 * rows, 128)

    def row(i, carry):
        x = jnp.concatenate(
            [scr[s, pl.ds(i, width, stride=rows), :] for s in range(cols // 128)], axis=1
        )
        normed = layer_norm(x, gcol_ref[...], 0).astype(jnp.bfloat16)
        update = dot_tn(normed, wo_ref[...])
        p = pair_ref[i].astype(jnp.float32)
        pn = layer_norm(p, gain_ref[0:1, :], -1).astype(jnp.bfloat16)
        gate = jax.nn.sigmoid(dot_nn(pn, w4_ref[...]))
        after = (p + gate * update).astype(jnp.bfloat16)
        out_ref[i] = after
        a = layer_norm(after.astype(jnp.float32), gain_ref[2:3, :], -1).astype(jnp.bfloat16)
        bias = dot_nt(wb_ref[...], a) * LOG2E
        bias_ref[i] = bias[:heads].astype(jnp.bfloat16)
        return carry

    lax.fori_loop(0, rows, row, 0, unroll=2)
    out_ref[rows, : mask_ref.shape[0], :] = mask_ref[...]
    out_ref[rows, mask_ref.shape[0] :, :] = jnp.zeros_like(out_ref[rows, mask_ref.shape[0] :, :])


def tri_output(prod, pair, mask_flat, gains, gcol, w4, wo, wb, heads):
    width, rows, cols = prod.shape
    return pl.pallas_call(
        output_kernel,
        out_shape=(
            jax.ShapeDtypeStruct((rows + 1, cols, width), jnp.bfloat16),
            jax.ShapeDtypeStruct((rows, heads, cols), jnp.bfloat16),
        ),
        in_specs=[VMEM] * 8,
        out_specs=(VMEM, VMEM),
        scratch_shapes=[pltpu.VMEM((cols // 128, width * rows, 128), jnp.float32)],
        compiler_params=pltpu.CompilerParams(vmem_limit_bytes=48 << 20),
    )(prod, pair, mask_flat, gains, gcol, w4, wo, wb)


def attention_kernel(
    halves, me_ref, bias_ref, gain_ref, wqg_ref, wkv_ref, wo_ref, e_ref, *refs
):
    xs, masks = refs[:halves], refs[halves : 2 * halves]
    out_ref, b32, bmax, mrow, qm, ks, vs, gs, at = refs[2 * halves :]
    i = pl.program_id(0)
    _, cols, width = xs[0].shape
    heads = b32.shape[0]
    hd = width // heads
    lane = lax.broadcasted_iota(jnp.int32, (1, width), 1)
    me = me_ref[0]
    sub = bias_ref.shape[3]

    @pl.when(i == 0)
    def _():
        big = jnp.zeros((8, 128), jnp.float32)
        for s in range(halves):
            kb = lax.rem(me + halves - s, halves)

            def put(t, big):
                for h in range(heads):
                    b = bias_ref[kb, t, h].astype(jnp.float32)
                    b32[h, pl.ds(pl.multiple_of(t * sub, sub), sub), s * cols : (s + 1) * cols] = b
                    big = jnp.maximum(
                        big, jnp.max(jnp.abs(b).reshape(sub // 8, 8, cols // 128, 128), axis=(0, 2))
                    )
                return big

            big = lax.fori_loop(0, bias_ref.shape[1], put, big)
            mrow[s] = masks[s][0, : mrow.shape[1], :].astype(jnp.float32)
            vs[s * cols : (s + 1) * cols, width:] = jnp.ones((cols, width), jnp.bfloat16)
        bmax[0] = jnp.max(big)

    parts = []
    for s in range(halves):
        a = layer_norm(xs[s][0].astype(jnp.float32), gain_ref[2:3, :], -1).astype(jnp.bfloat16)
        kv = dot_nn(a, wkv_ref[...]).astype(jnp.bfloat16)
        ks[s * cols : (s + 1) * cols, :] = kv[:, :width]
        vs[s * cols : (s + 1) * cols, :width] = kv[:, width:]
        parts.append(jnp.max(jnp.abs(kv[:, :width]), axis=0, keepdims=True))
        if s == 0:
            qg = dot_nn(a, wqg_ref[...])
            q = (qg[:, :width] * (LOG2E * hd**-0.5)).astype(jnp.bfloat16)
            gs[...] = jax.nn.sigmoid(qg[:, width:])
            for h in range(heads):
                on = jnp.broadcast_to(lane // hd == h, q.shape)
                qm[h] = jnp.where(on, q, jnp.zeros_like(q))
    kmax = functools.reduce(jnp.maximum, parts).astype(jnp.float32)
    reach = dot_nn((jnp.abs(q).astype(jnp.float32) * kmax).astype(jnp.bfloat16), e_ref[...])
    bound = jnp.max(reach) * 1.02 + bmax[0]
    step = cols // 128
    rows_m = [mrow[s, pl.ds(i * step, step), :] for s in range(halves)]
    mline = jnp.concatenate([r[t : t + 1] for r in rows_m for t in range(step)], axis=1)
    used = jnp.max(mline) > 0.0
    madd = jnp.where(mline > 0.0, 0.0, NEG)

    def attend(shift):
        num = jnp.zeros((cols, width), jnp.float32)
        den = jnp.ones((cols, width), jnp.float32)
        for h in range(heads):
            scores = dot_nt(qm[h], ks[...]) + b32[h] + madd
            if shift:
                scores = scores - jnp.max(scores, axis=-1, keepdims=True)
            weights = jnp.exp2(scores).astype(jnp.bfloat16)
            both = dot_nn(weights, vs[...])
            on = lane // hd == h
            num = jnp.where(on, both[:, :width], num)
            den = jnp.where(on, both[:, width:], den)
        at[...] = num / den

    @pl.when(used & (bound < SAFE))
    def _():
        attend(False)

    @pl.when(used & jnp.logical_not(bound < SAFE))
    def _():
        attend(True)

    @pl.when(jnp.logical_not(used))
    def _():
        mean = jnp.mean(vs[:, :width].astype(jnp.float32), axis=0, keepdims=True)
        at[...] = jnp.broadcast_to(mean, at.shape)

    gated = (at[...] * gs[...]).astype(jnp.bfloat16)
    out = dot_nn(gated, wo_ref[...])
    out_ref[0] = (xs[0][0].astype(jnp.float32) + out).astype(jnp.bfloat16)


def attention(me, bias, gains, wqg, wkv, wo, blocks):
    halves, _, heads, sub, _ = bias.shape
    rows, cols, width = blocks[0].shape
    rows -= 1
    lanes = jnp.arange(width) // (width // heads)
    e = (lanes[:, None] == lanes[None, :]).astype(jnp.bfloat16)
    keys = halves * cols
    step = cols // 128
    return pl.pallas_call(
        functools.partial(attention_kernel, halves),
        grid=(rows,),
        out_shape=jax.ShapeDtypeStruct((rows, cols, width), jnp.bfloat16),
        in_specs=[pl.BlockSpec(memory_space=pltpu.SMEM)]
        + [VMEM] * 6
        + [pl.BlockSpec((1, cols, width), lambda i: (i, 0, 0))] * halves
        + [pl.BlockSpec((1, cols, width), lambda i: (rows, 0, 0))] * halves,
        out_specs=pl.BlockSpec((1, cols, width), lambda i: (i, 0, 0)),
        scratch_shapes=[
            pltpu.VMEM((heads, cols, keys), jnp.float32),
            pltpu.SMEM((1,), jnp.float32),
            pltpu.VMEM((halves, rows * step, 128), jnp.float32),
            pltpu.VMEM((heads, cols, width), jnp.bfloat16),
            pltpu.VMEM((keys, width), jnp.bfloat16),
            pltpu.VMEM((keys, 2 * width), jnp.bfloat16),
            pltpu.VMEM((cols, width), jnp.float32),
            pltpu.VMEM((cols, width), jnp.float32),
        ],
        compiler_params=pltpu.CompilerParams(vmem_limit_bytes=56 << 20),
    )(me, bias, gains, wqg, wkv, wo, e, *blocks, *blocks)


def shards(sizes, pair, pair_mask, gains, w_tri, w_tri_out, w_att, w_bias, w_att_out):
    n_rows, halves = sizes
    rows, cols, width = pair.shape
    heads = w_bias.shape[1]
    mask = pair_mask.astype(jnp.float32)
    lr = edges(pair, mask, gains, w_tri[:, : 4 * width].T)
    lr = lax.all_to_all(lr, AXES, split_axis=0, concat_axis=0, tiled=True)
    prod = product(lr.reshape(n_rows, halves, 2, rows, cols))
    back = lax.all_to_all(
        prod.reshape(width, rows, cols), AXES, split_axis=0, concat_axis=0, tiled=True
    )
    wb = jnp.pad(w_bias.T, ((0, 8 - heads), (0, 0)))
    after, bias = tri_output(
        back,
        pair,
        mask.astype(jnp.bfloat16).reshape(rows * cols // width, width),
        gains,
        gains[1][:, None],
        w_tri[:, 4 * width :],
        w_tri_out,
        wb,
        heads,
    )
    blocks = [after]
    for s in range(1, halves):
        blocks.append(lax.ppermute(after, "half", [(y, (y + s) % halves) for y in range(halves)]))
    inner = n_rows // halves
    swap = [
        ((z * inner + k) * halves + y, (y * inner + k) * halves + z)
        for z in range(halves)
        for k in range(inner)
        for y in range(halves)
    ]
    bias = jnp.swapaxes(bias, 0, 1)
    bias = lax.ppermute(bias, AXES, swap)
    bias = lax.all_gather(bias, "rows", axis=0, tiled=False)
    bias = bias.reshape(halves, inner, heads, rows, cols)
    me = lax.axis_index("half").astype(jnp.int32).reshape(1)
    wqg = jnp.concatenate([w_att[:, :width], w_att[:, 3 * width :]], axis=1)
    wkv = w_att[:, width : 3 * width]
    return attention(me, bias, gains, wqg, wkv, w_att_out, blocks)


def solution(mesh):
    sizes = (mesh.shape["rows"], mesh.shape["half"])
    in_specs = (P("rows", "half", None), P("rows", "half"), P(), P(), P(), P(), P(), P())
    out_specs = P("rows", "half", None)
    return jax.shard_map(
        functools.partial(shards, sizes),
        mesh=mesh,
        in_specs=in_specs,
        out_specs=out_specs,
        check_vma=False,
    )
```

```python
import functools

import jax
import jax.numpy as jnp
from jax import lax
from jax.experimental import pallas as pl
from jax.experimental.pallas import tpu as pltpu
from jax.sharding import PartitionSpec as P

LOG2E = 1.4426950408889634
NEG = -1e30
SAFE = 100.0
AXES = ("rows", "half")
VMEM = pl.BlockSpec(memory_space=pltpu.VMEM)
SMEM = pl.BlockSpec(memory_space=pltpu.SMEM)
PARAMS = pltpu.CompilerParams(vmem_limit_bytes=52 << 20)
CHUNKS = 2


def dot_nn(a, b):
    return lax.dot_general(a, b, (((1,), (0,)), ((), ())), preferred_element_type=jnp.float32)


def dot_nt(a, b):
    return lax.dot_general(a, b, (((1,), (1,)), ((), ())), preferred_element_type=jnp.float32)


def dot_tn(a, b):
    return lax.dot_general(a, b, (((0,), (0,)), ((), ())), preferred_element_type=jnp.float32)


def sigmoid(x):
    return 0.5 * jnp.tanh(0.5 * x) + 0.5


def averager(width):
    return jnp.full((width, width), 1.0 / width, jnp.bfloat16)


def norm_lanes(x, gain):
    avg = averager(x.shape[-1])
    center = x.astype(jnp.float32) - dot_nn(x, avg)
    spread = dot_nn((center * center).astype(jnp.bfloat16), avg)
    return (center * lax.rsqrt(spread + 1e-05) * gain).astype(jnp.bfloat16)


def norm_sublanes(x, gain):
    avg = averager(x.shape[0])
    center = x.astype(jnp.float32) - dot_nn(avg, x)
    spread = dot_nn(avg, (center * center).astype(jnp.bfloat16))
    return (center * lax.rsqrt(spread + 1e-05) * gain).astype(jnp.bfloat16)


def edges_kernel(pair_ref, mask_ref, gain_ref, wt_ref, out_ref, scr):
    group, cols, width = pair_ref.shape
    gain = gain_ref[0:1, :]

    def row(i, carry):
        normed = norm_lanes(pair_ref[i], gain)
        mixed = dot_nt(wt_ref[...], normed)
        m = mask_ref[pl.ds(i, 1), :]
        left = m * sigmoid(mixed[width : 2 * width]) * mixed[:width]
        right = m * sigmoid(mixed[3 * width :]) * mixed[2 * width : 3 * width]
        for e, edge in enumerate((left, right)):
            for s in range(cols // 128):
                scr[e, s, pl.ds(i, width, stride=group), :] = edge[:, s * 128 : (s + 1) * 128]
        return carry

    lax.fori_loop(0, group, row, 0, unroll=EDGE_UNROLL)
    for e in range(2):
        for s in range(cols // 128):
            out_ref[:, e, :, s * 128 : (s + 1) * 128] = (
                scr[e, s].reshape(width, group, 128).astype(jnp.bfloat16)
            )


EDGE_UNROLL = 4


def edges(pair, mask, gains, wt, group=16):
    rows, cols, width = pair.shape
    return pl.pallas_call(
        edges_kernel,
        grid=(rows // group,),
        out_shape=jax.ShapeDtypeStruct((width, 2, rows, cols), jnp.bfloat16),
        in_specs=[
            pl.BlockSpec((group, cols, width), lambda i: (i, 0, 0)),
            pl.BlockSpec((group, cols), lambda i: (i, 0)),
            VMEM,
            VMEM,
        ],
        out_specs=pl.BlockSpec((width, 2, group, cols), lambda i: (0, 0, i, 0)),
        scratch_shapes=[pltpu.VMEM((2, cols // 128, width * group, 128), jnp.float32)],
        compiler_params=PARAMS,
    )(pair, mask, gains, wt)


def gate_kernel(pair_ref, gain_ref, w4_ref, out_ref):
    for i in range(pair_ref.shape[0]):
        normed = norm_lanes(pair_ref[i], gain_ref[0:1, :])
        out_ref[i] = sigmoid(dot_nn(normed, w4_ref[...])).astype(jnp.bfloat16)


def gate(pair, gains, w4, group=4):
    rows, cols, width = pair.shape
    block = pl.BlockSpec((group, cols, width), lambda i: (i, 0, 0))
    return pl.pallas_call(
        gate_kernel,
        grid=(rows // group,),
        out_shape=jax.ShapeDtypeStruct(pair.shape, jnp.bfloat16),
        in_specs=[block, VMEM, VMEM],
        out_specs=block,
        compiler_params=PARAMS,
        cost_estimate=pl.CostEstimate(
            flops=6 * rows * cols * width * width,
            bytes_accessed=4 * rows * cols * width,
            transcendentals=rows * cols * width,
        ),
    )(pair, gains, w4)


PRODUCT_ROWS = 512


def product_kernel(lr_ref, out_ref):
    blocks, halves, _, rows, cols = lr_ref.shape
    step = PRODUCT_ROWS // rows

    def tile(t, carry):
        acc = None
        for h in range(halves):
            left = lr_ref[pl.ds(t * step, step), h, 0].reshape(step * rows, cols)
            right = lr_ref[:, h, 1].reshape(blocks * rows, cols)
            part = dot_nt(left, right)
            acc = part if acc is None else acc + part
        for h in range(halves):
            out_ref[pl.ds(t * step, step), h] = (
                acc[:, h * cols : (h + 1) * cols].reshape(step, rows, cols).astype(jnp.bfloat16)
            )
        return carry

    lax.fori_loop(0, blocks // step, tile, 0)


def product(lr):
    blocks, halves, _, rows, cols = lr.shape
    return pl.pallas_call(
        product_kernel,
        out_shape=jax.ShapeDtypeStruct((blocks, halves, rows, cols), jnp.bfloat16),
        in_specs=[VMEM],
        out_specs=VMEM,
        compiler_params=PARAMS,
    )(lr)


OUT_UNROLL = 4


def output_kernel(prod_ref, pair_ref, gate_ref, mask_ref, gain_ref, gcol_ref, wo_ref, wb_ref, *refs):
    outs, bias_ref, scr = refs[:CHUNKS], refs[CHUNKS], refs[CHUNKS + 1]
    width, rows, cols = prod_ref.shape
    heads = bias_ref.shape[1]
    per = rows // CHUNKS
    for s in range(cols // 128):
        for c in range(0, width, 16):
            part = prod_ref[c : c + 16, :, s * 128 : (s + 1) * 128].astype(jnp.float32)
            scr[s, c * rows : (c + 16) * rows, :] = part.reshape(16 * rows, 128)

    for c in range(CHUNKS):

        def row(k, carry, c=c):
            i = c * per + k
            x = jnp.concatenate(
                [scr[s, pl.ds(i, width, stride=rows), :] for s in range(cols // 128)], axis=1
            )
            normed = norm_sublanes(x.astype(jnp.bfloat16), gcol_ref[...])
            update = dot_tn(normed, wo_ref[...])
            after = pair_ref[i].astype(jnp.float32) + gate_ref[i].astype(jnp.float32) * update
            after = after.astype(jnp.bfloat16)
            outs[c][k] = after
            a = norm_lanes(after, gain_ref[2:3, :])
            bias = dot_nt(wb_ref[...], a) * LOG2E
            bias_ref[i] = bias[:heads].astype(jnp.bfloat16)
            return carry

        lax.fori_loop(0, per, row, 0, unroll=OUT_UNROLL)
        used = per * cols // width
        outs[c][per, :used, :] = mask_ref[c * used : (c + 1) * used, :]
        outs[c][per, used:, :] = jnp.zeros((cols - used, width), jnp.bfloat16)


def tri_output(prod, pair, gates, mask_flat, gains, gcol, wo, wb, heads):
    width, rows, cols = prod.shape
    part = jax.ShapeDtypeStruct((rows // CHUNKS + 1, cols, width), jnp.bfloat16)
    return pl.pallas_call(
        output_kernel,
        out_shape=(part,) * CHUNKS + (jax.ShapeDtypeStruct((rows, heads, cols), jnp.bfloat16),),
        in_specs=[VMEM] * 8,
        out_specs=(VMEM,) * (CHUNKS + 1),
        scratch_shapes=[pltpu.VMEM((cols // 128, width * rows, 128), jnp.float32)],
        compiler_params=PARAMS,
    )(prod, pair, gates, mask_flat, gains, gcol, wo, wb)


def project_kernel(gain_ref, w_ref, *refs):
    width = gain_ref.shape[1]
    xs = refs[:-5]
    q_ref, g_ref, k_ref, v_ref, m_ref = refs[-5:]
    group, cols, _ = xs[0].shape
    scale = LOG2E * HEAD_DIM**-0.5
    for r in range(group):
        top = None
        for b, x_ref in enumerate(xs):
            a = norm_lanes(x_ref[r], gain_ref[2:3, :])
            at = slice(b * cols, (b + 1) * cols)
            if b == 0:
                mixed = dot_nn(a, w_ref[...])
                q_ref[r] = (mixed[:, :width] * scale).astype(jnp.bfloat16)
                g_ref[r] = sigmoid(mixed[:, 3 * width :]).astype(jnp.bfloat16)
                kv = mixed[:, width : 3 * width].astype(jnp.bfloat16)
            else:
                kv = dot_nn(a, w_ref[:, width : 3 * width]).astype(jnp.bfloat16)
            k_ref[r, at, :] = kv[:, :width]
            v_ref[r, at, :] = kv[:, width:]
            m = jnp.max(jnp.abs(kv[:, :width]), axis=0, keepdims=True).astype(jnp.float32)
            top = m if top is None else jnp.maximum(top, m)
        m_ref[r] = jnp.broadcast_to(top, m_ref.shape[1:])


HEAD_DIM = 32


def project(blocks, gains, w, group=4):
    rows, cols, width = blocks[0].shape
    rows -= 1
    n = len(blocks)
    one = lambda c: pl.BlockSpec((group, c, width), lambda i: (i, 0, 0))
    shape = lambda c: jax.ShapeDtypeStruct((rows, c, width), jnp.bfloat16)
    return pl.pallas_call(
        project_kernel,
        grid=(rows // group,),
        out_shape=(shape(cols), shape(cols), shape(n * cols), shape(n * cols), jax.ShapeDtypeStruct((rows, 8, width), jnp.float32)),
        in_specs=[VMEM, VMEM] + [one(cols)] * n,
        out_specs=(one(cols), one(cols), one(n * cols), one(n * cols), one(8)),
        compiler_params=PARAMS,
        cost_estimate=pl.CostEstimate(
            flops=8 * n * rows * cols * width * width,
            bytes_accessed=8 * n * rows * cols * width,
            transcendentals=rows * cols * width,
        ),
    )(gains, w, *blocks)


def project_last_kernel(gain_ref, w_ref, e_ref, x_ref, q_ref, top_ref, k_ref, v_ref, m_ref):
    width = gain_ref.shape[1]
    for r in range(x_ref.shape[0]):
        a = norm_lanes(x_ref[r], gain_ref[2:3, :])
        kv = dot_nn(a, w_ref[:, width : 3 * width]).astype(jnp.bfloat16)
        k_ref[r] = kv[:, :width]
        v_ref[r] = kv[:, width:]
        m = jnp.max(jnp.abs(kv[:, :width]), axis=0, keepdims=True).astype(jnp.float32)
        top = jnp.maximum(m, top_ref[r, 0:1, :])
        reach = dot_nn((jnp.abs(q_ref[r]).astype(jnp.float32) * top).astype(jnp.bfloat16), e_ref[...])
        m_ref[r] = jnp.broadcast_to(jnp.max(reach, axis=0, keepdims=True), m_ref.shape[1:])


def project_last(block, q, top, gains, w, group=4):
    rows, cols, width = q.shape
    lanes = jnp.arange(width) // HEAD_DIM
    e = (lanes[:, None] == lanes[None, :]).astype(jnp.bfloat16)
    one = lambda c: pl.BlockSpec((group, c, width), lambda i: (i, 0, 0))
    shape = jax.ShapeDtypeStruct((rows, cols, width), jnp.bfloat16)
    return pl.pallas_call(
        project_last_kernel,
        grid=(rows // group,),
        out_shape=(shape, shape, jax.ShapeDtypeStruct((rows, 8, width), jnp.float32)),
        in_specs=[VMEM] * 3 + [one(cols), one(cols), one(8)],
        out_specs=(one(cols), one(cols), one(8)),
        compiler_params=PARAMS,
        cost_estimate=pl.CostEstimate(
            flops=10 * rows * cols * width * width,
            bytes_accessed=8 * rows * cols * width,
            transcendentals=0,
        ),
    )(gains, w, e, block, q, top)


def attention_kernel(halves, me_ref, bias_ref, wo_ref, reach_ref, *refs):
    q_ref, g_ref, x_ref, ka_ref, va_ref, kb_ref, vb_ref = refs[:7]
    masks = refs[7 : 7 + halves]
    out_ref, flags, mrow, vs = refs[7 + halves :]
    i = pl.program_id(0)
    group, cols, width = q_ref.shape
    heads = bias_ref.shape[2]
    lane = lax.broadcasted_iota(jnp.int32, (1, width), 1)
    me = me_ref[0]
    where = [lax.rem(me + s, halves) for s in (0, halves - 1, 1, 2)]
    step = cols // 128
    count = mrow.shape[1] // step

    @pl.when(i == 0)
    def _():
        def big(t, top):
            b = jnp.abs(bias_ref[t // bias_ref.shape[1], lax.rem(t, bias_ref.shape[1])])
            return jnp.maximum(top, b)

        top = lax.fori_loop(
            0, halves * bias_ref.shape[1], big, jnp.zeros(bias_ref.shape[2:], jnp.bfloat16)
        )
        bound = jnp.max(reach_ref[...]) * 1.02 + jnp.max(top.astype(jnp.float32))
        flags[0] = (bound < SAFE).astype(jnp.int32)
        for s in range(halves):
            mrow[s] = masks[s][0, : mrow.shape[1], :].astype(jnp.float32)
        least = None
        seen = jnp.max(mrow[...], axis=0)
        for r in range(count):
            u = jnp.max(seen[r * step : (r + 1) * step], keepdims=True)
            least = u if least is None else jnp.minimum(least, u)
        flags[1] = (jnp.max(least) > 0.0).astype(jnp.int32)
        vs[:, :, width:] = jnp.ones((group, vs.shape[1], width), jnp.bfloat16)

    def mask_line(r):
        at = (i * group + r) * step
        return jnp.concatenate(
            [mrow[s, pl.ds(at + t, 1), :] for s in range(halves) for t in range(step)], axis=1
        )

    def finish(r, attended):
        gated = (attended * g_ref[r].astype(jnp.float32)).astype(jnp.bfloat16)
        return (x_ref[r].astype(jnp.float32) + dot_nn(gated, wo_ref[...])).astype(jnp.bfloat16)

    def attend(shift):
        for r in range(group):
            vs[r, : va_ref.shape[1], :width] = va_ref[r]
            vs[r, va_ref.shape[1] :, :width] = vb_ref[r]
            madd = jnp.where(mask_line(r) > 0.0, 0.0, NEG)
            q = q_ref[r]
            num = jnp.zeros((cols, width), jnp.float32)
            den = jnp.ones((cols, width), jnp.float32)
            for h in range(heads):
                on = lane // (width // heads) == h
                qm = jnp.where(jnp.broadcast_to(on, q.shape), q, jnp.zeros_like(q))
                scores = jnp.concatenate([dot_nt(qm, ka_ref[r]), dot_nt(qm, kb_ref[r])], axis=1)
                bias = jnp.concatenate(
                    [bias_ref[w, :, h].reshape(cols, cols) for w in where], axis=1
                )
                scores = scores + bias.astype(jnp.float32) + madd
                if shift:
                    scores = scores - jnp.max(scores, axis=-1, keepdims=True)
                weights = jnp.exp2(scores).astype(jnp.bfloat16)
                both = dot_nn(weights, vs[r])
                num = jnp.where(on, both[:, :width], num)
                den = jnp.where(on, both[:, width:], den)
            out_ref[r] = finish(r, num / den)

    @pl.when(flags[0] > 0)
    def _():
        attend(False)

    @pl.when(flags[0] == 0)
    def _():
        attend(True)

    @pl.when(flags[1] == 0)
    def _():
        for r in range(group):
            used = jnp.max(mask_line(r), keepdims=True) > 0.0
            mean = jnp.mean(vs[r, :, :width].astype(jnp.float32), axis=0, keepdims=True)
            plain = finish(r, jnp.broadcast_to(mean, (cols, width)))
            out_ref[r] = jnp.where(used, out_ref[r].astype(jnp.float32), plain.astype(jnp.float32)).astype(jnp.bfloat16)


def attention(me, bias, wo, reach, q, g, ka, va, kb, vb, blocks, group=4):
    halves = bias.shape[0]
    rows, cols, width = q.shape
    one = lambda c: pl.BlockSpec((group, c, width), lambda i: (i, 0, 0))
    last = pl.BlockSpec((1, cols, width), lambda i: (rows, 0, 0))
    na, nb = ka.shape[1], kb.shape[1]
    return pl.pallas_call(
        functools.partial(attention_kernel, halves),
        grid=(rows // group,),
        out_shape=jax.ShapeDtypeStruct((rows, cols, width), jnp.bfloat16),
        in_specs=[SMEM, VMEM, VMEM, VMEM]
        + [one(cols)] * 3
        + [one(na), one(na), one(nb), one(nb)]
        + [last] * halves,
        out_specs=one(cols),
        scratch_shapes=[
            pltpu.SMEM((2,), jnp.int32),
            pltpu.VMEM((halves, rows * cols // 128, 128), jnp.float32),
            pltpu.VMEM((group, halves * cols, 2 * width), jnp.bfloat16),
        ],
        compiler_params=PARAMS,
        cost_estimate=pl.CostEstimate(
            flops=8 * rows * 4 * cols * halves * cols * width * 2,
            bytes_accessed=8 * rows * cols * width * halves,
            transcendentals=rows * 4 * cols * cols * halves,
        ),
    )(me, bias, wo, reach, q, g, blocks[0], ka, va, kb, vb, *blocks)


def shards(sizes, pair, pair_mask, gains, w_tri, w_tri_out, w_att, w_bias, w_att_out):
    n_rows, halves = sizes
    rows, cols, width = pair.shape
    heads = w_bias.shape[1]
    mask = pair_mask.astype(jnp.float32)
    lr = edges(pair, mask, gains, w_tri[:, : 4 * width].T)
    lr = lax.all_to_all(lr, AXES, split_axis=0, concat_axis=0, tiled=True)
    gates = gate(pair, gains, w_tri[:, 4 * width :])
    prod = product(lr.reshape(n_rows, halves, 2, rows, cols))
    back = lax.all_to_all(
        prod.reshape(width, rows, cols), AXES, split_axis=0, concat_axis=0, tiled=True
    )
    wb = jnp.pad(w_bias.T, ((0, 8 - heads), (0, 0)))
    mask_flat = mask.astype(jnp.bfloat16).reshape(rows * cols // width, width)
    *after, bias = tri_output(
        back, pair, gates, mask_flat, gains, gains[1][:, None], w_tri_out, wb, heads
    )
    inner = n_rows // halves
    swap = [
        ((z * inner + k) * halves + y, (y * inner + k) * halves + z)
        for z in range(halves)
        for k in range(inner)
        for y in range(halves)
    ]
    bias = jnp.swapaxes(bias, 0, 1)
    bias = lax.ppermute(bias, AXES, swap)
    bias = lax.all_gather(bias, "rows", axis=0, tiled=False)
    bias = bias.reshape(halves, inner, heads, rows, cols)

    up = [(y, (y + 1) % halves) for y in range(halves)]
    down = [(y, (y - 1) % halves) for y in range(halves)]
    parts = []
    for c, own in enumerate(after):
        prev = lax.ppermute(own, "half", up)
        next_ = lax.ppermute(own, "half", down)
        far = lax.ppermute(prev, "half", up) if c % 2 == 0 else lax.ppermute(next_, "half", down)
        parts.append((own, prev, next_, far))
    me = lax.axis_index("half").astype(jnp.int32).reshape(1)
    out = []
    for own, prev, next_, far in parts:
        q, g, ka, va, top = project((own, prev, next_), gains, w_att)
        kb, vb, reach = project_last(far, q, top, gains, w_att)
        out.append(attention(me, bias, w_att_out, reach, q, g, ka, va, kb, vb, (own, prev, next_, far)))
    return jnp.concatenate(out, axis=0)


def solution(mesh):
    sizes = (mesh.shape["rows"], mesh.shape["half"])
    in_specs = (P("rows", "half", None), P("rows", "half"), P(), P(), P(), P(), P(), P())
    out_specs = P("rows", "half", None)
    return jax.shard_map(
        functools.partial(shards, sizes),
        mesh=mesh,
        in_specs=in_specs,
        out_specs=out_specs,
        check_vma=False,
    )
```

```python
import functools

import jax
import jax.numpy as jnp
from jax import lax
from jax.experimental import pallas as pl
from jax.experimental.pallas import tpu as pltpu
from jax.sharding import PartitionSpec as P

LOG2E = 1.4426950408889634
NEG = -1e30
SAFE = 100.0
AXES = ("rows", "half")
VMEM = pl.BlockSpec(memory_space=pltpu.VMEM)
SMEM = pl.BlockSpec(memory_space=pltpu.SMEM)
PARAMS = pltpu.CompilerParams(vmem_limit_bytes=52 << 20)
CHUNKS = 2


def dot_nn(a, b):
    return lax.dot_general(a, b, (((1,), (0,)), ((), ())), preferred_element_type=jnp.float32)


def dot_nt(a, b):
    return lax.dot_general(a, b, (((1,), (1,)), ((), ())), preferred_element_type=jnp.float32)


def dot_tn(a, b):
    return lax.dot_general(a, b, (((0,), (0,)), ((), ())), preferred_element_type=jnp.float32)


def sigmoid(x):
    return 0.5 * jnp.tanh(0.5 * x) + 0.5


def norm_lanes(x, gain):
    x = x.astype(jnp.float32)
    center = x - jnp.mean(x, axis=-1, keepdims=True)
    spread = jnp.mean(center * center, axis=-1, keepdims=True)
    return (center * lax.rsqrt(spread + 1e-05) * gain).astype(jnp.bfloat16)


def norm_sublanes(x, gain):
    x = x.astype(jnp.float32)
    center = x - jnp.mean(x, axis=0, keepdims=True)
    spread = jnp.mean(center * center, axis=0, keepdims=True)
    return (center * lax.rsqrt(spread + 1e-05) * gain).astype(jnp.bfloat16)


def edges_kernel(pair_ref, mask_ref, gain_ref, w_ref, out_ref, scr):
    group, cols, width = pair_ref.shape
    gain = gain_ref[0:1, :]
    wt = w_ref[:, : 4 * width].T

    def some(t, carry):
        x = pair_ref[pl.ds(t * EDGE_ROWS, EDGE_ROWS)].reshape(EDGE_ROWS * cols, width)
        mixed = dot_nt(wt, norm_lanes(x, gain))
        m = jnp.concatenate(
            [mask_ref[pl.ds(t * EDGE_ROWS + r, 1), :] for r in range(EDGE_ROWS)], axis=1
        ).astype(jnp.float32)
        left = m * sigmoid(mixed[width : 2 * width]) * mixed[:width]
        right = m * sigmoid(mixed[3 * width :]) * mixed[2 * width : 3 * width]
        for e, edge in enumerate((left, right)):
            for r in range(EDGE_ROWS):
                for s in range(cols // 128):
                    at = r * cols + s * 128
                    scr[e, s, pl.ds(t * EDGE_ROWS + r, width, stride=group), :] = edge[:, at : at + 128]
        return carry

    lax.fori_loop(0, group // EDGE_ROWS, some, 0, unroll=EDGE_UNROLL)
    for e in range(2):
        for s in range(cols // 128):
            out_ref[:, e, :, s * 128 : (s + 1) * 128] = (
                scr[e, s].reshape(width, group, 128).astype(jnp.bfloat16)
            )


EDGE_UNROLL = 1
EDGE_ROWS = 8


def edges(pair, mask, gains, w, group=16):
    rows, cols, width = pair.shape
    return pl.pallas_call(
        edges_kernel,
        grid=(rows // group,),
        out_shape=jax.ShapeDtypeStruct((width, 2, rows, cols), jnp.bfloat16),
        in_specs=[
            pl.BlockSpec((group, cols, width), lambda i: (i, 0, 0)),
            pl.BlockSpec((group, cols), lambda i: (i, 0)),
            VMEM,
            VMEM,
        ],
        out_specs=pl.BlockSpec((width, 2, group, cols), lambda i: (0, 0, i, 0)),
        scratch_shapes=[pltpu.VMEM((2, cols // 128, width * group, 128), jnp.float32)],
        compiler_params=PARAMS,
    )(pair, mask, gains, w)


def gate_kernel(pair_ref, gain_ref, w_ref, out_ref):
    group, cols, width = pair_ref.shape
    normed = norm_lanes(pair_ref[...].reshape(group * cols, width), gain_ref[0:1, :])
    gates = sigmoid(dot_nn(normed, w_ref[:, 4 * width :])).astype(jnp.bfloat16)
    out_ref[...] = gates.reshape(group, cols, width)


def gate(pair, gains, w, group=8):
    rows, cols, width = pair.shape
    block = pl.BlockSpec((group, cols, width), lambda i: (i, 0, 0))
    return pl.pallas_call(
        gate_kernel,
        grid=(rows // group,),
        out_shape=jax.ShapeDtypeStruct(pair.shape, jnp.bfloat16),
        in_specs=[block, VMEM, VMEM],
        out_specs=block,
        compiler_params=PARAMS,
        cost_estimate=pl.CostEstimate(
            flops=6 * rows * cols * width * width,
            bytes_accessed=4 * rows * cols * width,
            transcendentals=rows * cols * width,
        ),
    )(pair, gains, w)


PRODUCT_ROWS = 512


def product_kernel(lr_ref, out_ref):
    blocks, halves, _, rows, cols = lr_ref.shape
    step = PRODUCT_ROWS // rows

    def tile(t, carry):
        acc = None
        for h in range(halves):
            left = lr_ref[pl.ds(t * step, step), h, 0].reshape(step * rows, cols)
            right = lr_ref[:, h, 1].reshape(blocks * rows, cols)
            part = dot_nt(left, right)
            acc = part if acc is None else acc + part
        for h in range(halves):
            out_ref[pl.ds(t * step, step), h] = (
                acc[:, h * cols : (h + 1) * cols].reshape(step, rows, cols).astype(jnp.bfloat16)
            )
        return carry

    lax.fori_loop(0, blocks // step, tile, 0)


def product(lr):
    blocks, halves, _, rows, cols = lr.shape
    return pl.pallas_call(
        product_kernel,
        out_shape=jax.ShapeDtypeStruct((blocks, halves, rows, cols), jnp.bfloat16),
        in_specs=[VMEM],
        out_specs=VMEM,
        compiler_params=PARAMS,
    )(lr)


OUT_UNROLL = 1
OUT_ROWS = 8


def output_kernel(prod_ref, pair_ref, gate_ref, mask_ref, gain_ref, gcol_ref, wo_ref, wb_ref, *refs):
    outs, bias_ref, scr = refs[:CHUNKS], refs[CHUNKS], refs[CHUNKS + 1]
    width, rows, cols = prod_ref.shape
    heads = bias_ref.shape[1]
    per = rows // CHUNKS
    for s in range(cols // 128):
        for c in range(0, width, 16):
            part = prod_ref[c : c + 16, :, s * 128 : (s + 1) * 128].astype(jnp.float32)
            scr[s, c * rows : (c + 16) * rows, :] = part.reshape(16 * rows, 128)

    for c in range(CHUNKS):

        def some(t, carry, c=c):
            i = c * per + t * OUT_ROWS
            x = jnp.concatenate(
                [
                    scr[s, pl.ds(i + r, width, stride=rows), :]
                    for r in range(OUT_ROWS)
                    for s in range(cols // 128)
                ],
                axis=1,
            )
            normed = norm_sublanes(x.astype(jnp.bfloat16), gcol_ref[...])
            update = dot_tn(normed, wo_ref[...])
            here = pl.ds(i, OUT_ROWS)
            flat = (OUT_ROWS * cols, width)
            p = pair_ref[here].reshape(flat).astype(jnp.float32)
            after = p + gate_ref[here].reshape(flat).astype(jnp.float32) * update
            after = after.astype(jnp.bfloat16)
            outs[c][pl.ds(t * OUT_ROWS, OUT_ROWS)] = after.reshape(OUT_ROWS, cols, width)
            a = norm_lanes(after, gain_ref[2:3, :])
            bias = (dot_nt(wb_ref[...], a) * LOG2E).astype(jnp.bfloat16)
            for r in range(OUT_ROWS):
                bias_ref[i + r] = bias[:heads, r * cols : (r + 1) * cols]
            return carry

        lax.fori_loop(0, per // OUT_ROWS, some, 0, unroll=OUT_UNROLL)
        used = per * cols // width
        outs[c][per, :used, :] = mask_ref[c * used : (c + 1) * used, :]
        outs[c][per, used:, :] = jnp.zeros((cols - used, width), jnp.bfloat16)


def tri_output(prod, pair, gates, mask_flat, gains, gcol, wo, wb, heads):
    width, rows, cols = prod.shape
    part = jax.ShapeDtypeStruct((rows // CHUNKS + 1, cols, width), jnp.bfloat16)
    return pl.pallas_call(
        output_kernel,
        out_shape=(part,) * CHUNKS + (jax.ShapeDtypeStruct((rows, heads, cols), jnp.bfloat16),),
        in_specs=[VMEM] * 8,
        out_specs=(VMEM,) * (CHUNKS + 1),
        scratch_shapes=[pltpu.VMEM((cols // 128, width * rows, 128), jnp.float32)],
        compiler_params=PARAMS,
    )(prod, pair, gates, mask_flat, gains, gcol, wo, wb)


def project_kernel(gain_ref, w_ref, *refs):
    width = gain_ref.shape[1]
    xs = refs[:-5]
    q_ref, g_ref, k_ref, v_ref, m_ref = refs[-5:]
    group, cols, _ = xs[0].shape
    scale = LOG2E * HEAD_DIM**-0.5
    tops = [None] * group
    for b, x_ref in enumerate(xs):
        a = norm_lanes(x_ref[...].reshape(group * cols, width), gain_ref[2:3, :])
        at = slice(b * cols, (b + 1) * cols)
        if b == 0:
            mixed = dot_nn(a, w_ref[...])
            q_ref[...] = (mixed[:, :width] * scale).astype(jnp.bfloat16).reshape(q_ref.shape)
            g_ref[...] = sigmoid(mixed[:, 3 * width :]).astype(jnp.bfloat16).reshape(g_ref.shape)
            kv = mixed[:, width : 3 * width].astype(jnp.bfloat16)
        else:
            kv = dot_nn(a, w_ref[:, width : 3 * width]).astype(jnp.bfloat16)
        k_ref[:, at, :] = kv[:, :width].reshape(group, cols, width)
        v_ref[:, at, :] = kv[:, width:].reshape(group, cols, width)
        for r in range(group):
            m = jnp.max(jnp.abs(kv[r * cols : (r + 1) * cols, :width]), axis=0, keepdims=True)
            tops[r] = m if tops[r] is None else jnp.maximum(tops[r], m)
    for r in range(group):
        m_ref[r] = jnp.broadcast_to(tops[r].astype(jnp.float32), m_ref.shape[1:])


HEAD_DIM = 32
AHEAD = 1


def project(blocks, gains, w, group=8):
    rows, cols, width = blocks[0].shape
    rows -= 1
    n = len(blocks)
    one = lambda c: pl.BlockSpec((group, c, width), lambda i: (i, 0, 0))
    shape = lambda c: jax.ShapeDtypeStruct((rows, c, width), jnp.bfloat16)
    return pl.pallas_call(
        project_kernel,
        grid=(rows // group,),
        out_shape=(shape(cols), shape(cols), shape(n * cols), shape(n * cols), jax.ShapeDtypeStruct((rows, 8, width), jnp.float32)),
        in_specs=[VMEM, VMEM] + [one(cols)] * n,
        out_specs=(one(cols), one(cols), one(n * cols), one(n * cols), one(8)),
        compiler_params=PARAMS,
        cost_estimate=pl.CostEstimate(
            flops=8 * n * rows * cols * width * width,
            bytes_accessed=8 * n * rows * cols * width,
            transcendentals=rows * cols * width,
        ),
    )(gains, w, *blocks)


def project_last_kernel(gain_ref, w_ref, e_ref, x_ref, q_ref, top_ref, k_ref, v_ref, m_ref):
    width = gain_ref.shape[1]
    group, cols, _ = x_ref.shape
    a = norm_lanes(x_ref[...].reshape(group * cols, width), gain_ref[2:3, :])
    kv = dot_nn(a, w_ref[:, width : 3 * width]).astype(jnp.bfloat16)
    k_ref[...] = kv[:, :width].reshape(k_ref.shape)
    v_ref[...] = kv[:, width:].reshape(v_ref.shape)
    sized = []
    for r in range(group):
        m = jnp.max(jnp.abs(kv[r * cols : (r + 1) * cols, :width]), axis=0, keepdims=True)
        top = jnp.maximum(m.astype(jnp.float32), top_ref[r, 0:1, :])
        sized.append((jnp.abs(q_ref[r]).astype(jnp.float32) * top).astype(jnp.bfloat16))
    reach = dot_nn(jnp.concatenate(sized, axis=0), e_ref[...])
    for r in range(group):
        m = jnp.max(reach[r * cols : (r + 1) * cols], axis=0, keepdims=True)
        m_ref[r] = jnp.broadcast_to(m, m_ref.shape[1:])


def project_last(block, q, top, gains, w, group=8):
    rows, cols, width = q.shape
    lanes = jnp.arange(width) // HEAD_DIM
    e = (lanes[:, None] == lanes[None, :]).astype(jnp.bfloat16)
    one = lambda c: pl.BlockSpec((group, c, width), lambda i: (i, 0, 0))
    shape = jax.ShapeDtypeStruct((rows, cols, width), jnp.bfloat16)
    return pl.pallas_call(
        project_last_kernel,
        grid=(rows // group,),
        out_shape=(shape, shape, jax.ShapeDtypeStruct((rows, 8, width), jnp.float32)),
        in_specs=[VMEM] * 3 + [one(cols), one(cols), one(8)],
        out_specs=(one(cols), one(cols), one(8)),
        compiler_params=PARAMS,
        cost_estimate=pl.CostEstimate(
            flops=10 * rows * cols * width * width,
            bytes_accessed=8 * rows * cols * width,
            transcendentals=0,
        ),
    )(gains, w, e, block, q, top)


def attention_kernel(halves, me_ref, bias_ref, wo_ref, reach_ref, *refs):
    q_ref, g_ref, x_ref, ka_ref, va_ref, kb_ref, vb_ref = refs[:7]
    masks = refs[7 : 7 + halves]
    out_ref, flags, mrow, vs, b32, gated = refs[-6:]
    i = pl.program_id(0)
    group, cols, width = q_ref.shape
    heads = bias_ref.shape[2]
    lane = lax.broadcasted_iota(jnp.int32, (1, width), 1)
    me = me_ref[0]
    where = [lax.rem(me + s, halves) for s in (0, halves - 1, 1, 2)]
    step = cols // 128
    count = mrow.shape[1] // step

    @pl.when(i == 0)
    def _():
        top = jnp.zeros((bias_ref.shape[3], cols), jnp.float32)
        sub = bias_ref.shape[3]
        for s, w in enumerate(where):

            def put(t, top, s=s, w=w):
                for h in range(heads):
                    b = bias_ref[w, t, h].astype(jnp.float32)
                    b32[h, pl.ds(pl.multiple_of(t * sub, sub), sub), s * cols : (s + 1) * cols] = b
                    top = jnp.maximum(top, jnp.abs(b))
                return top

            top = lax.fori_loop(0, bias_ref.shape[1], put, top)
        bound = jnp.max(reach_ref[...]) * 1.02 + jnp.max(top)
        flags[0] = (bound < SAFE).astype(jnp.int32)
        for s in range(halves):
            mrow[s] = masks[s][0, : mrow.shape[1], :].astype(jnp.float32)
        least = None
        seen = jnp.max(mrow[...], axis=0)
        for r in range(count):
            u = jnp.max(seen[r * step : (r + 1) * step], keepdims=True)
            least = u if least is None else jnp.minimum(least, u)
        flags[1] = (jnp.max(least) > 0.0).astype(jnp.int32)
        vs[:, :, width:] = jnp.ones((group, vs.shape[1], width), jnp.bfloat16)

    def mask_line(r):
        at = (i * group + r) * step
        return jnp.concatenate(
            [mrow[s, pl.ds(at + t, 1), :] for s in range(halves) for t in range(step)], axis=1
        )

    def finish(r, attended):
        gated[r] = (attended * g_ref[r].astype(jnp.float32)).astype(jnp.bfloat16)

    def attend(shift):
        def score(r, h):
            q = q_ref[r]
            on = jnp.broadcast_to(lane // (width // heads) == h, q.shape)
            qm = jnp.where(on, q, jnp.zeros_like(q))
            scores = jnp.concatenate([dot_nt(qm, ka_ref[r]), dot_nt(qm, kb_ref[r])], axis=1)
            return scores + b32[h] + jnp.where(mask_line(r) > 0.0, 0.0, NEG)

        order = [(r, h) for r in range(group) for h in range(heads)]
        ahead = [score(*order[t]) for t in range(AHEAD)]
        for t, (r, h) in enumerate(order):
            if t + AHEAD < len(order):
                ahead.append(score(*order[t + AHEAD]))
            scores = ahead.pop(0)
            if h == 0:
                vs[r, : va_ref.shape[1], :width] = va_ref[r]
                vs[r, va_ref.shape[1] :, :width] = vb_ref[r]
                num = jnp.zeros((cols, width), jnp.float32)
                den = jnp.ones((cols, width), jnp.float32)
            if shift:
                scores = scores - jnp.max(scores, axis=-1, keepdims=True)
            weights = jnp.exp2(scores).astype(jnp.bfloat16)
            both = dot_nn(weights, vs[r])
            on = lane // (width // heads) == h
            num = jnp.where(on, both[:, :width], num)
            den = jnp.where(on, both[:, width:], den)
            if h == heads - 1:
                finish(r, num / den)

    @pl.when(flags[0] > 0)
    def _():
        attend(False)

    @pl.when(flags[0] == 0)
    def _():
        attend(True)

    @pl.when(flags[1] == 0)
    def _():
        for r in range(group):
            used = jnp.max(mask_line(r), keepdims=True) > 0.0
            mean = jnp.mean(vs[r, :, :width].astype(jnp.float32), axis=0, keepdims=True)
            plain = mean * g_ref[r].astype(jnp.float32)
            gated[r] = jnp.where(used, gated[r].astype(jnp.float32), plain).astype(jnp.bfloat16)

    flat = (group * cols, width)
    out = dot_nn(gated[...].reshape(flat), wo_ref[...])
    out = x_ref[...].reshape(flat).astype(jnp.float32) + out
    out_ref[...] = out.astype(jnp.bfloat16).reshape(out_ref.shape)


def attention(me, bias, wo, reach, q, g, ka, va, kb, vb, blocks, chunk, filled, group=4):
    halves = bias.shape[0]
    rows, cols, width = q.shape
    one = lambda c: pl.BlockSpec((group, c, width), lambda i: (i, 0, 0))
    last = pl.BlockSpec((1, cols, width), lambda i: (rows, 0, 0))
    na, nb = ka.shape[1], kb.shape[1]
    return pl.pallas_call(
        functools.partial(attention_kernel, halves),
        grid=(rows // group,),
        out_shape=jax.ShapeDtypeStruct((CHUNKS * rows, cols, width), jnp.bfloat16),
        in_specs=[SMEM, VMEM, VMEM, VMEM]
        + [one(cols)] * 3
        + [one(na), one(na), one(nb), one(nb)]
        + [last] * halves
        + [pl.BlockSpec(memory_space=pl.ANY)] * len(filled),
        out_specs=pl.BlockSpec((group, cols, width), lambda i: (chunk * (rows // group) + i, 0, 0)),
        input_output_aliases={11 + halves: 0} if filled else {},
        scratch_shapes=[
            pltpu.SMEM((2,), jnp.int32),
            pltpu.VMEM((halves, rows * cols // 128, 128), jnp.float32),
            pltpu.VMEM((group, halves * cols, 2 * width), jnp.bfloat16),
            pltpu.VMEM((bias.shape[2], cols, halves * cols), jnp.float32),
            pltpu.VMEM((group, cols, width), jnp.bfloat16),
        ],
        compiler_params=PARAMS,
        cost_estimate=pl.CostEstimate(
            flops=8 * rows * 4 * cols * halves * cols * width * 2,
            bytes_accessed=8 * rows * cols * width * halves,
            transcendentals=rows * 4 * cols * cols * halves,
        ),
    )(me, bias, wo, reach, q, g, blocks[0], ka, va, kb, vb, *blocks, *filled)


def shards(sizes, pair, pair_mask, gains, w_tri, w_tri_out, w_att, w_bias, w_att_out):
    n_rows, halves = sizes
    rows, cols, width = pair.shape
    heads = w_bias.shape[1]
    lr = edges(pair, pair_mask, gains, w_tri)
    lr = lax.all_to_all(lr, AXES, split_axis=0, concat_axis=0, tiled=True)
    gates = gate(pair, gains, w_tri)
    prod = product(lr.reshape(n_rows, halves, 2, rows, cols))
    back = lax.all_to_all(
        prod.reshape(width, rows, cols), AXES, split_axis=0, concat_axis=0, tiled=True
    )
    wb = jnp.pad(w_bias.T, ((0, 8 - heads), (0, 0)))
    mask_flat = pair_mask.astype(jnp.bfloat16).reshape(rows * cols // width, width)
    *after, bias = tri_output(
        back, pair, gates, mask_flat, gains, gains[1][:, None], w_tri_out, wb, heads
    )
    inner = n_rows // halves
    swap = [
        ((z * inner + k) * halves + y, (y * inner + k) * halves + z)
        for z in range(halves)
        for k in range(inner)
        for y in range(halves)
    ]
    bias = jnp.swapaxes(bias, 0, 1)
    bias = lax.ppermute(bias, AXES, swap)
    bias = lax.all_gather(bias, "rows", axis=0, tiled=False)
    bias = bias.reshape(halves, inner, heads, rows, cols)

    up = [(y, (y + 1) % halves) for y in range(halves)]
    down = [(y, (y - 1) % halves) for y in range(halves)]
    parts = []
    for c, own in enumerate(after):
        prev = lax.ppermute(own, "half", up)
        next_ = lax.ppermute(own, "half", down)
        far = lax.ppermute(prev, "half", up) if c % 2 == 0 else lax.ppermute(next_, "half", down)
        parts.append((own, prev, next_, far))
    me = lax.axis_index("half").astype(jnp.int32).reshape(1)
    out = []
    for c, (own, prev, next_, far) in enumerate(parts):
        q, g, ka, va, top = project((own, prev, next_), gains, w_att)
        if out:
            far, out[0] = lax.optimization_barrier((far, out[0]))
        kb, vb, reach = project_last(far, q, top, gains, w_att)
        blocks = (own, prev, next_, far)
        out = [attention(me, bias, w_att_out, reach, q, g, ka, va, kb, vb, blocks, c, out)]
    return out[0]


def solution(mesh):
    sizes = (mesh.shape["rows"], mesh.shape["half"])
    in_specs = (P("rows", "half", None), P("rows", "half"), P(), P(), P(), P(), P(), P())
    out_specs = P("rows", "half", None)
    return jax.shard_map(
        functools.partial(shards, sizes),
        mesh=mesh,
        in_specs=in_specs,
        out_specs=out_specs,
        check_vma=False,
    )
```

```python
import functools

import jax
import jax.numpy as jnp
from jax import lax
from jax.experimental import pallas as pl
from jax.experimental.pallas import tpu as pltpu
from jax.sharding import PartitionSpec as P

LOG2E = 1.4426950408889634
NEG = -1e30
SAFE = 100.0
AXES = ("rows", "half")
VMEM = pl.BlockSpec(memory_space=pltpu.VMEM)
SMEM = pl.BlockSpec(memory_space=pltpu.SMEM)
PARAMS = pltpu.CompilerParams(vmem_limit_bytes=52 << 20)
CHUNKS = 2


def dot_nn(a, b):
    return lax.dot_general(a, b, (((1,), (0,)), ((), ())), preferred_element_type=jnp.float32)


def dot_nt(a, b):
    return lax.dot_general(a, b, (((1,), (1,)), ((), ())), preferred_element_type=jnp.float32)


def dot_tn(a, b):
    return lax.dot_general(a, b, (((0,), (0,)), ((), ())), preferred_element_type=jnp.float32)


def sigmoid(x):
    return 0.5 * jnp.tanh(0.5 * x) + 0.5


def norm_lanes(x, gain):
    x = x.astype(jnp.float32)
    center = x - jnp.mean(x, axis=-1, keepdims=True)
    spread = jnp.mean(center * center, axis=-1, keepdims=True)
    return (center * lax.rsqrt(spread + 1e-05) * gain).astype(jnp.bfloat16)


def norm_sublanes(x, gain):
    x = x.astype(jnp.float32)
    center = x - jnp.mean(x, axis=0, keepdims=True)
    spread = jnp.mean(center * center, axis=0, keepdims=True)
    return (center * lax.rsqrt(spread + 1e-05) * gain).astype(jnp.bfloat16)


def edges_kernel(pair_ref, mask_ref, gain_ref, w_ref, out_ref, scr):
    group, cols, width = pair_ref.shape
    gain = gain_ref[0:1, :]
    wt = w_ref[:, : 4 * width].T

    def some(t, carry):
        x = pair_ref[pl.ds(t * EDGE_ROWS, EDGE_ROWS)].reshape(EDGE_ROWS * cols, width)
        mixed = dot_nt(wt, norm_lanes(x, gain))
        m = jnp.concatenate(
            [mask_ref[pl.ds(t * EDGE_ROWS + r, 1), :] for r in range(EDGE_ROWS)], axis=1
        ).astype(jnp.float32)
        left = m * sigmoid(mixed[width : 2 * width]) * mixed[:width]
        right = m * sigmoid(mixed[3 * width :]) * mixed[2 * width : 3 * width]
        for e, edge in enumerate((left, right)):
            for r in range(EDGE_ROWS):
                for s in range(cols // 128):
                    at = r * cols + s * 128
                    scr[e, s, pl.ds(t * EDGE_ROWS + r, width, stride=group), :] = edge[:, at : at + 128]
        return carry

    lax.fori_loop(0, group // EDGE_ROWS, some, 0, unroll=EDGE_UNROLL)
    for e in range(2):
        for s in range(cols // 128):
            out_ref[:, e, :, s * 128 : (s + 1) * 128] = (
                scr[e, s].reshape(width, group, 128).astype(jnp.bfloat16)
            )


EDGE_UNROLL = 1
EDGE_ROWS = 8


def edges(pair, mask, gains, w, group=16):
    rows, cols, width = pair.shape
    return pl.pallas_call(
        edges_kernel,
        grid=(rows // group,),
        out_shape=jax.ShapeDtypeStruct((width, 2, rows, cols), jnp.bfloat16),
        in_specs=[
            pl.BlockSpec((group, cols, width), lambda i: (i, 0, 0)),
            pl.BlockSpec((group, cols), lambda i: (i, 0)),
            VMEM,
            VMEM,
        ],
        out_specs=pl.BlockSpec((width, 2, group, cols), lambda i: (0, 0, i, 0)),
        scratch_shapes=[pltpu.VMEM((2, cols // 128, width * group, 128), jnp.float32)],
        compiler_params=PARAMS,
    )(pair, mask, gains, w)


def gate_kernel(pair_ref, gain_ref, w_ref, out_ref):
    group, cols, width = pair_ref.shape
    normed = norm_lanes(pair_ref[...].reshape(group * cols, width), gain_ref[0:1, :])
    gates = sigmoid(dot_nn(normed, w_ref[:, 4 * width :])).astype(jnp.bfloat16)
    out_ref[...] = gates.reshape(group, cols, width)


def gate(pair, gains, w, group=8):
    rows, cols, width = pair.shape
    block = pl.BlockSpec((group, cols, width), lambda i: (i, 0, 0))
    return pl.pallas_call(
        gate_kernel,
        grid=(rows // group,),
        out_shape=jax.ShapeDtypeStruct(pair.shape, jnp.bfloat16),
        in_specs=[block, VMEM, VMEM],
        out_specs=block,
        compiler_params=PARAMS,
        cost_estimate=pl.CostEstimate(
            flops=6 * rows * cols * width * width,
            bytes_accessed=4 * rows * cols * width,
            transcendentals=rows * cols * width,
        ),
    )(pair, gains, w)


PRODUCT_ROWS = 512


def product_kernel(lr_ref, out_ref):
    blocks, halves, _, rows, cols = lr_ref.shape
    step = PRODUCT_ROWS // rows

    def tile(t, carry):
        acc = None
        for h in range(halves):
            left = lr_ref[pl.ds(t * step, step), h, 0].reshape(step * rows, cols)
            right = lr_ref[:, h, 1].reshape(blocks * rows, cols)
            part = dot_nt(left, right)
            acc = part if acc is None else acc + part
        for h in range(halves):
            out_ref[pl.ds(t * step, step), h] = (
                acc[:, h * cols : (h + 1) * cols].reshape(step, rows, cols).astype(jnp.bfloat16)
            )
        return carry

    lax.fori_loop(0, blocks // step, tile, 0)


def product(lr):
    blocks, halves, _, rows, cols = lr.shape
    return pl.pallas_call(
        product_kernel,
        out_shape=jax.ShapeDtypeStruct((blocks, halves, rows, cols), jnp.bfloat16),
        in_specs=[VMEM],
        out_specs=VMEM,
        compiler_params=PARAMS,
    )(lr)


OUT_ROWS = 8


def output_kernel(prod_ref, pair_ref, gate_ref, mask_ref, gain_ref, gcol_ref, wo_ref, wb_ref, after_ref, norm_ref, bias_ref, scr):
    width, rows, cols = prod_ref.shape
    heads = bias_ref.shape[1]
    for s in range(cols // 128):
        for c in range(0, width, 16):
            part = prod_ref[c : c + 16, :, s * 128 : (s + 1) * 128].astype(jnp.float32)
            scr[s, c * rows : (c + 16) * rows, :] = part.reshape(16 * rows, 128)

    def some(t, carry):
        i = t * OUT_ROWS
        x = jnp.concatenate(
            [
                scr[s, pl.ds(i + r, width, stride=rows), :]
                for r in range(OUT_ROWS)
                for s in range(cols // 128)
            ],
            axis=1,
        )
        normed = norm_sublanes(x.astype(jnp.bfloat16), gcol_ref[...])
        update = dot_tn(normed, wo_ref[...])
        here = pl.ds(i, OUT_ROWS)
        flat = (OUT_ROWS * cols, width)
        p = pair_ref[here].reshape(flat).astype(jnp.float32)
        after = p + gate_ref[here].reshape(flat).astype(jnp.float32) * update
        after = after.astype(jnp.bfloat16)
        after_ref[here] = after.reshape(OUT_ROWS, cols, width)
        a = norm_lanes(after, gain_ref[2:3, :])
        norm_ref[here] = a.reshape(OUT_ROWS, cols, width)
        bias = (dot_nt(wb_ref[...], a) * LOG2E).astype(jnp.bfloat16)
        for r in range(OUT_ROWS):
            bias_ref[i + r] = bias[:heads, r * cols : (r + 1) * cols]
        return carry

    lax.fori_loop(0, rows // OUT_ROWS, some, 0)
    used = rows * cols // width
    norm_ref[rows, :used, :] = mask_ref[...]
    norm_ref[rows, used:, :] = jnp.zeros((cols - used, width), jnp.bfloat16)


def tri_output(prod, pair, gates, mask_flat, gains, gcol, wo, wb, heads, chunk):
    width, rows, cols = prod.shape
    rows //= CHUNKS
    block = pl.BlockSpec((rows, cols, width), lambda i: (chunk, 0, 0))
    return pl.pallas_call(
        output_kernel,
        grid=(1,),
        out_shape=(
            jax.ShapeDtypeStruct((rows, cols, width), jnp.bfloat16),
            jax.ShapeDtypeStruct((rows + 1, cols, width), jnp.bfloat16),
            jax.ShapeDtypeStruct((rows, heads, cols), jnp.bfloat16),
        ),
        in_specs=[
            pl.BlockSpec((width, rows, cols), lambda i: (0, chunk, 0)),
            block,
            block,
            pl.BlockSpec((rows * cols // width, width), lambda i: (chunk, 0)),
        ]
        + [VMEM] * 4,
        out_specs=(VMEM,) * 3,
        scratch_shapes=[pltpu.VMEM((cols // 128, width * rows, 128), jnp.float32)],
        compiler_params=PARAMS,
    )(prod, pair, gates, mask_flat, gains, gcol, wo, wb)


def project_kernel(w_ref, *refs):
    width = w_ref.shape[0]
    xs = refs[:-5]
    q_ref, g_ref, k_ref, v_ref, m_ref = refs[-5:]
    group, cols, _ = xs[0].shape
    scale = LOG2E * HEAD_DIM**-0.5
    tops = [None] * group
    for b, x_ref in enumerate(xs):
        a = x_ref[...].reshape(group * cols, width)
        at = slice(b * cols, (b + 1) * cols)
        if b == 0:
            mixed = dot_nn(a, w_ref[...])
            q_ref[...] = (mixed[:, :width] * scale).astype(jnp.bfloat16).reshape(q_ref.shape)
            g_ref[...] = sigmoid(mixed[:, 3 * width :]).astype(jnp.bfloat16).reshape(g_ref.shape)
            kv = mixed[:, width : 3 * width].astype(jnp.bfloat16)
        else:
            kv = dot_nn(a, w_ref[:, width : 3 * width]).astype(jnp.bfloat16)
        k_ref[:, at, :] = kv[:, :width].reshape(group, cols, width)
        v_ref[:, at, :] = kv[:, width:].reshape(group, cols, width)
        for r in range(group):
            m = jnp.max(jnp.abs(kv[r * cols : (r + 1) * cols, :width]), axis=0, keepdims=True)
            tops[r] = m if tops[r] is None else jnp.maximum(tops[r], m)
    for r in range(group):
        m_ref[r] = jnp.broadcast_to(tops[r].astype(jnp.float32), m_ref.shape[1:])


HEAD_DIM = 32
AHEAD = 1


def project(blocks, w, group=8):
    rows, cols, width = blocks[0].shape
    rows -= 1
    n = len(blocks)
    one = lambda c: pl.BlockSpec((group, c, width), lambda i: (i, 0, 0))
    shape = lambda c: jax.ShapeDtypeStruct((rows, c, width), jnp.bfloat16)
    return pl.pallas_call(
        project_kernel,
        grid=(rows // group,),
        out_shape=(shape(cols), shape(cols), shape(n * cols), shape(n * cols), jax.ShapeDtypeStruct((rows, 8, width), jnp.float32)),
        in_specs=[VMEM] + [one(cols)] * n,
        out_specs=(one(cols), one(cols), one(n * cols), one(n * cols), one(8)),
        compiler_params=PARAMS,
        cost_estimate=pl.CostEstimate(
            flops=8 * n * rows * cols * width * width,
            bytes_accessed=8 * n * rows * cols * width,
            transcendentals=rows * cols * width,
        ),
    )(w, *blocks)


def project_last_kernel(w_ref, e_ref, x_ref, q_ref, top_ref, k_ref, v_ref, m_ref):
    width = w_ref.shape[0]
    group, cols, _ = x_ref.shape
    a = x_ref[...].reshape(group * cols, width)
    kv = dot_nn(a, w_ref[:, width : 3 * width]).astype(jnp.bfloat16)
    k_ref[...] = kv[:, :width].reshape(k_ref.shape)
    v_ref[...] = kv[:, width:].reshape(v_ref.shape)
    sized = []
    for r in range(group):
        m = jnp.max(jnp.abs(kv[r * cols : (r + 1) * cols, :width]), axis=0, keepdims=True)
        top = jnp.maximum(m.astype(jnp.float32), top_ref[r, 0:1, :])
        sized.append((jnp.abs(q_ref[r]).astype(jnp.float32) * top).astype(jnp.bfloat16))
    reach = dot_nn(jnp.concatenate(sized, axis=0), e_ref[...])
    for r in range(group):
        m = jnp.max(reach[r * cols : (r + 1) * cols], axis=0, keepdims=True)
        m_ref[r] = jnp.broadcast_to(m, m_ref.shape[1:])


def project_last(block, q, top, w, group=8):
    rows, cols, width = q.shape
    lanes = jnp.arange(width) // HEAD_DIM
    e = (lanes[:, None] == lanes[None, :]).astype(jnp.bfloat16)
    one = lambda c: pl.BlockSpec((group, c, width), lambda i: (i, 0, 0))
    shape = jax.ShapeDtypeStruct((rows, cols, width), jnp.bfloat16)
    return pl.pallas_call(
        project_last_kernel,
        grid=(rows // group,),
        out_shape=(shape, shape, jax.ShapeDtypeStruct((rows, 8, width), jnp.float32)),
        in_specs=[VMEM] * 2 + [one(cols), one(cols), one(8)],
        out_specs=(one(cols), one(cols), one(8)),
        compiler_params=PARAMS,
        cost_estimate=pl.CostEstimate(
            flops=10 * rows * cols * width * width,
            bytes_accessed=8 * rows * cols * width,
            transcendentals=0,
        ),
    )(w, e, block, q, top)


def attention_kernel(halves, me_ref, bias_a_ref, bias_b_ref, wo_ref, reach_ref, *refs):
    q_ref, g_ref, x_ref, ka_ref, va_ref, kb_ref, vb_ref = refs[:7]
    masks = refs[7 : 7 + halves]
    out_ref, flags, mrow, vs, b32, gated = refs[-6:]
    i = pl.program_id(0)
    group, cols, width = q_ref.shape
    _, outer, heads, sub, _ = bias_a_ref.shape
    lane = lax.broadcasted_iota(jnp.int32, (1, width), 1)
    me = me_ref[0]
    where = [lax.rem(me + s, halves) for s in (0, halves - 1, 1, 2)]
    step = cols // 128
    count = mrow.shape[1] // step

    @pl.when(i == 0)
    def _():
        top = jnp.zeros((sub, cols), jnp.float32)
        for s, w in enumerate(where):

            def put(t, top, s=s, w=w):
                for p, piece in enumerate((bias_a_ref, bias_b_ref)):
                    core = me_ref[1] if p == 0 else 1 - me_ref[1]
                    j = pl.ds(pl.multiple_of((2 * t + core) * sub, sub), sub)
                    for h in range(heads):
                        b = piece[w, t, h].astype(jnp.float32)
                        b32[h, j, s * cols : (s + 1) * cols] = b
                        top = jnp.maximum(top, jnp.abs(b))
                return top

            top = lax.fori_loop(0, outer, put, top)
        bound = jnp.max(reach_ref[...]) * 1.02 + jnp.max(top)
        flags[0] = (bound < SAFE).astype(jnp.int32)
        for s in range(halves):
            mrow[s] = masks[s][0, : mrow.shape[1], :].astype(jnp.float32)
        least = None
        seen = jnp.max(mrow[...], axis=0)
        for r in range(count):
            u = jnp.max(seen[r * step : (r + 1) * step], keepdims=True)
            least = u if least is None else jnp.minimum(least, u)
        flags[1] = (jnp.max(least) > 0.0).astype(jnp.int32)
        vs[:, :, width:] = jnp.ones((group, vs.shape[1], width), jnp.bfloat16)

    def mask_line(r):
        at = (i * group + r) * step
        return jnp.concatenate(
            [mrow[s, pl.ds(at + t, 1), :] for s in range(halves) for t in range(step)], axis=1
        )

    def finish(r, attended):
        gated[r] = (attended * g_ref[r].astype(jnp.float32)).astype(jnp.bfloat16)

    def attend(shift):
        def score(r, h):
            q = q_ref[r]
            on = jnp.broadcast_to(lane // (width // heads) == h, q.shape)
            qm = jnp.where(on, q, jnp.zeros_like(q))
            scores = jnp.concatenate([dot_nt(qm, ka_ref[r]), dot_nt(qm, kb_ref[r])], axis=1)
            return scores + b32[h] + jnp.where(mask_line(r) > 0.0, 0.0, NEG)

        order = [(r, h) for r in range(group) for h in range(heads)]
        ahead = [score(*order[t]) for t in range(AHEAD)]
        for t, (r, h) in enumerate(order):
            if t + AHEAD < len(order):
                ahead.append(score(*order[t + AHEAD]))
            scores = ahead.pop(0)
            if h == 0:
                vs[r, : va_ref.shape[1], :width] = va_ref[r]
                vs[r, va_ref.shape[1] :, :width] = vb_ref[r]
                num = jnp.zeros((cols, width), jnp.float32)
                den = jnp.ones((cols, width), jnp.float32)
            if shift:
                scores = scores - jnp.max(scores, axis=-1, keepdims=True)
            weights = jnp.exp2(scores).astype(jnp.bfloat16)
            both = dot_nn(weights, vs[r])
            on = lane // (width // heads) == h
            num = jnp.where(on, both[:, :width], num)
            den = jnp.where(on, both[:, width:], den)
            if h == heads - 1:
                finish(r, num / den)

    @pl.when(flags[0] > 0)
    def _():
        attend(False)

    @pl.when(flags[0] == 0)
    def _():
        attend(True)

    @pl.when(flags[1] == 0)
    def _():
        for r in range(group):
            used = jnp.max(mask_line(r), keepdims=True) > 0.0
            mean = jnp.mean(vs[r, :, :width].astype(jnp.float32), axis=0, keepdims=True)
            plain = mean * g_ref[r].astype(jnp.float32)
            gated[r] = jnp.where(used, gated[r].astype(jnp.float32), plain).astype(jnp.bfloat16)

    flat = (group * cols, width)
    out = dot_nn(gated[...].reshape(flat), wo_ref[...])
    out = x_ref[...].reshape(flat).astype(jnp.float32) + out
    out_ref[...] = out.astype(jnp.bfloat16).reshape(out_ref.shape)


def attention(me, bias, wo, reach, q, g, x, ka, va, kb, vb, blocks, chunk, filled, group=4):
    halves, _, heads, _, _ = bias[0].shape
    rows, cols, width = q.shape
    one = lambda c: pl.BlockSpec((group, c, width), lambda i: (i, 0, 0))
    last = pl.BlockSpec((1, cols, width), lambda i: (rows, 0, 0))
    na, nb = ka.shape[1], kb.shape[1]
    return pl.pallas_call(
        functools.partial(attention_kernel, halves),
        grid=(rows // group,),
        out_shape=jax.ShapeDtypeStruct((CHUNKS * rows, cols, width), jnp.bfloat16),
        in_specs=[SMEM, VMEM, VMEM, VMEM, VMEM]
        + [one(cols)] * 3
        + [one(na), one(na), one(nb), one(nb)]
        + [last] * halves
        + [pl.BlockSpec(memory_space=pl.ANY)] * len(filled),
        out_specs=pl.BlockSpec((group, cols, width), lambda i: (chunk * (rows // group) + i, 0, 0)),
        input_output_aliases={12 + halves: 0} if filled else {},
        scratch_shapes=[
            pltpu.SMEM((2,), jnp.int32),
            pltpu.VMEM((halves, rows * cols // 128, 128), jnp.float32),
            pltpu.VMEM((group, halves * cols, 2 * width), jnp.bfloat16),
            pltpu.VMEM((heads, cols, halves * cols), jnp.float32),
            pltpu.VMEM((group, cols, width), jnp.bfloat16),
        ],
        compiler_params=PARAMS,
        cost_estimate=pl.CostEstimate(
            flops=8 * rows * 4 * cols * halves * cols * width * 2,
            bytes_accessed=8 * rows * cols * width * halves,
            transcendentals=rows * 4 * cols * cols * halves,
        ),
    )(me, *bias, wo, reach, q, g, x, ka, va, kb, vb, *blocks, *filled)


def shards(sizes, pair, pair_mask, gains, w_tri, w_tri_out, w_att, w_bias, w_att_out):
    n_rows, halves = sizes
    rows, cols, width = pair.shape
    heads = w_bias.shape[1]
    lr = edges(pair, pair_mask, gains, w_tri)
    lr = lax.all_to_all(lr, AXES, split_axis=0, concat_axis=0, tiled=True)
    gates = gate(pair, gains, w_tri)
    prod = product(lr.reshape(n_rows, halves, 2, rows, cols))
    back = lax.all_to_all(
        prod.reshape(width, rows, cols), AXES, split_axis=0, concat_axis=0, tiled=True
    )
    wb = jnp.pad(w_bias.T, ((0, 8 - heads), (0, 0)))
    mask_flat = pair_mask.astype(jnp.bfloat16).reshape(rows * cols // width, width)
    up = [(y, (y + 1) % halves) for y in range(halves)]
    down = [(y, (y - 1) % halves) for y in range(halves)]
    after, blocks, bias = [], [], []
    for c in range(CHUNKS):
        x, own, b = tri_output(
            back, pair, gates, mask_flat, gains, gains[1][:, None], w_tri_out, wb, heads, c
        )
        prev = lax.ppermute(own, "half", up)
        next_ = lax.ppermute(own, "half", down)
        far = lax.ppermute(prev, "half", up) if c % 2 == 0 else lax.ppermute(next_, "half", down)
        after.append(x)
        blocks.append((own, prev, next_, far))
        bias.append(b)
    inner = n_rows // halves
    swap = [
        ((z * inner + k) * halves + y, (y * inner + k) * halves + z)
        for z in range(halves)
        for k in range(inner)
        for y in range(halves)
    ]
    bias = jnp.swapaxes(jnp.concatenate(bias, axis=0), 0, 1)
    bias = lax.ppermute(bias, AXES, swap)
    half_rows = n_rows // 2
    bias = jnp.broadcast_to(bias[None], (half_rows,) + bias.shape)
    cores = [[2 * t + core for t in range(half_rows)] for core in range(2)]
    bias = lax.all_to_all(
        bias, "rows", split_axis=0, concat_axis=0, axis_index_groups=cores, tiled=True
    )
    other = lax.ppermute(bias, "rows", [(r, r ^ 1) for r in range(n_rows)])
    bias = [v.reshape(halves, inner // 2, heads, rows, cols) for v in (bias, other)]

    me = jnp.stack([lax.axis_index("half"), lax.axis_index("rows") & 1]).astype(jnp.int32)
    out = []
    for c, (own, prev, next_, far) in enumerate(blocks):
        q, g, ka, va, top = project((own, prev, next_), w_att)
        if out:
            far, out[0] = lax.optimization_barrier((far, out[0]))
        kb, vb, reach = project_last(far, q, top, w_att)
        out = [
            attention(
                me, bias, w_att_out, reach, q, g, after[c], ka, va, kb, vb, blocks[c], c, out
            )
        ]
    return out[0]


def solution(mesh):
    sizes = (mesh.shape["rows"], mesh.shape["half"])
    in_specs = (P("rows", "half", None), P("rows", "half"), P(), P(), P(), P(), P(), P())
    out_specs = P("rows", "half", None)
    return jax.shard_map(
        functools.partial(shards, sizes),
        mesh=mesh,
        in_specs=in_specs,
        out_specs=out_specs,
        check_vma=False,
    )
```

```python
import functools

import jax
import jax.numpy as jnp
from jax import lax
from jax.experimental import pallas as pl
from jax.experimental.pallas import tpu as pltpu
from jax.sharding import PartitionSpec as P

LOG2E = 1.4426950408889634
NEG = -1e30
SAFE = 100.0
AXES = ("rows", "half")
VMEM = pl.BlockSpec(memory_space=pltpu.VMEM)
SMEM = pl.BlockSpec(memory_space=pltpu.SMEM)
PARAMS = pltpu.CompilerParams(vmem_limit_bytes=62 << 20)
CHUNKS = 2


def dot_nn(a, b):
    return lax.dot_general(a, b, (((1,), (0,)), ((), ())), preferred_element_type=jnp.float32)


def dot_nt(a, b):
    return lax.dot_general(a, b, (((1,), (1,)), ((), ())), preferred_element_type=jnp.float32)


def dot_tn(a, b):
    return lax.dot_general(a, b, (((0,), (0,)), ((), ())), preferred_element_type=jnp.float32)


def sigmoid(x):
    return 0.5 * jnp.tanh(0.5 * x) + 0.5


def norm_lanes(x, gain):
    x = x.astype(jnp.float32)
    center = x - jnp.mean(x, axis=-1, keepdims=True)
    spread = jnp.mean(center * center, axis=-1, keepdims=True)
    return (center * lax.rsqrt(spread + 1e-05) * gain).astype(jnp.bfloat16)


def norm_sublanes(x, gain):
    x = x.astype(jnp.float32)
    center = x - jnp.mean(x, axis=0, keepdims=True)
    spread = jnp.mean(center * center, axis=0, keepdims=True)
    return (center * lax.rsqrt(spread + 1e-05) * gain).astype(jnp.bfloat16)


def edges_kernel(pair_ref, mask_ref, gain_ref, w_ref, out_ref, scr):
    group, cols, width = pair_ref.shape
    gain = gain_ref[0:1, :]
    wt = w_ref[:, : 4 * width].T

    def some(t, carry):
        x = pair_ref[pl.ds(t * EDGE_ROWS, EDGE_ROWS)].reshape(EDGE_ROWS * cols, width)
        mixed = dot_nt(wt, norm_lanes(x, gain))
        m = jnp.concatenate(
            [mask_ref[pl.ds(t * EDGE_ROWS + r, 1), :] for r in range(EDGE_ROWS)], axis=1
        ).astype(jnp.float32)
        left = m * sigmoid(mixed[width : 2 * width]) * mixed[:width]
        right = m * sigmoid(mixed[3 * width :]) * mixed[2 * width : 3 * width]
        for e, edge in enumerate((left, right)):
            for r in range(EDGE_ROWS):
                for s in range(cols // 128):
                    at = r * cols + s * 128
                    scr[e, s, pl.ds(t * EDGE_ROWS + r, width, stride=group), :] = edge[:, at : at + 128]
        return carry

    lax.fori_loop(0, group // EDGE_ROWS, some, 0, unroll=EDGE_UNROLL)
    for e in range(2):
        for s in range(cols // 128):
            out_ref[:, e, :, s * 128 : (s + 1) * 128] = (
                scr[e, s].reshape(width, group, 128).astype(jnp.bfloat16)
            )


EDGE_UNROLL = 1
EDGE_ROWS = 8


def edges(pair, mask, gains, w, group=16):
    rows, cols, width = pair.shape
    return pl.pallas_call(
        edges_kernel,
        grid=(rows // group,),
        out_shape=jax.ShapeDtypeStruct((width, 2, rows, cols), jnp.bfloat16),
        in_specs=[
            pl.BlockSpec((group, cols, width), lambda i: (i, 0, 0)),
            pl.BlockSpec((group, cols), lambda i: (i, 0)),
            VMEM,
            VMEM,
        ],
        out_specs=pl.BlockSpec((width, 2, group, cols), lambda i: (0, 0, i, 0)),
        scratch_shapes=[pltpu.VMEM((2, cols // 128, width * group, 128), jnp.float32)],
        compiler_params=PARAMS,
    )(pair, mask, gains, w)


def gate_kernel(pair_ref, gain_ref, w_ref, out_ref):
    group, cols, width = pair_ref.shape
    normed = norm_lanes(pair_ref[...].reshape(group * cols, width), gain_ref[0:1, :])
    gates = sigmoid(dot_nn(normed, w_ref[:, 4 * width :])).astype(jnp.bfloat16)
    out_ref[...] = gates.reshape(group, cols, width)


def gate(pair, gains, w, group=8):
    rows, cols, width = pair.shape
    block = pl.BlockSpec((group, cols, width), lambda i: (i, 0, 0))
    return pl.pallas_call(
        gate_kernel,
        grid=(rows // group,),
        out_shape=jax.ShapeDtypeStruct(pair.shape, jnp.bfloat16),
        in_specs=[block, VMEM, VMEM],
        out_specs=block,
        compiler_params=PARAMS,
        cost_estimate=pl.CostEstimate(
            flops=6 * rows * cols * width * width,
            bytes_accessed=4 * rows * cols * width,
            transcendentals=rows * cols * width,
        ),
    )(pair, gains, w)


PRODUCT_ROWS = 512


def product_kernel(lr_ref, out_ref):
    blocks, halves, _, rows, cols = lr_ref.shape
    step = PRODUCT_ROWS // rows

    def tile(t, carry):
        acc = None
        for h in range(halves):
            left = lr_ref[pl.ds(t * step, step), h, 0].reshape(step * rows, cols)
            right = lr_ref[:, h, 1].reshape(blocks * rows, cols)
            part = dot_nt(left, right)
            acc = part if acc is None else acc + part
        for h in range(halves):
            out_ref[pl.ds(t * step, step), h] = (
                acc[:, h * cols : (h + 1) * cols].reshape(step, rows, cols).astype(jnp.bfloat16)
            )
        return carry

    lax.fori_loop(0, blocks // step, tile, 0)


def product(lr):
    blocks, halves, _, rows, cols = lr.shape
    return pl.pallas_call(
        product_kernel,
        out_shape=jax.ShapeDtypeStruct((blocks, halves, rows, cols), jnp.bfloat16),
        in_specs=[VMEM],
        out_specs=VMEM,
        compiler_params=PARAMS,
    )(lr)


OUT_ROWS = 8


def output_kernel(prod_ref, pair_ref, gate_ref, mask_ref, gain_ref, gcol_ref, wo_ref, wb_ref, after_ref, norm_ref, bias_ref, scr):
    width, rows, cols = prod_ref.shape
    heads = bias_ref.shape[1]
    for s in range(cols // 128):
        for c in range(0, width, 16):
            part = prod_ref[c : c + 16, :, s * 128 : (s + 1) * 128].astype(jnp.float32)
            scr[s, c * rows : (c + 16) * rows, :] = part.reshape(16 * rows, 128)

    def some(t, carry):
        i = t * OUT_ROWS
        x = jnp.concatenate(
            [
                scr[s, pl.ds(i + r, width, stride=rows), :]
                for r in range(OUT_ROWS)
                for s in range(cols // 128)
            ],
            axis=1,
        )
        normed = norm_sublanes(x.astype(jnp.bfloat16), gcol_ref[...])
        update = dot_tn(normed, wo_ref[...])
        here = pl.ds(i, OUT_ROWS)
        flat = (OUT_ROWS * cols, width)
        p = pair_ref[here].reshape(flat).astype(jnp.float32)
        after = p + gate_ref[here].reshape(flat).astype(jnp.float32) * update
        after = after.astype(jnp.bfloat16)
        after_ref[here] = after.reshape(OUT_ROWS, cols, width)
        a = norm_lanes(after, gain_ref[2:3, :])
        norm_ref[here] = a.reshape(OUT_ROWS, cols, width)
        bias = (dot_nt(wb_ref[...], a) * LOG2E).astype(jnp.bfloat16)
        for r in range(OUT_ROWS):
            bias_ref[i + r] = bias[:heads, r * cols : (r + 1) * cols]
        return carry

    lax.fori_loop(0, rows // OUT_ROWS, some, 0)
    used = rows * cols // width
    norm_ref[rows, :used, :] = mask_ref[...]
    norm_ref[rows, used:, :] = jnp.zeros((cols - used, width), jnp.bfloat16)


def tri_output(prod, pair, gates, mask_flat, gains, gcol, wo, wb, heads, chunk):
    width, rows, cols = prod.shape
    rows //= CHUNKS
    block = pl.BlockSpec((rows, cols, width), lambda i: (chunk, 0, 0))
    return pl.pallas_call(
        output_kernel,
        grid=(1,),
        out_shape=(
            jax.ShapeDtypeStruct((rows, cols, width), jnp.bfloat16),
            jax.ShapeDtypeStruct((rows + 1, cols, width), jnp.bfloat16),
            jax.ShapeDtypeStruct((rows, heads, cols), jnp.bfloat16),
        ),
        in_specs=[
            pl.BlockSpec((width, rows, cols), lambda i: (0, chunk, 0)),
            block,
            block,
            pl.BlockSpec((rows * cols // width, width), lambda i: (chunk, 0)),
        ]
        + [VMEM] * 4,
        out_specs=(VMEM,) * 3,
        scratch_shapes=[pltpu.VMEM((cols // 128, width * rows, 128), jnp.float32)],
        compiler_params=PARAMS,
    )(prod, pair, gates, mask_flat, gains, gcol, wo, wb)


def project_kernel(w_ref, *refs):
    width = w_ref.shape[0]
    xs = refs[:-5]
    q_ref, g_ref, k_ref, v_ref, m_ref = refs[-5:]
    group, cols, _ = xs[0].shape
    scale = LOG2E * HEAD_DIM**-0.5
    tops = [None] * group
    for b, x_ref in enumerate(xs):
        a = x_ref[...].reshape(group * cols, width)
        at = slice(b * cols, (b + 1) * cols)
        if b == 0:
            mixed = dot_nn(a, w_ref[...])
            q_ref[...] = (mixed[:, :width] * scale).astype(jnp.bfloat16).reshape(q_ref.shape)
            g_ref[...] = sigmoid(mixed[:, 3 * width :]).astype(jnp.bfloat16).reshape(g_ref.shape)
            kv = mixed[:, width : 3 * width].astype(jnp.bfloat16)
        else:
            kv = dot_nn(a, w_ref[:, width : 3 * width]).astype(jnp.bfloat16)
        k_ref[:, at, :] = kv[:, :width].reshape(group, cols, width)
        v_ref[:, at, :] = kv[:, width:].reshape(group, cols, width)
        for r in range(group):
            m = jnp.max(jnp.abs(kv[r * cols : (r + 1) * cols, :width]), axis=0, keepdims=True)
            tops[r] = m if tops[r] is None else jnp.maximum(tops[r], m)
    for r in range(group):
        m_ref[r] = jnp.broadcast_to(tops[r].astype(jnp.float32), m_ref.shape[1:])


HEAD_DIM = 32
AHEAD = 1


def project(blocks, w, group=8):
    rows, cols, width = blocks[0].shape
    rows -= 1
    n = len(blocks)
    one = lambda c: pl.BlockSpec((group, c, width), lambda i: (i, 0, 0))
    shape = lambda c: jax.ShapeDtypeStruct((rows, c, width), jnp.bfloat16)
    return pl.pallas_call(
        project_kernel,
        grid=(rows // group,),
        out_shape=(shape(cols), shape(cols), shape(n * cols), shape(n * cols), jax.ShapeDtypeStruct((rows, 8, width), jnp.float32)),
        in_specs=[VMEM] + [one(cols)] * n,
        out_specs=(one(cols), one(cols), one(n * cols), one(n * cols), one(8)),
        compiler_params=PARAMS,
        cost_estimate=pl.CostEstimate(
            flops=8 * n * rows * cols * width * width,
            bytes_accessed=8 * n * rows * cols * width,
            transcendentals=rows * cols * width,
        ),
    )(w, *blocks)


def project_last_kernel(w_ref, e_ref, x_ref, q_ref, top_ref, k_ref, v_ref, m_ref):
    width = w_ref.shape[0]
    group, cols, _ = x_ref.shape
    a = x_ref[...].reshape(group * cols, width)
    kv = dot_nn(a, w_ref[:, width : 3 * width]).astype(jnp.bfloat16)
    k_ref[...] = kv[:, :width].reshape(k_ref.shape)
    v_ref[...] = kv[:, width:].reshape(v_ref.shape)
    sized = []
    for r in range(group):
        m = jnp.max(jnp.abs(kv[r * cols : (r + 1) * cols, :width]), axis=0, keepdims=True)
        top = jnp.maximum(m.astype(jnp.float32), top_ref[r, 0:1, :])
        sized.append((jnp.abs(q_ref[r]).astype(jnp.float32) * top).astype(jnp.bfloat16))
    reach = dot_nn(jnp.concatenate(sized, axis=0), e_ref[...])
    for r in range(group):
        m = jnp.max(reach[r * cols : (r + 1) * cols], axis=0, keepdims=True)
        m_ref[r] = jnp.broadcast_to(m, m_ref.shape[1:])


def project_last(block, q, top, w, group=8):
    rows, cols, width = q.shape
    lanes = jnp.arange(width) // HEAD_DIM
    e = (lanes[:, None] == lanes[None, :]).astype(jnp.bfloat16)
    one = lambda c: pl.BlockSpec((group, c, width), lambda i: (i, 0, 0))
    shape = jax.ShapeDtypeStruct((rows, cols, width), jnp.bfloat16)
    return pl.pallas_call(
        project_last_kernel,
        grid=(rows // group,),
        out_shape=(shape, shape, jax.ShapeDtypeStruct((rows, 8, width), jnp.float32)),
        in_specs=[VMEM] * 2 + [one(cols), one(cols), one(8)],
        out_specs=(one(cols), one(cols), one(8)),
        compiler_params=PARAMS,
        cost_estimate=pl.CostEstimate(
            flops=10 * rows * cols * width * width,
            bytes_accessed=8 * rows * cols * width,
            transcendentals=0,
        ),
    )(w, e, block, q, top)


def attention_kernel(halves, me_ref, bias_a_ref, bias_b_ref, wo_ref, reach_ref, *refs):
    q_ref, g_ref, x_ref, ka_ref, va_ref, kb_ref, vb_ref = refs[:7]
    masks = refs[7 : 7 + halves]
    out_ref, flags, mrow, vs, b32, gated = refs[-6:]
    i = pl.program_id(0)
    group, cols, width = q_ref.shape
    _, outer, heads, sub, _ = bias_a_ref.shape
    lane = lax.broadcasted_iota(jnp.int32, (1, width), 1)
    me = me_ref[0]
    where = [lax.rem(me + s, halves) for s in (0, halves - 1, 1, 2)]
    step = cols // 128
    count = mrow.shape[1] // step

    @pl.when(i == 0)
    def _():
        top = jnp.zeros((sub, cols), jnp.float32)
        for s, w in enumerate(where):

            def put(t, top, s=s, w=w):
                for p, piece in enumerate((bias_a_ref, bias_b_ref)):
                    core = me_ref[1] if p == 0 else 1 - me_ref[1]
                    j = pl.ds(pl.multiple_of((2 * t + core) * sub, sub), sub)
                    for h in range(heads):
                        b = piece[w, t, h].astype(jnp.float32)
                        b32[h, j, s * cols : (s + 1) * cols] = b
                        top = jnp.maximum(top, jnp.abs(b))
                return top

            top = lax.fori_loop(0, outer, put, top)
        bound = jnp.max(reach_ref[...]) * 1.02 + jnp.max(top)
        flags[0] = (bound < SAFE).astype(jnp.int32)
        for s in range(halves):
            mrow[s] = masks[s][0, : mrow.shape[1], :].astype(jnp.float32)
        least = None
        seen = jnp.max(mrow[...], axis=0)
        for r in range(count):
            u = jnp.max(seen[r * step : (r + 1) * step], keepdims=True)
            least = u if least is None else jnp.minimum(least, u)
        flags[1] = (jnp.max(least) > 0.0).astype(jnp.int32)
        vs[:, :, width:] = jnp.ones((group, vs.shape[1], width), jnp.bfloat16)

    def mask_line(r):
        at = (i * group + r) * step
        return jnp.concatenate(
            [mrow[s, pl.ds(at + t, 1), :] for s in range(halves) for t in range(step)], axis=1
        )

    def finish(r, attended):
        gated[r] = (attended * g_ref[r].astype(jnp.float32)).astype(jnp.bfloat16)

    def attend(shift):
        def score(r, h):
            q = q_ref[r]
            on = jnp.broadcast_to(lane // (width // heads) == h, q.shape)
            qm = jnp.where(on, q, jnp.zeros_like(q))
            scores = jnp.concatenate([dot_nt(qm, ka_ref[r]), dot_nt(qm, kb_ref[r])], axis=1)
            return scores + b32[h] + jnp.where(mask_line(r) > 0.0, 0.0, NEG)

        order = [(r, h) for r in range(group) for h in range(heads)]
        ahead = [score(*order[t]) for t in range(AHEAD)]
        for t, (r, h) in enumerate(order):
            if t + AHEAD < len(order):
                ahead.append(score(*order[t + AHEAD]))
            scores = ahead.pop(0)
            if h == 0:
                vs[r, : va_ref.shape[1], :width] = va_ref[r]
                vs[r, va_ref.shape[1] :, :width] = vb_ref[r]
                num = jnp.zeros((cols, width), jnp.float32)
                den = jnp.ones((cols, width), jnp.float32)
            if shift:
                scores = scores - jnp.max(scores, axis=-1, keepdims=True)
            weights = jnp.exp2(scores).astype(jnp.bfloat16)
            both = dot_nn(weights, vs[r])
            on = lane // (width // heads) == h
            num = jnp.where(on, both[:, :width], num)
            den = jnp.where(on, both[:, width:], den)
            if h == heads - 1:
                finish(r, num / den)

    @pl.when(flags[0] > 0)
    def _():
        attend(False)

    @pl.when(flags[0] == 0)
    def _():
        attend(True)

    @pl.when(flags[1] == 0)
    def _():
        for r in range(group):
            used = jnp.max(mask_line(r), keepdims=True) > 0.0
            mean = jnp.mean(vs[r, :, :width].astype(jnp.float32), axis=0, keepdims=True)
            plain = mean * g_ref[r].astype(jnp.float32)
            gated[r] = jnp.where(used, gated[r].astype(jnp.float32), plain).astype(jnp.bfloat16)

    flat = (group * cols, width)
    out = dot_nn(gated[...].reshape(flat), wo_ref[...])
    out = x_ref[...].reshape(flat).astype(jnp.float32) + out
    out_ref[...] = out.astype(jnp.bfloat16).reshape(out_ref.shape)


def attention(me, bias, wo, reach, q, g, x, ka, va, kb, vb, blocks, chunk, filled, group=4):
    halves, _, heads, _, _ = bias[0].shape
    rows, cols, width = q.shape
    one = lambda c: pl.BlockSpec((group, c, width), lambda i: (i, 0, 0))
    last = pl.BlockSpec((1, cols, width), lambda i: (rows, 0, 0))
    na, nb = ka.shape[1], kb.shape[1]
    return pl.pallas_call(
        functools.partial(attention_kernel, halves),
        grid=(rows // group,),
        out_shape=jax.ShapeDtypeStruct((CHUNKS * rows, cols, width), jnp.bfloat16),
        in_specs=[SMEM, VMEM, VMEM, VMEM, VMEM]
        + [one(cols)] * 3
        + [one(na), one(na), one(nb), one(nb)]
        + [last] * halves
        + [pl.BlockSpec(memory_space=pl.ANY)] * len(filled),
        out_specs=pl.BlockSpec((group, cols, width), lambda i: (chunk * (rows // group) + i, 0, 0)),
        input_output_aliases={12 + halves: 0} if filled else {},
        scratch_shapes=[
            pltpu.SMEM((2,), jnp.int32),
            pltpu.VMEM((halves, rows * cols // 128, 128), jnp.float32),
            pltpu.VMEM((group, halves * cols, 2 * width), jnp.bfloat16),
            pltpu.VMEM((heads, cols, halves * cols), jnp.float32),
            pltpu.VMEM((group, cols, width), jnp.bfloat16),
        ],
        compiler_params=PARAMS,
        cost_estimate=pl.CostEstimate(
            flops=8 * rows * 4 * cols * halves * cols * width * 2,
            bytes_accessed=8 * rows * cols * width * halves,
            transcendentals=rows * 4 * cols * cols * halves,
        ),
    )(me, *bias, wo, reach, q, g, x, ka, va, kb, vb, *blocks, *filled)


def shards(sizes, pair, pair_mask, gains, w_tri, w_tri_out, w_att, w_bias, w_att_out):
    n_rows, halves = sizes
    rows, cols, width = pair.shape
    heads = w_bias.shape[1]
    lr = edges(pair, pair_mask, gains, w_tri)
    lr = lax.all_to_all(lr, AXES, split_axis=0, concat_axis=0, tiled=True)
    gates = gate(pair, gains, w_tri)
    prod = product(lr.reshape(n_rows, halves, 2, rows, cols))
    back = lax.all_to_all(
        prod.reshape(width, rows, cols), AXES, split_axis=0, concat_axis=0, tiled=True
    )
    wb = jnp.pad(w_bias.T, ((0, 8 - heads), (0, 0)))
    mask_flat = pair_mask.astype(jnp.bfloat16).reshape(rows * cols // width, width)
    up = [(y, (y + 1) % halves) for y in range(halves)]
    down = [(y, (y - 1) % halves) for y in range(halves)]
    after, blocks, bias = [], [], []
    for c in range(CHUNKS):
        x, own, b = tri_output(
            back, pair, gates, mask_flat, gains, gains[1][:, None], w_tri_out, wb, heads, c
        )
        prev = lax.ppermute(own, "half", up)
        next_ = lax.ppermute(own, "half", down)
        far = lax.ppermute(prev, "half", up) if c % 2 == 0 else lax.ppermute(next_, "half", down)
        after.append(x)
        blocks.append((own, prev, next_, far))
        bias.append(b)
    inner = n_rows // halves
    swap = [
        ((z * inner + k) * halves + y, (y * inner + k) * halves + z)
        for z in range(halves)
        for k in range(inner)
        for y in range(halves)
    ]
    bias = jnp.swapaxes(jnp.concatenate(bias, axis=0), 0, 1)
    bias = lax.ppermute(bias, AXES, swap)
    bias, p, n = lax.optimization_barrier((bias, *blocks[0][1:3]))
    blocks[0] = (blocks[0][0], p, n, blocks[0][3])
    half_rows = n_rows // 2
    bias = jnp.broadcast_to(bias[None], (half_rows,) + bias.shape)
    cores = [[2 * t + core for t in range(half_rows)] for core in range(2)]
    bias = lax.all_to_all(
        bias, "rows", split_axis=0, concat_axis=0, axis_index_groups=cores, tiled=True
    )
    other = lax.ppermute(bias, "rows", [(r, r ^ 1) for r in range(n_rows)])
    bias = [v.reshape(halves, inner // 2, heads, rows, cols) for v in (bias, other)]

    *bias, p, n = lax.optimization_barrier((*bias, *blocks[1][1:3]))
    blocks[1] = (blocks[1][0], p, n, blocks[1][3])
    me = jnp.stack([lax.axis_index("half"), lax.axis_index("rows") & 1]).astype(jnp.int32)
    out = []
    for c, (own, prev, next_, far) in enumerate(blocks):
        q, g, ka, va, top = project((own, prev, next_), w_att)
        if out:
            far, out[0] = lax.optimization_barrier((far, out[0]))
        kb, vb, reach = project_last(far, q, top, w_att)
        out = [
            attention(
                me, bias, w_att_out, reach, q, g, after[c], ka, va, kb, vb, blocks[c], c, out
            )
        ]
    return out[0]


def solution(mesh):
    sizes = (mesh.shape["rows"], mesh.shape["half"])
    in_specs = (P("rows", "half", None), P("rows", "half"), P(), P(), P(), P(), P(), P())
    out_specs = P("rows", "half", None)
    return jax.shard_map(
        functools.partial(shards, sizes),
        mesh=mesh,
        in_specs=in_specs,
        out_specs=out_specs,
        check_vma=False,
    )
```

```python
import functools

import jax
import jax.numpy as jnp
from jax import lax
from jax.experimental import pallas as pl
from jax.experimental.pallas import tpu as pltpu
from jax.sharding import PartitionSpec as P

LOG2E = 1.4426950408889634
NEG = -1e30
SAFE = 100.0
AXES = ("rows", "half")
VMEM = pl.BlockSpec(memory_space=pltpu.VMEM)
SMEM = pl.BlockSpec(memory_space=pltpu.SMEM)
PARAMS = pltpu.CompilerParams(vmem_limit_bytes=62 << 20)
CHUNKS = 2


def dot_nn(a, b):
    return lax.dot_general(a, b, (((1,), (0,)), ((), ())), preferred_element_type=jnp.float32)


def dot_nt(a, b):
    return lax.dot_general(a, b, (((1,), (1,)), ((), ())), preferred_element_type=jnp.float32)


def dot_tn(a, b):
    return lax.dot_general(a, b, (((0,), (0,)), ((), ())), preferred_element_type=jnp.float32)


def sigmoid(x):
    return 0.5 * jnp.tanh(0.5 * x) + 0.5


def norm_lanes(x, gain):
    x = x.astype(jnp.float32)
    center = x - jnp.mean(x, axis=-1, keepdims=True)
    spread = jnp.mean(center * center, axis=-1, keepdims=True)
    return (center * lax.rsqrt(spread + 1e-05) * gain).astype(jnp.bfloat16)


def norm_sublanes(x, gain):
    x = x.astype(jnp.float32)
    center = x - jnp.mean(x, axis=0, keepdims=True)
    spread = jnp.mean(center * center, axis=0, keepdims=True)
    return (center * lax.rsqrt(spread + 1e-05) * gain).astype(jnp.bfloat16)


def edges_kernel(pair_ref, mask_ref, gain_ref, w_ref, out_ref, scr):
    group, cols, width = pair_ref.shape
    gain = gain_ref[0:1, :]
    wt = w_ref[:, : 4 * width].T

    def some(t, carry):
        x = pair_ref[pl.ds(t * EDGE_ROWS, EDGE_ROWS)].reshape(EDGE_ROWS * cols, width)
        mixed = dot_nt(wt, norm_lanes(x, gain))
        m = jnp.concatenate(
            [mask_ref[pl.ds(t * EDGE_ROWS + r, 1), :] for r in range(EDGE_ROWS)], axis=1
        ).astype(jnp.float32)
        left = m * sigmoid(mixed[width : 2 * width]) * mixed[:width]
        right = m * sigmoid(mixed[3 * width :]) * mixed[2 * width : 3 * width]
        for e, edge in enumerate((left, right)):
            for r in range(EDGE_ROWS):
                for s in range(cols // 128):
                    at = r * cols + s * 128
                    scr[e, s, pl.ds(t * EDGE_ROWS + r, width, stride=group), :] = edge[:, at : at + 128]
        return carry

    lax.fori_loop(0, group // EDGE_ROWS, some, 0, unroll=EDGE_UNROLL)
    for e in range(2):
        for s in range(cols // 128):
            out_ref[:, e, :, s * 128 : (s + 1) * 128] = (
                scr[e, s].reshape(width, group, 128).astype(jnp.bfloat16)
            )


EDGE_UNROLL = 1
EDGE_ROWS = 8


def edges(pair, mask, gains, w, group=8):
    rows, cols, width = pair.shape
    return pl.pallas_call(
        edges_kernel,
        grid=(rows // group,),
        out_shape=jax.ShapeDtypeStruct((width, 2, rows, cols), jnp.bfloat16),
        in_specs=[
            pl.BlockSpec((group, cols, width), lambda i: (i, 0, 0)),
            pl.BlockSpec((group, cols), lambda i: (i, 0)),
            VMEM,
            VMEM,
        ],
        out_specs=pl.BlockSpec((width, 2, group, cols), lambda i: (0, 0, i, 0)),
        scratch_shapes=[pltpu.VMEM((2, cols // 128, width * group, 128), jnp.float32)],
        compiler_params=PARAMS,
    )(pair, mask, gains, w)


def gate_kernel(pair_ref, gain_ref, w_ref, out_ref):
    group, cols, width = pair_ref.shape
    normed = norm_lanes(pair_ref[...].reshape(group * cols, width), gain_ref[0:1, :])
    gates = sigmoid(dot_nn(normed, w_ref[:, 4 * width :])).astype(jnp.bfloat16)
    out_ref[...] = gates.reshape(group, cols, width)


def gate(pair, gains, w, group=8):
    rows, cols, width = pair.shape
    block = pl.BlockSpec((group, cols, width), lambda i: (i, 0, 0))
    return pl.pallas_call(
        gate_kernel,
        grid=(rows // group,),
        out_shape=jax.ShapeDtypeStruct(pair.shape, jnp.bfloat16),
        in_specs=[block, VMEM, VMEM],
        out_specs=block,
        compiler_params=PARAMS,
        cost_estimate=pl.CostEstimate(
            flops=6 * rows * cols * width * width,
            bytes_accessed=4 * rows * cols * width,
            transcendentals=rows * cols * width,
        ),
    )(pair, gains, w)


PRODUCT_ROWS = 512


def product_kernel(lr_ref, out_ref):
    blocks, halves, _, rows, cols = lr_ref.shape
    step = PRODUCT_ROWS // rows

    def tile(t, carry):
        acc = None
        for h in range(halves):
            left = lr_ref[pl.ds(t * step, step), h, 0].reshape(step * rows, cols)
            right = lr_ref[:, h, 1].reshape(blocks * rows, cols)
            part = dot_nt(left, right)
            acc = part if acc is None else acc + part
        for h in range(halves):
            out_ref[pl.ds(t * step, step), h] = (
                acc[:, h * cols : (h + 1) * cols].reshape(step, rows, cols).astype(jnp.bfloat16)
            )
        return carry

    lax.fori_loop(0, blocks // step, tile, 0)


def product(lr):
    blocks, halves, _, rows, cols = lr.shape
    return pl.pallas_call(
        product_kernel,
        out_shape=jax.ShapeDtypeStruct((blocks, halves, rows, cols), jnp.bfloat16),
        in_specs=[VMEM],
        out_specs=VMEM,
        compiler_params=PARAMS,
    )(lr)


OUT_ROWS = 8


def output_kernel(prod_ref, pair_ref, gate_ref, mask_ref, gain_ref, gcol_ref, wo_ref, wb_ref, after_ref, norm_ref, bias_ref, scr):
    width, rows, cols = prod_ref.shape
    heads = bias_ref.shape[1]
    for s in range(cols // 128):
        for c in range(0, width, 16):
            part = prod_ref[c : c + 16, :, s * 128 : (s + 1) * 128].astype(jnp.float32)
            scr[s, c * rows : (c + 16) * rows, :] = part.reshape(16 * rows, 128)

    def some(t, carry):
        i = t * OUT_ROWS
        x = jnp.concatenate(
            [
                scr[s, pl.ds(i + r, width, stride=rows), :]
                for r in range(OUT_ROWS)
                for s in range(cols // 128)
            ],
            axis=1,
        )
        normed = norm_sublanes(x.astype(jnp.bfloat16), gcol_ref[...])
        update = dot_tn(normed, wo_ref[...])
        here = pl.ds(i, OUT_ROWS)
        flat = (OUT_ROWS * cols, width)
        p = pair_ref[here].reshape(flat).astype(jnp.float32)
        after = p + gate_ref[here].reshape(flat).astype(jnp.float32) * update
        after = after.astype(jnp.bfloat16)
        after_ref[here] = after.reshape(OUT_ROWS, cols, width)
        a = norm_lanes(after, gain_ref[2:3, :])
        norm_ref[here] = a.reshape(OUT_ROWS, cols, width)
        bias = (dot_nt(wb_ref[...], a) * LOG2E).astype(jnp.bfloat16)
        for r in range(OUT_ROWS):
            bias_ref[i + r] = bias[:heads, r * cols : (r + 1) * cols]
        return carry

    lax.fori_loop(0, rows // OUT_ROWS, some, 0)
    used = rows * cols // width
    norm_ref[rows, :used, :] = mask_ref[...]
    norm_ref[rows, used:, :] = jnp.zeros((cols - used, width), jnp.bfloat16)


def tri_output(prod, pair, gates, mask_flat, gains, gcol, wo, wb, heads, chunk):
    width, rows, cols = prod.shape
    rows //= CHUNKS
    block = pl.BlockSpec((rows, cols, width), lambda i: (chunk, 0, 0))
    return pl.pallas_call(
        output_kernel,
        grid=(1,),
        out_shape=(
            jax.ShapeDtypeStruct((rows, cols, width), jnp.bfloat16),
            jax.ShapeDtypeStruct((rows + 1, cols, width), jnp.bfloat16),
            jax.ShapeDtypeStruct((rows, heads, cols), jnp.bfloat16),
        ),
        in_specs=[
            pl.BlockSpec((width, rows, cols), lambda i: (0, chunk, 0)),
            block,
            block,
            pl.BlockSpec((rows * cols // width, width), lambda i: (chunk, 0)),
        ]
        + [VMEM] * 4,
        out_specs=(VMEM,) * 3,
        scratch_shapes=[pltpu.VMEM((cols // 128, width * rows, 128), jnp.float32)],
        compiler_params=PARAMS,
    )(prod, pair, gates, mask_flat, gains, gcol, wo, wb)


def project_kernel(w_ref, *refs):
    width = w_ref.shape[0]
    xs = refs[:-5]
    q_ref, g_ref, k_ref, v_ref, m_ref = refs[-5:]
    group, cols, _ = xs[0].shape
    scale = LOG2E * HEAD_DIM**-0.5
    tops = [None] * group
    for b, x_ref in enumerate(xs):
        a = x_ref[...].reshape(group * cols, width)
        at = slice(b * cols, (b + 1) * cols)
        if b == 0:
            mixed = dot_nn(a, w_ref[...])
            q_ref[...] = (mixed[:, :width] * scale).astype(jnp.bfloat16).reshape(q_ref.shape)
            g_ref[...] = sigmoid(mixed[:, 3 * width :]).astype(jnp.bfloat16).reshape(g_ref.shape)
            kv = mixed[:, width : 3 * width].astype(jnp.bfloat16)
        else:
            kv = dot_nn(a, w_ref[:, width : 3 * width]).astype(jnp.bfloat16)
        k_ref[:, at, :] = kv[:, :width].reshape(group, cols, width)
        v_ref[:, at, :] = kv[:, width:].reshape(group, cols, width)
        for r in range(group):
            m = jnp.max(jnp.abs(kv[r * cols : (r + 1) * cols, :width]), axis=0, keepdims=True)
            tops[r] = m if tops[r] is None else jnp.maximum(tops[r], m)
    for r in range(group):
        m_ref[r] = jnp.broadcast_to(tops[r].astype(jnp.float32), m_ref.shape[1:])


HEAD_DIM = 32
AHEAD = 1


def project(blocks, w, group=8):
    rows, cols, width = blocks[0].shape
    rows -= 1
    n = len(blocks)
    one = lambda c: pl.BlockSpec((group, c, width), lambda i: (i, 0, 0))
    shape = lambda c: jax.ShapeDtypeStruct((rows, c, width), jnp.bfloat16)
    return pl.pallas_call(
        project_kernel,
        grid=(rows // group,),
        out_shape=(shape(cols), shape(cols), shape(n * cols), shape(n * cols), jax.ShapeDtypeStruct((rows, 8, width), jnp.float32)),
        in_specs=[VMEM] + [one(cols)] * n,
        out_specs=(one(cols), one(cols), one(n * cols), one(n * cols), one(8)),
        compiler_params=PARAMS,
        cost_estimate=pl.CostEstimate(
            flops=8 * n * rows * cols * width * width,
            bytes_accessed=8 * n * rows * cols * width,
            transcendentals=rows * cols * width,
        ),
    )(w, *blocks)


def project_last_kernel(w_ref, e_ref, x_ref, q_ref, top_ref, k_ref, v_ref, m_ref):
    width = w_ref.shape[0]
    group, cols, _ = x_ref.shape
    a = x_ref[...].reshape(group * cols, width)
    kv = dot_nn(a, w_ref[:, width : 3 * width]).astype(jnp.bfloat16)
    k_ref[...] = kv[:, :width].reshape(k_ref.shape)
    v_ref[...] = kv[:, width:].reshape(v_ref.shape)
    sized = []
    for r in range(group):
        m = jnp.max(jnp.abs(kv[r * cols : (r + 1) * cols, :width]), axis=0, keepdims=True)
        top = jnp.maximum(m.astype(jnp.float32), top_ref[r, 0:1, :])
        sized.append((jnp.abs(q_ref[r]).astype(jnp.float32) * top).astype(jnp.bfloat16))
    reach = dot_nn(jnp.concatenate(sized, axis=0), e_ref[...])
    for r in range(group):
        m = jnp.max(reach[r * cols : (r + 1) * cols], axis=0, keepdims=True)
        m_ref[r] = jnp.broadcast_to(m, m_ref.shape[1:])


def project_last(block, q, top, w, group=8):
    rows, cols, width = q.shape
    lanes = jnp.arange(width) // HEAD_DIM
    e = (lanes[:, None] == lanes[None, :]).astype(jnp.bfloat16)
    one = lambda c: pl.BlockSpec((group, c, width), lambda i: (i, 0, 0))
    shape = jax.ShapeDtypeStruct((rows, cols, width), jnp.bfloat16)
    return pl.pallas_call(
        project_last_kernel,
        grid=(rows // group,),
        out_shape=(shape, shape, jax.ShapeDtypeStruct((rows, 8, width), jnp.float32)),
        in_specs=[VMEM] * 2 + [one(cols), one(cols), one(8)],
        out_specs=(one(cols), one(cols), one(8)),
        compiler_params=PARAMS,
        cost_estimate=pl.CostEstimate(
            flops=10 * rows * cols * width * width,
            bytes_accessed=8 * rows * cols * width,
            transcendentals=0,
        ),
    )(w, e, block, q, top)


def attention_kernel(halves, me_ref, bias_a_ref, bias_b_ref, wo_ref, reach_ref, *refs):
    q_ref, g_ref, x_ref, ka_ref, va_ref, kb_ref, vb_ref = refs[:7]
    masks = refs[7 : 7 + halves]
    out_ref, flags, mrow, vs, b32, gated = refs[-6:]
    i = pl.program_id(0)
    group, cols, width = q_ref.shape
    _, outer, heads, sub, _ = bias_a_ref.shape
    lane = lax.broadcasted_iota(jnp.int32, (1, width), 1)
    me = me_ref[0]
    where = [lax.rem(me + s, halves) for s in (0, halves - 1, 1, 2)]
    step = cols // 128
    count = mrow.shape[1] // step

    @pl.when(i == 0)
    def _():
        top = jnp.zeros((sub, cols), jnp.float32)
        for s, w in enumerate(where):

            def put(t, top, s=s, w=w):
                for p, piece in enumerate((bias_a_ref, bias_b_ref)):
                    core = me_ref[1] if p == 0 else 1 - me_ref[1]
                    j = pl.ds(pl.multiple_of((2 * t + core) * sub, sub), sub)
                    for h in range(heads):
                        b = piece[w, t, h].astype(jnp.float32)
                        b32[h, j, s * cols : (s + 1) * cols] = b
                        top = jnp.maximum(top, jnp.abs(b))
                return top

            top = lax.fori_loop(0, outer, put, top)
        bound = jnp.max(reach_ref[...]) * 1.02 + jnp.max(top)
        flags[0] = (bound < SAFE).astype(jnp.int32)
        for s in range(halves):
            mrow[s] = masks[s][0, : mrow.shape[1], :].astype(jnp.float32)
        least = None
        seen = jnp.max(mrow[...], axis=0)
        for r in range(count):
            u = jnp.max(seen[r * step : (r + 1) * step], keepdims=True)
            least = u if least is None else jnp.minimum(least, u)
        flags[1] = (jnp.max(least) > 0.0).astype(jnp.int32)
        vs[:, :, width:] = jnp.ones((group, vs.shape[1], width), jnp.bfloat16)

    def mask_line(r):
        at = (i * group + r) * step
        return jnp.concatenate(
            [mrow[s, pl.ds(at + t, 1), :] for s in range(halves) for t in range(step)], axis=1
        )

    def finish(r, attended):
        gated[r] = (attended * g_ref[r].astype(jnp.float32)).astype(jnp.bfloat16)

    def attend(shift):
        def score(r, h):
            q = q_ref[r]
            on = jnp.broadcast_to(lane // (width // heads) == h, q.shape)
            qm = jnp.where(on, q, jnp.zeros_like(q))
            scores = jnp.concatenate([dot_nt(qm, ka_ref[r]), dot_nt(qm, kb_ref[r])], axis=1)
            return scores + b32[h] + jnp.where(mask_line(r) > 0.0, 0.0, NEG)

        order = [(r, h) for r in range(group) for h in range(heads)]
        ahead = [score(*order[t]) for t in range(AHEAD)]
        for t, (r, h) in enumerate(order):
            if t + AHEAD < len(order):
                ahead.append(score(*order[t + AHEAD]))
            scores = ahead.pop(0)
            if h == 0:
                vs[r, : va_ref.shape[1], :width] = va_ref[r]
                vs[r, va_ref.shape[1] :, :width] = vb_ref[r]
                num = jnp.zeros((cols, width), jnp.float32)
                den = jnp.ones((cols, width), jnp.float32)
            if shift:
                scores = scores - jnp.max(scores, axis=-1, keepdims=True)
            weights = jnp.exp2(scores).astype(jnp.bfloat16)
            both = dot_nn(weights, vs[r])
            on = lane // (width // heads) == h
            num = jnp.where(on, both[:, :width], num)
            den = jnp.where(on, both[:, width:], den)
            if h == heads - 1:
                finish(r, num / den)

    @pl.when(flags[0] > 0)
    def _():
        attend(False)

    @pl.when(flags[0] == 0)
    def _():
        attend(True)

    @pl.when(flags[1] == 0)
    def _():
        for r in range(group):
            used = jnp.max(mask_line(r), keepdims=True) > 0.0
            mean = jnp.mean(vs[r, :, :width].astype(jnp.float32), axis=0, keepdims=True)
            plain = mean * g_ref[r].astype(jnp.float32)
            gated[r] = jnp.where(used, gated[r].astype(jnp.float32), plain).astype(jnp.bfloat16)

    flat = (group * cols, width)
    out = dot_nn(gated[...].reshape(flat), wo_ref[...])
    out = x_ref[...].reshape(flat).astype(jnp.float32) + out
    out_ref[...] = out.astype(jnp.bfloat16).reshape(out_ref.shape)


def attention(me, bias, wo, reach, q, g, x, ka, va, kb, vb, blocks, chunk, filled, group=4):
    halves, _, heads, _, _ = bias[0].shape
    rows, cols, width = q.shape
    one = lambda c: pl.BlockSpec((group, c, width), lambda i: (i, 0, 0))
    last = pl.BlockSpec((1, cols, width), lambda i: (rows, 0, 0))
    na, nb = ka.shape[1], kb.shape[1]
    return pl.pallas_call(
        functools.partial(attention_kernel, halves),
        grid=(rows // group,),
        out_shape=jax.ShapeDtypeStruct((CHUNKS * rows, cols, width), jnp.bfloat16),
        in_specs=[SMEM, VMEM, VMEM, VMEM, VMEM]
        + [one(cols)] * 3
        + [one(na), one(na), one(nb), one(nb)]
        + [last] * halves
        + [pl.BlockSpec(memory_space=pl.ANY)] * len(filled),
        out_specs=pl.BlockSpec((group, cols, width), lambda i: (chunk * (rows // group) + i, 0, 0)),
        input_output_aliases={12 + halves: 0} if filled else {},
        scratch_shapes=[
            pltpu.SMEM((2,), jnp.int32),
            pltpu.VMEM((halves, rows * cols // 128, 128), jnp.float32),
            pltpu.VMEM((group, halves * cols, 2 * width), jnp.bfloat16),
            pltpu.VMEM((heads, cols, halves * cols), jnp.float32),
            pltpu.VMEM((group, cols, width), jnp.bfloat16),
        ],
        compiler_params=PARAMS,
        cost_estimate=pl.CostEstimate(
            flops=8 * rows * 4 * cols * halves * cols * width * 2,
            bytes_accessed=8 * rows * cols * width * halves,
            transcendentals=rows * 4 * cols * cols * halves,
        ),
    )(me, *bias, wo, reach, q, g, x, ka, va, kb, vb, *blocks, *filled)


def shards(sizes, pair, pair_mask, gains, w_tri, w_tri_out, w_att, w_bias, w_att_out):
    n_rows, halves = sizes
    rows, cols, width = pair.shape
    heads = w_bias.shape[1]
    lr = edges(pair, pair_mask, gains, w_tri)
    lr = lax.all_to_all(lr, AXES, split_axis=0, concat_axis=0, tiled=True)
    gates = gate(pair, gains, w_tri)
    prod = product(lr.reshape(n_rows, halves, 2, rows, cols))
    back = lax.all_to_all(
        prod.reshape(width, rows, cols), AXES, split_axis=0, concat_axis=0, tiled=True
    )
    wb = jnp.pad(w_bias.T, ((0, 8 - heads), (0, 0)))
    mask_flat = pair_mask.astype(jnp.bfloat16).reshape(rows * cols // width, width)
    up = [(y, (y + 1) % halves) for y in range(halves)]
    down = [(y, (y - 1) % halves) for y in range(halves)]
    after, blocks, bias = [], [], []
    for c in range(CHUNKS):
        x, own, b = tri_output(
            back, pair, gates, mask_flat, gains, gains[1][:, None], w_tri_out, wb, heads, c
        )
        prev = lax.ppermute(own, "half", up)
        next_ = lax.ppermute(own, "half", down)
        far = lax.ppermute(prev, "half", up) if c % 2 == 0 else lax.ppermute(next_, "half", down)
        after.append(x)
        blocks.append((own, prev, next_, far))
        bias.append(b)
    inner = n_rows // halves
    swap = [
        ((z * inner + k) * halves + y, (y * inner + k) * halves + z)
        for z in range(halves)
        for k in range(inner)
        for y in range(halves)
    ]
    bias = jnp.swapaxes(jnp.concatenate(bias, axis=0), 0, 1)
    bias = lax.ppermute(bias, AXES, swap)
    near = [b[1:3] for b in blocks]
    bias, near = lax.optimization_barrier((bias, near))
    blocks = [(b[0], *n, b[3]) for b, n in zip(blocks, near)]
    half_rows = n_rows // 2
    bias = jnp.broadcast_to(bias[None], (half_rows,) + bias.shape)
    cores = [[2 * t + core for t in range(half_rows)] for core in range(2)]
    bias = lax.all_to_all(
        bias, "rows", split_axis=0, concat_axis=0, axis_index_groups=cores, tiled=True
    )
    other = lax.ppermute(bias, "rows", [(r, r ^ 1) for r in range(n_rows)])
    bias = [v.reshape(halves, inner // 2, heads, rows, cols) for v in (bias, other)]

    me = jnp.stack([lax.axis_index("half"), lax.axis_index("rows") & 1]).astype(jnp.int32)
    out = []
    for c, (own, prev, next_, far) in enumerate(blocks):
        q, g, ka, va, top = project((own, prev, next_), w_att)
        if out:
            far, out[0] = lax.optimization_barrier((far, out[0]))
        kb, vb, reach = project_last(far, q, top, w_att)
        out = [
            attention(
                me, bias, w_att_out, reach, q, g, after[c], ka, va, kb, vb, blocks[c], c, out
            )
        ]
    return out[0]


def solution(mesh):
    sizes = (mesh.shape["rows"], mesh.shape["half"])
    in_specs = (P("rows", "half", None), P("rows", "half"), P(), P(), P(), P(), P(), P())
    out_specs = P("rows", "half", None)
    return jax.shard_map(
        functools.partial(shards, sizes),
        mesh=mesh,
        in_specs=in_specs,
        out_specs=out_specs,
        check_vma=False,
    )
```

```python
import functools

import jax
import jax.numpy as jnp
from jax import lax
from jax.experimental import pallas as pl
from jax.experimental.pallas import tpu as pltpu
from jax.sharding import PartitionSpec as P

LOG2E = 1.4426950408889634
NEG = -1e30
SAFE = 100.0
AXES = ("rows", "half")
VMEM = pl.BlockSpec(memory_space=pltpu.VMEM)
SMEM = pl.BlockSpec(memory_space=pltpu.SMEM)
PARAMS = pltpu.CompilerParams(vmem_limit_bytes=62 << 20)
CHUNKS = 2


def dot_nn(a, b):
    return lax.dot_general(a, b, (((1,), (0,)), ((), ())), preferred_element_type=jnp.float32)


def dot_nt(a, b):
    return lax.dot_general(a, b, (((1,), (1,)), ((), ())), preferred_element_type=jnp.float32)


def dot_tn(a, b):
    return lax.dot_general(a, b, (((0,), (0,)), ((), ())), preferred_element_type=jnp.float32)


def sigmoid(x):
    return 0.5 * jnp.tanh(0.5 * x) + 0.5


def norm_lanes(x, gain):
    x = x.astype(jnp.float32)
    center = x - jnp.mean(x, axis=-1, keepdims=True)
    spread = jnp.mean(center * center, axis=-1, keepdims=True)
    return (center * lax.rsqrt(spread + 1e-05) * gain).astype(jnp.bfloat16)


def norm_sublanes(x, gain):
    x = x.astype(jnp.float32)
    center = x - jnp.mean(x, axis=0, keepdims=True)
    spread = jnp.mean(center * center, axis=0, keepdims=True)
    return (center * lax.rsqrt(spread + 1e-05) * gain).astype(jnp.bfloat16)


def edges_kernel(pair_ref, mask_ref, gain_ref, w_ref, out_ref, scr):
    group, cols, width = pair_ref.shape
    gain = gain_ref[0:1, :]
    wt = w_ref[:, : 4 * width].T

    def some(t, carry):
        x = pair_ref[pl.ds(t * EDGE_ROWS, EDGE_ROWS)].reshape(EDGE_ROWS * cols, width)
        mixed = dot_nt(wt, norm_lanes(x, gain))
        m = jnp.concatenate(
            [mask_ref[pl.ds(t * EDGE_ROWS + r, 1), :] for r in range(EDGE_ROWS)], axis=1
        ).astype(jnp.float32)
        left = m * sigmoid(mixed[width : 2 * width]) * mixed[:width]
        right = m * sigmoid(mixed[3 * width :]) * mixed[2 * width : 3 * width]
        for e, edge in enumerate((left, right)):
            for r in range(EDGE_ROWS):
                for s in range(cols // 128):
                    at = r * cols + s * 128
                    scr[e, s, pl.ds(t * EDGE_ROWS + r, width, stride=group), :] = edge[:, at : at + 128]
        return carry

    lax.fori_loop(0, group // EDGE_ROWS, some, 0, unroll=EDGE_UNROLL)
    for e in range(2):
        for s in range(cols // 128):
            out_ref[:, e, :, s * 128 : (s + 1) * 128] = (
                scr[e, s].reshape(width, group, 128).astype(jnp.bfloat16)
            )


EDGE_UNROLL = 1
EDGE_ROWS = 8


def edges(pair, mask, gains, w, group=8):
    rows, cols, width = pair.shape
    return pl.pallas_call(
        edges_kernel,
        grid=(rows // group,),
        out_shape=jax.ShapeDtypeStruct((width, 2, rows, cols), jnp.bfloat16),
        in_specs=[
            pl.BlockSpec((group, cols, width), lambda i: (i, 0, 0)),
            pl.BlockSpec((group, cols), lambda i: (i, 0)),
            VMEM,
            VMEM,
        ],
        out_specs=pl.BlockSpec((width, 2, group, cols), lambda i: (0, 0, i, 0)),
        scratch_shapes=[pltpu.VMEM((2, cols // 128, width * group, 128), jnp.float32)],
        compiler_params=PARAMS,
    )(pair, mask, gains, w)


def gate_kernel(pair_ref, gain_ref, w_ref, out_ref):
    group, cols, width = pair_ref.shape
    normed = norm_lanes(pair_ref[...].reshape(group * cols, width), gain_ref[0:1, :])
    gates = sigmoid(dot_nn(normed, w_ref[:, 4 * width :])).astype(jnp.bfloat16)
    out_ref[...] = gates.reshape(group, cols, width)


def gate(pair, gains, w, group=8):
    rows, cols, width = pair.shape
    block = pl.BlockSpec((group, cols, width), lambda i: (i, 0, 0))
    return pl.pallas_call(
        gate_kernel,
        grid=(rows // group,),
        out_shape=jax.ShapeDtypeStruct(pair.shape, jnp.bfloat16),
        in_specs=[block, VMEM, VMEM],
        out_specs=block,
        compiler_params=PARAMS,
        cost_estimate=pl.CostEstimate(
            flops=6 * rows * cols * width * width,
            bytes_accessed=4 * rows * cols * width,
            transcendentals=rows * cols * width,
        ),
    )(pair, gains, w)


PRODUCT_ROWS = 512


def product_kernel(lr_ref, out_ref):
    blocks, halves, _, rows, cols = lr_ref.shape
    step = PRODUCT_ROWS // rows

    def tile(t, carry):
        acc = None
        for h in range(halves):
            left = lr_ref[pl.ds(t * step, step), h, 0].reshape(step * rows, cols)
            right = lr_ref[:, h, 1].reshape(blocks * rows, cols)
            part = dot_nt(left, right)
            acc = part if acc is None else acc + part
        for h in range(halves):
            out_ref[pl.ds(t * step, step), h] = (
                acc[:, h * cols : (h + 1) * cols].reshape(step, rows, cols).astype(jnp.bfloat16)
            )
        return carry

    lax.fori_loop(0, blocks // step, tile, 0)


def product(lr):
    blocks, halves, _, rows, cols = lr.shape
    return pl.pallas_call(
        product_kernel,
        out_shape=jax.ShapeDtypeStruct((blocks, halves, rows, cols), jnp.bfloat16),
        in_specs=[VMEM],
        out_specs=VMEM,
        compiler_params=PARAMS,
    )(lr)


OUT_ROWS = 8


def output_kernel(prod_ref, pair_ref, gate_ref, mask_ref, gain_ref, gcol_ref, wo_ref, wb_ref, after_ref, norm_ref, bias_ref, scr):
    width, rows, cols = prod_ref.shape
    heads = bias_ref.shape[1]
    for s in range(cols // 128):
        for c in range(0, width, 16):
            part = prod_ref[c : c + 16, :, s * 128 : (s + 1) * 128].astype(jnp.float32)
            scr[s, c * rows : (c + 16) * rows, :] = part.reshape(16 * rows, 128)

    def some(t, carry):
        i = t * OUT_ROWS
        x = jnp.concatenate(
            [
                scr[s, pl.ds(i + r, width, stride=rows), :]
                for r in range(OUT_ROWS)
                for s in range(cols // 128)
            ],
            axis=1,
        )
        normed = norm_sublanes(x.astype(jnp.bfloat16), gcol_ref[...])
        update = dot_tn(normed, wo_ref[...])
        here = pl.ds(i, OUT_ROWS)
        flat = (OUT_ROWS * cols, width)
        p = pair_ref[here].reshape(flat).astype(jnp.float32)
        after = p + gate_ref[here].reshape(flat).astype(jnp.float32) * update
        after = after.astype(jnp.bfloat16)
        after_ref[here] = after.reshape(OUT_ROWS, cols, width)
        a = norm_lanes(after, gain_ref[2:3, :])
        norm_ref[here] = a.reshape(OUT_ROWS, cols, width)
        bias = (dot_nt(wb_ref[...], a) * LOG2E).astype(jnp.bfloat16)
        for r in range(OUT_ROWS):
            bias_ref[i + r] = bias[:heads, r * cols : (r + 1) * cols]
        return carry

    lax.fori_loop(0, rows // OUT_ROWS, some, 0)
    used = rows * cols // width
    norm_ref[rows, :used, :] = mask_ref[...]
    norm_ref[rows, used:, :] = jnp.zeros((cols - used, width), jnp.bfloat16)


def tri_output(prod, pair, gates, mask_flat, gains, gcol, wo, wb, heads, chunk):
    width, rows, cols = prod.shape
    rows //= CHUNKS
    block = pl.BlockSpec((rows, cols, width), lambda i: (chunk, 0, 0))
    return pl.pallas_call(
        output_kernel,
        grid=(1,),
        out_shape=(
            jax.ShapeDtypeStruct((rows, cols, width), jnp.bfloat16),
            jax.ShapeDtypeStruct((rows + 1, cols, width), jnp.bfloat16),
            jax.ShapeDtypeStruct((rows, heads, cols), jnp.bfloat16),
        ),
        in_specs=[
            pl.BlockSpec((width, rows, cols), lambda i: (0, chunk, 0)),
            block,
            block,
            pl.BlockSpec((rows * cols // width, width), lambda i: (chunk, 0)),
        ]
        + [VMEM] * 4,
        out_specs=(VMEM,) * 3,
        scratch_shapes=[pltpu.VMEM((cols // 128, width * rows, 128), jnp.float32)],
        compiler_params=PARAMS,
    )(prod, pair, gates, mask_flat, gains, gcol, wo, wb)


def project_kernel(w_ref, *refs):
    width = w_ref.shape[0]
    xs = refs[:-5]
    q_ref, g_ref, k_ref, v_ref, m_ref = refs[-5:]
    group, cols, _ = xs[0].shape
    scale = LOG2E * HEAD_DIM**-0.5
    tops = [None] * group
    for b, x_ref in enumerate(xs):
        a = x_ref[...].reshape(group * cols, width)
        at = slice(b * cols, (b + 1) * cols)
        if b == 0:
            mixed = dot_nn(a, w_ref[...])
            q_ref[...] = (mixed[:, :width] * scale).astype(jnp.bfloat16).reshape(q_ref.shape)
            g_ref[...] = sigmoid(mixed[:, 3 * width :]).astype(jnp.bfloat16).reshape(g_ref.shape)
            kv = mixed[:, width : 3 * width].astype(jnp.bfloat16)
        else:
            kv = dot_nn(a, w_ref[:, width : 3 * width]).astype(jnp.bfloat16)
        k_ref[:, at, :] = kv[:, :width].reshape(group, cols, width)
        v_ref[:, at, :] = kv[:, width:].reshape(group, cols, width)
        for r in range(group):
            m = jnp.max(jnp.abs(kv[r * cols : (r + 1) * cols, :width]), axis=0, keepdims=True)
            tops[r] = m if tops[r] is None else jnp.maximum(tops[r], m)
    for r in range(group):
        m_ref[r] = jnp.broadcast_to(tops[r].astype(jnp.float32), m_ref.shape[1:])


HEAD_DIM = 32
AHEAD = 1


def project(blocks, w, group=8):
    rows, cols, width = blocks[0].shape
    rows -= 1
    n = len(blocks)
    one = lambda c: pl.BlockSpec((group, c, width), lambda i: (i, 0, 0))
    shape = lambda c: jax.ShapeDtypeStruct((rows, c, width), jnp.bfloat16)
    return pl.pallas_call(
        project_kernel,
        grid=(rows // group,),
        out_shape=(shape(cols), shape(cols), shape(n * cols), shape(n * cols), jax.ShapeDtypeStruct((rows, 8, width), jnp.float32)),
        in_specs=[VMEM] + [one(cols)] * n,
        out_specs=(one(cols), one(cols), one(n * cols), one(n * cols), one(8)),
        compiler_params=PARAMS,
        cost_estimate=pl.CostEstimate(
            flops=8 * n * rows * cols * width * width,
            bytes_accessed=8 * n * rows * cols * width,
            transcendentals=rows * cols * width,
        ),
    )(w, *blocks)


def project_last_kernel(w_ref, e_ref, x_ref, q_ref, top_ref, k_ref, v_ref, m_ref):
    width = w_ref.shape[0]
    group, cols, _ = x_ref.shape
    a = x_ref[...].reshape(group * cols, width)
    kv = dot_nn(a, w_ref[:, width : 3 * width]).astype(jnp.bfloat16)
    k_ref[...] = kv[:, :width].reshape(k_ref.shape)
    v_ref[...] = kv[:, width:].reshape(v_ref.shape)
    sized = []
    for r in range(group):
        m = jnp.max(jnp.abs(kv[r * cols : (r + 1) * cols, :width]), axis=0, keepdims=True)
        top = jnp.maximum(m.astype(jnp.float32), top_ref[r, 0:1, :])
        sized.append((jnp.abs(q_ref[r]).astype(jnp.float32) * top).astype(jnp.bfloat16))
    reach = dot_nn(jnp.concatenate(sized, axis=0), e_ref[...])
    for r in range(group):
        m = jnp.max(reach[r * cols : (r + 1) * cols], axis=0, keepdims=True)
        m_ref[r] = jnp.broadcast_to(m, m_ref.shape[1:])


def project_last(block, q, top, w, group=8):
    rows, cols, width = q.shape
    lanes = jnp.arange(width) // HEAD_DIM
    e = (lanes[:, None] == lanes[None, :]).astype(jnp.bfloat16)
    one = lambda c: pl.BlockSpec((group, c, width), lambda i: (i, 0, 0))
    shape = jax.ShapeDtypeStruct((rows, cols, width), jnp.bfloat16)
    return pl.pallas_call(
        project_last_kernel,
        grid=(rows // group,),
        out_shape=(shape, shape, jax.ShapeDtypeStruct((rows, 8, width), jnp.float32)),
        in_specs=[VMEM] * 2 + [one(cols), one(cols), one(8)],
        out_specs=(one(cols), one(cols), one(8)),
        compiler_params=PARAMS,
        cost_estimate=pl.CostEstimate(
            flops=10 * rows * cols * width * width,
            bytes_accessed=8 * rows * cols * width,
            transcendentals=0,
        ),
    )(w, e, block, q, top)


def attention_kernel(halves, me_ref, bias_a_ref, bias_b_ref, wo_ref, reach_ref, *refs):
    q_ref, g_ref, x_ref, ka_ref, va_ref, kb_ref, vb_ref = refs[:7]
    masks = refs[7 : 7 + halves]
    out_ref, flags, mrow, vs, b32, gated = refs[-6:]
    i = pl.program_id(0)
    group, cols, width = q_ref.shape
    _, outer, heads, sub, _ = bias_a_ref.shape
    lane = lax.broadcasted_iota(jnp.int32, (1, width), 1)
    me = me_ref[0]
    where = [lax.rem(me + s, halves) for s in (0, halves - 1, 1, 2)]
    step = cols // 128
    count = mrow.shape[1] // step

    @pl.when(i == 0)
    def _():
        top = jnp.zeros((sub, cols), jnp.float32)
        for s, w in enumerate(where):

            def put(t, top, s=s, w=w):
                for p, piece in enumerate((bias_a_ref, bias_b_ref)):
                    core = me_ref[1] if p == 0 else 1 - me_ref[1]
                    j = pl.ds(pl.multiple_of((2 * t + core) * sub, sub), sub)
                    for h in range(heads):
                        b = piece[w, t, h].astype(jnp.float32)
                        b32[h, j, s * cols : (s + 1) * cols] = b
                        top = jnp.maximum(top, jnp.abs(b))
                return top

            top = lax.fori_loop(0, outer, put, top)
        bound = jnp.max(reach_ref[...]) * 1.02 + jnp.max(top)
        flags[0] = (bound < SAFE).astype(jnp.int32)
        for s in range(halves):
            mrow[s] = masks[s][0, : mrow.shape[1], :].astype(jnp.float32)
        least = None
        seen = jnp.max(mrow[...], axis=0)
        for r in range(count):
            u = jnp.max(seen[r * step : (r + 1) * step], keepdims=True)
            least = u if least is None else jnp.minimum(least, u)
        flags[1] = (jnp.max(least) > 0.0).astype(jnp.int32)
        vs[:, :, width:] = jnp.ones((group, vs.shape[1], width), jnp.bfloat16)

    def mask_line(r):
        at = (i * group + r) * step
        return jnp.concatenate(
            [mrow[s, pl.ds(at + t, 1), :] for s in range(halves) for t in range(step)], axis=1
        )

    def finish(r, attended):
        gated[r] = (attended * g_ref[r].astype(jnp.float32)).astype(jnp.bfloat16)

    def attend(shift):
        def score(r, h):
            q = q_ref[r]
            on = jnp.broadcast_to(lane // (width // heads) == h, q.shape)
            qm = jnp.where(on, q, jnp.zeros_like(q))
            scores = jnp.concatenate([dot_nt(qm, ka_ref[r]), dot_nt(qm, kb_ref[r])], axis=1)
            return scores + b32[h] + jnp.where(mask_line(r) > 0.0, 0.0, NEG)

        order = [(r, h) for r in range(group) for h in range(heads)]
        ahead = [score(*order[t]) for t in range(AHEAD)]
        for t, (r, h) in enumerate(order):
            if t + AHEAD < len(order):
                ahead.append(score(*order[t + AHEAD]))
            scores = ahead.pop(0)
            if h == 0:
                vs[r, : va_ref.shape[1], :width] = va_ref[r]
                vs[r, va_ref.shape[1] :, :width] = vb_ref[r]
                num = jnp.zeros((cols, width), jnp.float32)
                den = jnp.ones((cols, width), jnp.float32)
            if shift:
                scores = scores - jnp.max(scores, axis=-1, keepdims=True)
            weights = jnp.exp2(scores).astype(jnp.bfloat16)
            both = dot_nn(weights, vs[r])
            on = lane // (width // heads) == h
            num = jnp.where(on, both[:, :width], num)
            den = jnp.where(on, both[:, width:], den)
            if h == heads - 1:
                finish(r, num / den)

    @pl.when(flags[0] > 0)
    def _():
        attend(False)

    @pl.when(flags[0] == 0)
    def _():
        attend(True)

    @pl.when(flags[1] == 0)
    def _():
        for r in range(group):
            used = jnp.max(mask_line(r), keepdims=True) > 0.0
            mean = jnp.mean(vs[r, :, :width].astype(jnp.float32), axis=0, keepdims=True)
            plain = mean * g_ref[r].astype(jnp.float32)
            gated[r] = jnp.where(used, gated[r].astype(jnp.float32), plain).astype(jnp.bfloat16)

    flat = (group * cols, width)
    out = dot_nn(gated[...].reshape(flat), wo_ref[...])
    out = x_ref[...].reshape(flat).astype(jnp.float32) + out
    out_ref[...] = out.astype(jnp.bfloat16).reshape(out_ref.shape)


def attention(me, bias, wo, reach, q, g, x, ka, va, kb, vb, blocks, chunk, filled, group=4):
    halves, _, heads, _, _ = bias[0].shape
    rows, cols, width = q.shape
    one = lambda c: pl.BlockSpec((group, c, width), lambda i: (i, 0, 0))
    last = pl.BlockSpec((1, cols, width), lambda i: (rows, 0, 0))
    na, nb = ka.shape[1], kb.shape[1]
    return pl.pallas_call(
        functools.partial(attention_kernel, halves),
        grid=(rows // group,),
        out_shape=jax.ShapeDtypeStruct((CHUNKS * rows, cols, width), jnp.bfloat16),
        in_specs=[SMEM, VMEM, VMEM, VMEM, VMEM]
        + [one(cols)] * 3
        + [one(na), one(na), one(nb), one(nb)]
        + [last] * halves
        + [pl.BlockSpec(memory_space=pl.ANY)] * len(filled),
        out_specs=pl.BlockSpec((group, cols, width), lambda i: (chunk * (rows // group) + i, 0, 0)),
        input_output_aliases={12 + halves: 0} if filled else {},
        scratch_shapes=[
            pltpu.SMEM((2,), jnp.int32),
            pltpu.VMEM((halves, rows * cols // 128, 128), jnp.float32),
            pltpu.VMEM((group, halves * cols, 2 * width), jnp.bfloat16),
            pltpu.VMEM((heads, cols, halves * cols), jnp.float32),
            pltpu.VMEM((group, cols, width), jnp.bfloat16),
        ],
        compiler_params=PARAMS,
        cost_estimate=pl.CostEstimate(
            flops=8 * rows * 4 * cols * halves * cols * width * 2,
            bytes_accessed=8 * rows * cols * width * halves,
            transcendentals=rows * 4 * cols * cols * halves,
        ),
    )(me, *bias, wo, reach, q, g, x, ka, va, kb, vb, *blocks, *filled)


def shards(sizes, pair, pair_mask, gains, w_tri, w_tri_out, w_att, w_bias, w_att_out):
    n_rows, halves = sizes
    rows, cols, width = pair.shape
    heads = w_bias.shape[1]
    lr = edges(pair, pair_mask, gains, w_tri)
    lr = lax.all_to_all(lr, AXES, split_axis=0, concat_axis=0, tiled=True)
    gates = gate(pair, gains, w_tri)
    prod = product(lr.reshape(n_rows, halves, 2, rows, cols))
    back = lax.all_to_all(
        prod.reshape(width, rows, cols), AXES, split_axis=0, concat_axis=0, tiled=True
    )
    wb = jnp.pad(w_bias.T, ((0, 8 - heads), (0, 0)))
    mask_flat = pair_mask.astype(jnp.bfloat16).reshape(rows * cols // width, width)
    up = [(y, (y + 1) % halves) for y in range(halves)]
    down = [(y, (y - 1) % halves) for y in range(halves)]
    after, blocks, bias = [], [], []
    for c in range(CHUNKS):
        x, own, b = tri_output(
            back, pair, gates, mask_flat, gains, gains[1][:, None], w_tri_out, wb, heads, c
        )
        prev = lax.ppermute(own, "half", up)
        next_ = lax.ppermute(own, "half", down)
        far = lax.ppermute(prev, "half", up) if c % 2 == 0 else lax.ppermute(next_, "half", down)
        after.append(x)
        blocks.append((own, prev, next_, far))
        bias.append(b)
    inner = n_rows // halves
    swap = [
        ((z * inner + k) * halves + y, (y * inner + k) * halves + z)
        for z in range(halves)
        for k in range(inner)
        for y in range(halves)
    ]
    bias = jnp.swapaxes(jnp.concatenate(bias, axis=0), 0, 1)
    bias = lax.ppermute(bias, AXES, swap)
    bias, near = lax.optimization_barrier((bias, blocks[0][1:3]))
    blocks[0] = (blocks[0][0], *near, blocks[0][3])
    half_rows = n_rows // 2
    bias = jnp.broadcast_to(bias[None], (half_rows,) + bias.shape)
    cores = [[2 * t + core for t in range(half_rows)] for core in range(2)]
    bias = lax.all_to_all(
        bias, "rows", split_axis=0, concat_axis=0, axis_index_groups=cores, tiled=True
    )
    other = lax.ppermute(bias, "rows", [(r, r ^ 1) for r in range(n_rows)])
    bias = [v.reshape(halves, inner // 2, heads, rows, cols) for v in (bias, other)]

    *bias, near = lax.optimization_barrier((*bias, blocks[1][2]))
    blocks[1] = (*blocks[1][:2], near, blocks[1][3])
    me = jnp.stack([lax.axis_index("half"), lax.axis_index("rows") & 1]).astype(jnp.int32)
    out = []
    for c, (own, prev, next_, far) in enumerate(blocks):
        if out:
            prev, far, out[0] = lax.optimization_barrier((prev, far, out[0]))
            blocks[c] = (own, prev, next_, far)
        q, g, ka, va, top = project((own, prev, next_), w_att)
        kb, vb, reach = project_last(far, q, top, w_att)
        out = [
            attention(
                me, bias, w_att_out, reach, q, g, after[c], ka, va, kb, vb, blocks[c], c, out
            )
        ]
    return out[0]


def solution(mesh):
    sizes = (mesh.shape["rows"], mesh.shape["half"])
    in_specs = (P("rows", "half", None), P("rows", "half"), P(), P(), P(), P(), P(), P())
    out_specs = P("rows", "half", None)
    return jax.shard_map(
        functools.partial(shards, sizes),
        mesh=mesh,
        in_specs=in_specs,
        out_specs=out_specs,
        check_vma=False,
    )
```

```python
import functools

import jax
import jax.numpy as jnp
from jax import lax
from jax.experimental import pallas as pl
from jax.experimental.pallas import tpu as pltpu
from jax.sharding import PartitionSpec as P

LOG2E = 1.4426950408889634
NEG = -1e30
SAFE = 100.0
AXES = ("rows", "half")
VMEM = pl.BlockSpec(memory_space=pltpu.VMEM)
SMEM = pl.BlockSpec(memory_space=pltpu.SMEM)
PARAMS = pltpu.CompilerParams(vmem_limit_bytes=62 << 20)
CHUNKS = 2


def dot_nn(a, b):
    return lax.dot_general(a, b, (((1,), (0,)), ((), ())), preferred_element_type=jnp.float32)


def dot_nt(a, b):
    return lax.dot_general(a, b, (((1,), (1,)), ((), ())), preferred_element_type=jnp.float32)


def dot_tn(a, b):
    return lax.dot_general(a, b, (((0,), (0,)), ((), ())), preferred_element_type=jnp.float32)


def sigmoid(x):
    return 0.5 * jnp.tanh(0.5 * x) + 0.5


def norm_lanes(x, gain):
    x = x.astype(jnp.float32)
    center = x - jnp.mean(x, axis=-1, keepdims=True)
    spread = jnp.mean(center * center, axis=-1, keepdims=True)
    return (center * lax.rsqrt(spread + 1e-05) * gain).astype(jnp.bfloat16)


def norm_sublanes(x, gain):
    x = x.astype(jnp.float32)
    center = x - jnp.mean(x, axis=0, keepdims=True)
    spread = jnp.mean(center * center, axis=0, keepdims=True)
    return (center * lax.rsqrt(spread + 1e-05) * gain).astype(jnp.bfloat16)


def edges_kernel(pair_ref, mask_ref, gain_ref, w_ref, out_ref, scr):
    group, cols, width = pair_ref.shape
    gain = gain_ref[0:1, :]
    wt = w_ref[:, : 4 * width].T

    def some(t, carry):
        x = pair_ref[pl.ds(t * EDGE_ROWS, EDGE_ROWS)].reshape(EDGE_ROWS * cols, width)
        mixed = dot_nt(wt, norm_lanes(x, gain))
        m = jnp.concatenate(
            [mask_ref[pl.ds(t * EDGE_ROWS + r, 1), :] for r in range(EDGE_ROWS)], axis=1
        ).astype(jnp.float32)
        left = m * sigmoid(mixed[width : 2 * width]) * mixed[:width]
        right = m * sigmoid(mixed[3 * width :]) * mixed[2 * width : 3 * width]
        for e, edge in enumerate((left, right)):
            for r in range(EDGE_ROWS):
                for s in range(cols // 128):
                    at = r * cols + s * 128
                    scr[e, s, pl.ds(t * EDGE_ROWS + r, width, stride=group), :] = edge[:, at : at + 128]
        return carry

    lax.fori_loop(0, group // EDGE_ROWS, some, 0, unroll=EDGE_UNROLL)
    for e in range(2):
        for s in range(cols // 128):
            out_ref[:, e, :, s * 128 : (s + 1) * 128] = (
                scr[e, s].reshape(width, group, 128).astype(jnp.bfloat16)
            )


EDGE_UNROLL = 1
EDGE_ROWS = 8


def edges(pair, mask, gains, w, group=8):
    rows, cols, width = pair.shape
    return pl.pallas_call(
        edges_kernel,
        grid=(rows // group,),
        out_shape=jax.ShapeDtypeStruct((width, 2, rows, cols), jnp.bfloat16),
        in_specs=[
            pl.BlockSpec((group, cols, width), lambda i: (i, 0, 0)),
            pl.BlockSpec((group, cols), lambda i: (i, 0)),
            VMEM,
            VMEM,
        ],
        out_specs=pl.BlockSpec((width, 2, group, cols), lambda i: (0, 0, i, 0)),
        scratch_shapes=[pltpu.VMEM((2, cols // 128, width * group, 128), jnp.float32)],
        compiler_params=PARAMS,
    )(pair, mask, gains, w)


def gate_kernel(pair_ref, gain_ref, w_ref, out_ref):
    group, cols, width = pair_ref.shape
    normed = norm_lanes(pair_ref[...].reshape(group * cols, width), gain_ref[0:1, :])
    gates = sigmoid(dot_nn(normed, w_ref[:, 4 * width :])).astype(jnp.bfloat16)
    out_ref[...] = gates.reshape(group, cols, width)


def gate(pair, gains, w, group=8):
    rows, cols, width = pair.shape
    block = pl.BlockSpec((group, cols, width), lambda i: (i, 0, 0))
    return pl.pallas_call(
        gate_kernel,
        grid=(rows // group,),
        out_shape=jax.ShapeDtypeStruct(pair.shape, jnp.bfloat16),
        in_specs=[block, VMEM, VMEM],
        out_specs=block,
        compiler_params=PARAMS,
        cost_estimate=pl.CostEstimate(
            flops=6 * rows * cols * width * width,
            bytes_accessed=4 * rows * cols * width,
            transcendentals=rows * cols * width,
        ),
    )(pair, gains, w)


PRODUCT_ROWS = 512


def product_kernel(lr_ref, out_ref):
    blocks, halves, _, rows, cols = lr_ref.shape
    step = PRODUCT_ROWS // rows

    def tile(t, carry):
        acc = None
        for h in range(halves):
            left = lr_ref[pl.ds(t * step, step), h, 0].reshape(step * rows, cols)
            right = lr_ref[:, h, 1].reshape(blocks * rows, cols)
            part = dot_nt(left, right)
            acc = part if acc is None else acc + part
        for h in range(halves):
            out_ref[pl.ds(t * step, step), h] = (
                acc[:, h * cols : (h + 1) * cols].reshape(step, rows, cols).astype(jnp.bfloat16)
            )
        return carry

    lax.fori_loop(0, blocks // step, tile, 0)


def product(lr):
    blocks, halves, _, rows, cols = lr.shape
    return pl.pallas_call(
        product_kernel,
        out_shape=jax.ShapeDtypeStruct((blocks, halves, rows, cols), jnp.bfloat16),
        in_specs=[VMEM],
        out_specs=VMEM,
        compiler_params=PARAMS,
    )(lr)


OUT_ROWS = 8


def output_kernel(prod_ref, pair_ref, gate_ref, mask_ref, gain_ref, gcol_ref, wo_ref, wb_ref, after_ref, norm_ref, bias_ref, scr):
    width, rows, cols = prod_ref.shape
    heads = bias_ref.shape[1]
    for s in range(cols // 128):
        for c in range(0, width, 16):
            part = prod_ref[c : c + 16, :, s * 128 : (s + 1) * 128].astype(jnp.float32)
            scr[s, c * rows : (c + 16) * rows, :] = part.reshape(16 * rows, 128)

    def some(t, carry):
        i = t * OUT_ROWS
        x = jnp.concatenate(
            [
                scr[s, pl.ds(i + r, width, stride=rows), :]
                for r in range(OUT_ROWS)
                for s in range(cols // 128)
            ],
            axis=1,
        )
        normed = norm_sublanes(x.astype(jnp.bfloat16), gcol_ref[...])
        update = dot_tn(normed, wo_ref[...])
        here = pl.ds(i, OUT_ROWS)
        flat = (OUT_ROWS * cols, width)
        p = pair_ref[here].reshape(flat).astype(jnp.float32)
        after = p + gate_ref[here].reshape(flat).astype(jnp.float32) * update
        after = after.astype(jnp.bfloat16)
        after_ref[here] = after.reshape(OUT_ROWS, cols, width)
        a = norm_lanes(after, gain_ref[2:3, :])
        norm_ref[here] = a.reshape(OUT_ROWS, cols, width)
        bias = (dot_nt(wb_ref[...], a) * LOG2E).astype(jnp.bfloat16)
        for r in range(OUT_ROWS):
            bias_ref[i + r] = bias[:heads, r * cols : (r + 1) * cols]
        return carry

    lax.fori_loop(0, rows // OUT_ROWS, some, 0)
    used = rows * cols // width
    norm_ref[rows, :used, :] = mask_ref[...]
    norm_ref[rows, used:, :] = jnp.zeros((cols - used, width), jnp.bfloat16)


def tri_output(prod, pair, gates, mask_flat, gains, gcol, wo, wb, heads, chunk):
    width, rows, cols = prod.shape
    rows //= CHUNKS
    block = pl.BlockSpec((rows, cols, width), lambda i: (chunk, 0, 0))
    return pl.pallas_call(
        output_kernel,
        grid=(1,),
        out_shape=(
            jax.ShapeDtypeStruct((rows, cols, width), jnp.bfloat16),
            jax.ShapeDtypeStruct((rows + 1, cols, width), jnp.bfloat16),
            jax.ShapeDtypeStruct((rows, heads, cols), jnp.bfloat16),
        ),
        in_specs=[
            pl.BlockSpec((width, rows, cols), lambda i: (0, chunk, 0)),
            block,
            block,
            pl.BlockSpec((rows * cols // width, width), lambda i: (chunk, 0)),
        ]
        + [VMEM] * 4,
        out_specs=(VMEM,) * 3,
        scratch_shapes=[pltpu.VMEM((cols // 128, width * rows, 128), jnp.float32)],
        compiler_params=PARAMS,
    )(prod, pair, gates, mask_flat, gains, gcol, wo, wb)


def project_kernel(own, n, n_top, w_ref, *refs):
    refs = list(refs)
    take = lambda k: [refs.pop(0) for _ in range(k)]
    xs, last = take(n), n_top > 0
    (e_ref, q_in) = take(2) if last else (None, None)
    tops_in = take(n_top)
    q_ref, g_ref = take(2) if own else (None, None)
    k_ref, v_ref, m_ref = refs
    width = w_ref.shape[0]
    group, cols, _ = xs[0].shape
    tops = [functools.reduce(jnp.maximum, [t[r, 0:1, :] for t in tops_in]) if last else None for r in range(group)]
    for b, x_ref in enumerate(xs):
        a = x_ref[...].reshape(group * cols, width)
        at = slice(b * cols, (b + 1) * cols)
        if own:
            mixed = dot_nn(a, w_ref[...])
            scale = LOG2E * HEAD_DIM**-0.5
            q_ref[...] = (mixed[:, :width] * scale).astype(jnp.bfloat16).reshape(q_ref.shape)
            g_ref[...] = sigmoid(mixed[:, 3 * width :]).astype(jnp.bfloat16).reshape(g_ref.shape)
            kv = mixed[:, width : 3 * width].astype(jnp.bfloat16)
        else:
            kv = dot_nn(a, w_ref[:, width : 3 * width]).astype(jnp.bfloat16)
        k_ref[:, at, :] = kv[:, :width].reshape(group, cols, width)
        v_ref[:, at, :] = kv[:, width:].reshape(group, cols, width)
        for r in range(group):
            m = jnp.max(jnp.abs(kv[r * cols : (r + 1) * cols, :width]), axis=0, keepdims=True)
            m = m.astype(jnp.float32)
            tops[r] = m if tops[r] is None else jnp.maximum(tops[r], m)
    if last:
        sized = [
            (jnp.abs(q_in[r]).astype(jnp.float32) * tops[r]).astype(jnp.bfloat16)
            for r in range(group)
        ]
        reach = dot_nn(jnp.concatenate(sized, axis=0), e_ref[...])
        tops = [
            jnp.max(reach[r * cols : (r + 1) * cols], axis=0, keepdims=True) for r in range(group)
        ]
    for r in range(group):
        m_ref[r] = jnp.broadcast_to(tops[r], m_ref.shape[1:])


HEAD_DIM = 32
AHEAD = 1


def project(blocks, w, own=False, q=None, tops=(), group=8):
    rows, cols, width = blocks[0].shape
    rows -= 1
    n = len(blocks)
    one = lambda c: pl.BlockSpec((group, c, width), lambda i: (i, 0, 0))
    shape = lambda c: jax.ShapeDtypeStruct((rows, c, width), jnp.bfloat16)
    extra, specs = [], []
    if tops:
        lanes = jnp.arange(width) // HEAD_DIM
        extra = [(lanes[:, None] == lanes[None, :]).astype(jnp.bfloat16), q, *tops]
        specs = [VMEM, one(cols)] + [one(8)] * len(tops)
    return pl.pallas_call(
        functools.partial(project_kernel, own, n, len(tops)),
        grid=(rows // group,),
        out_shape=[shape(cols)] * (2 * own)
        + [shape(n * cols), shape(n * cols), jax.ShapeDtypeStruct((rows, 8, width), jnp.float32)],
        in_specs=[VMEM] + [one(cols)] * n + specs,
        out_specs=[one(cols)] * (2 * own) + [one(n * cols), one(n * cols), one(8)],
        compiler_params=PARAMS,
        cost_estimate=pl.CostEstimate(
            flops=8 * n * rows * cols * width * width,
            bytes_accessed=8 * n * rows * cols * width,
            transcendentals=rows * cols * width,
        ),
    )(w, *blocks, *extra)


def attention_kernel(halves, pieces, me_ref, bias_a_ref, bias_b_ref, wo_ref, reach_ref, *refs):
    q_ref, g_ref, x_ref = refs[:3]
    k_refs, v_refs = refs[3 : 3 + pieces], refs[3 + pieces : 3 + 2 * pieces]
    masks = refs[3 + 2 * pieces : 3 + 2 * pieces + halves]
    out_ref, flags, mrow, vs, b32, gated = refs[-6:]
    i = pl.program_id(0)
    group, cols, width = q_ref.shape
    _, outer, heads, sub, _ = bias_a_ref.shape
    lane = lax.broadcasted_iota(jnp.int32, (1, width), 1)
    me = me_ref[0]
    where = [lax.rem(me + s, halves) for s in (0, halves - 1, 1, 2)]
    step = cols // 128
    count = mrow.shape[1] // step

    @pl.when(i == 0)
    def _():
        top = jnp.zeros((sub, cols), jnp.float32)
        for s, w in enumerate(where):

            def put(t, top, s=s, w=w):
                for p, piece in enumerate((bias_a_ref, bias_b_ref)):
                    core = me_ref[1] if p == 0 else 1 - me_ref[1]
                    j = pl.ds(pl.multiple_of((2 * t + core) * sub, sub), sub)
                    for h in range(heads):
                        b = piece[w, t, h].astype(jnp.float32)
                        b32[h, j, s * cols : (s + 1) * cols] = b
                        top = jnp.maximum(top, jnp.abs(b))
                return top

            top = lax.fori_loop(0, outer, put, top)
        bound = jnp.max(reach_ref[...]) * 1.02 + jnp.max(top)
        flags[0] = (bound < SAFE).astype(jnp.int32)
        for s in range(halves):
            mrow[s] = masks[s][0, : mrow.shape[1], :].astype(jnp.float32)
        least = None
        seen = jnp.max(mrow[...], axis=0)
        for r in range(count):
            u = jnp.max(seen[r * step : (r + 1) * step], keepdims=True)
            least = u if least is None else jnp.minimum(least, u)
        flags[1] = (jnp.max(least) > 0.0).astype(jnp.int32)
        vs[:, :, width:] = jnp.ones((group, vs.shape[1], width), jnp.bfloat16)

    def mask_line(r):
        at = (i * group + r) * step
        return jnp.concatenate(
            [mrow[s, pl.ds(at + t, 1), :] for s in range(halves) for t in range(step)], axis=1
        )

    def finish(r, attended):
        gated[r] = (attended * g_ref[r].astype(jnp.float32)).astype(jnp.bfloat16)

    def attend(shift):
        def score(r, h):
            q = q_ref[r]
            on = jnp.broadcast_to(lane // (width // heads) == h, q.shape)
            qm = jnp.where(on, q, jnp.zeros_like(q))
            scores = jnp.concatenate([dot_nt(qm, k[r]) for k in k_refs], axis=1)
            return scores + b32[h] + jnp.where(mask_line(r) > 0.0, 0.0, NEG)

        order = [(r, h) for r in range(group) for h in range(heads)]
        ahead = [score(*order[t]) for t in range(AHEAD)]
        for t, (r, h) in enumerate(order):
            if t + AHEAD < len(order):
                ahead.append(score(*order[t + AHEAD]))
            scores = ahead.pop(0)
            if h == 0:
                at = 0
                for v in v_refs:
                    vs[r, at : at + v.shape[1], :width] = v[r]
                    at += v.shape[1]
                num = jnp.zeros((cols, width), jnp.float32)
                den = jnp.ones((cols, width), jnp.float32)
            if shift:
                scores = scores - jnp.max(scores, axis=-1, keepdims=True)
            weights = jnp.exp2(scores).astype(jnp.bfloat16)
            both = dot_nn(weights, vs[r])
            on = lane // (width // heads) == h
            num = jnp.where(on, both[:, :width], num)
            den = jnp.where(on, both[:, width:], den)
            if h == heads - 1:
                finish(r, num / den)

    @pl.when(flags[0] > 0)
    def _():
        attend(False)

    @pl.when(flags[0] == 0)
    def _():
        attend(True)

    @pl.when(flags[1] == 0)
    def _():
        for r in range(group):
            used = jnp.max(mask_line(r), keepdims=True) > 0.0
            mean = jnp.mean(vs[r, :, :width].astype(jnp.float32), axis=0, keepdims=True)
            plain = mean * g_ref[r].astype(jnp.float32)
            gated[r] = jnp.where(used, gated[r].astype(jnp.float32), plain).astype(jnp.bfloat16)

    flat = (group * cols, width)
    out = dot_nn(gated[...].reshape(flat), wo_ref[...])
    out = x_ref[...].reshape(flat).astype(jnp.float32) + out
    out_ref[...] = out.astype(jnp.bfloat16).reshape(out_ref.shape)


def attention(me, bias, wo, reach, q, g, x, keys, values, blocks, chunk, filled, group=4):
    halves, _, heads, _, _ = bias[0].shape
    rows, cols, width = q.shape
    one = lambda c: pl.BlockSpec((group, c, width), lambda i: (i, 0, 0))
    last = pl.BlockSpec((1, cols, width), lambda i: (rows, 0, 0))
    pieces = len(keys)
    return pl.pallas_call(
        functools.partial(attention_kernel, halves, pieces),
        grid=(rows // group,),
        out_shape=jax.ShapeDtypeStruct((CHUNKS * rows, cols, width), jnp.bfloat16),
        in_specs=[SMEM, VMEM, VMEM, VMEM, VMEM]
        + [one(cols)] * 3
        + [one(k.shape[1]) for k in keys] * 2
        + [last] * halves
        + [pl.BlockSpec(memory_space=pl.ANY)] * len(filled),
        out_specs=pl.BlockSpec((group, cols, width), lambda i: (chunk * (rows // group) + i, 0, 0)),
        input_output_aliases={8 + 2 * pieces + halves: 0} if filled else {},
        scratch_shapes=[
            pltpu.SMEM((2,), jnp.int32),
            pltpu.VMEM((halves, rows * cols // 128, 128), jnp.float32),
            pltpu.VMEM((group, halves * cols, 2 * width), jnp.bfloat16),
            pltpu.VMEM((heads, cols, halves * cols), jnp.float32),
            pltpu.VMEM((group, cols, width), jnp.bfloat16),
        ],
        compiler_params=PARAMS,
        cost_estimate=pl.CostEstimate(
            flops=8 * rows * 4 * cols * halves * cols * width * 2,
            bytes_accessed=8 * rows * cols * width * halves,
            transcendentals=rows * 4 * cols * cols * halves,
        ),
    )(me, *bias, wo, reach, q, g, x, *keys, *values, *blocks, *filled)


def shards(sizes, pair, pair_mask, gains, w_tri, w_tri_out, w_att, w_bias, w_att_out):
    n_rows, halves = sizes
    rows, cols, width = pair.shape
    heads = w_bias.shape[1]
    lr = edges(pair, pair_mask, gains, w_tri)
    lr = lax.all_to_all(lr, AXES, split_axis=0, concat_axis=0, tiled=True)
    gates = gate(pair, gains, w_tri)
    prod = product(lr.reshape(n_rows, halves, 2, rows, cols))
    back = lax.all_to_all(
        prod.reshape(width, rows, cols), AXES, split_axis=0, concat_axis=0, tiled=True
    )
    wb = jnp.pad(w_bias.T, ((0, 8 - heads), (0, 0)))
    mask_flat = pair_mask.astype(jnp.bfloat16).reshape(rows * cols // width, width)
    up = [(y, (y + 1) % halves) for y in range(halves)]
    down = [(y, (y - 1) % halves) for y in range(halves)]
    after, blocks, bias = [], [], []
    for c in range(CHUNKS):
        x, own, b = tri_output(
            back, pair, gates, mask_flat, gains, gains[1][:, None], w_tri_out, wb, heads, c
        )
        prev = lax.ppermute(own, "half", up)
        next_ = lax.ppermute(own, "half", down)
        far = lax.ppermute(prev, "half", up) if c % 2 == 0 else lax.ppermute(next_, "half", down)
        after.append(x)
        blocks.append((own, prev, next_, far))
        bias.append(b)
    inner = n_rows // halves
    swap = [
        ((z * inner + k) * halves + y, (y * inner + k) * halves + z)
        for z in range(halves)
        for k in range(inner)
        for y in range(halves)
    ]
    bias = jnp.swapaxes(jnp.concatenate(bias, axis=0), 0, 1)
    bias = lax.ppermute(bias, AXES, swap)
    bias, near = lax.optimization_barrier((bias, blocks[0][1:3]))
    blocks[0] = (blocks[0][0], *near, blocks[0][3])
    half_rows = n_rows // 2
    bias = jnp.broadcast_to(bias[None], (half_rows,) + bias.shape)
    cores = [[2 * t + core for t in range(half_rows)] for core in range(2)]
    bias = lax.all_to_all(
        bias, "rows", split_axis=0, concat_axis=0, axis_index_groups=cores, tiled=True
    )
    first = [project((b[0],), w_att, own=True) for b in blocks]
    near = project(blocks[0][1:3], w_att)
    bias, first, near = lax.optimization_barrier((bias, first, near))
    other = lax.ppermute(bias, "rows", [(r, r ^ 1) for r in range(n_rows)])
    bias = [v.reshape(halves, inner // 2, heads, rows, cols) for v in (bias, other)]
    *bias, next_ = lax.optimization_barrier((*bias, blocks[1][2]))
    blocks[1] = (*blocks[1][:2], next_, blocks[1][3])

    me = jnp.stack([lax.axis_index("half"), lax.axis_index("rows") & 1]).astype(jnp.int32)
    q, g, k, v, top = first[0]
    far = project((blocks[0][3],), w_att, q=q, tops=(top, near[2]))
    out = attention(
        me, bias, w_att_out, far[2], q, g, after[0], (k, near[0], far[0]), (v, near[1], far[1]), blocks[0], 0, []
    )
    rest, out = lax.optimization_barrier((blocks[1][1:], out))
    q, g, k, v, top = first[1]
    far = project(rest, w_att, q=q, tops=(top,))
    return attention(
        me, bias, w_att_out, far[2], q, g, after[1], (k, far[0]), (v, far[1]), (blocks[1][0], *rest), 1, [out]
    )


def solution(mesh):
    sizes = (mesh.shape["rows"], mesh.shape["half"])
    in_specs = (P("rows", "half", None), P("rows", "half"), P(), P(), P(), P(), P(), P())
    out_specs = P("rows", "half", None)
    return jax.shard_map(
        functools.partial(shards, sizes),
        mesh=mesh,
        in_specs=in_specs,
        out_specs=out_specs,
        check_vma=False,
    )
```

```python
import functools

import jax
import jax.numpy as jnp
from jax import lax
from jax.experimental import pallas as pl
from jax.experimental.pallas import tpu as pltpu
from jax.sharding import PartitionSpec as P

LOG2E = 1.4426950408889634
NEG = -1e30
SAFE = 100.0
AXES = ("rows", "half")
VMEM = pl.BlockSpec(memory_space=pltpu.VMEM)
SMEM = pl.BlockSpec(memory_space=pltpu.SMEM)
PARAMS = pltpu.CompilerParams(vmem_limit_bytes=62 << 20)
CHUNKS = 2


def dot_nn(a, b):
    return lax.dot_general(a, b, (((1,), (0,)), ((), ())), preferred_element_type=jnp.float32)


def dot_nt(a, b):
    return lax.dot_general(a, b, (((1,), (1,)), ((), ())), preferred_element_type=jnp.float32)


def dot_tn(a, b):
    return lax.dot_general(a, b, (((0,), (0,)), ((), ())), preferred_element_type=jnp.float32)


def sigmoid(x):
    return 0.5 * jnp.tanh(0.5 * x) + 0.5


def norm_lanes(x, gain):
    x = x.astype(jnp.float32)
    center = x - jnp.mean(x, axis=-1, keepdims=True)
    spread = jnp.mean(center * center, axis=-1, keepdims=True)
    return (center * lax.rsqrt(spread + 1e-05) * gain).astype(jnp.bfloat16)


def norm_sublanes(x, gain):
    x = x.astype(jnp.float32)
    center = x - jnp.mean(x, axis=0, keepdims=True)
    spread = jnp.mean(center * center, axis=0, keepdims=True)
    return (center * lax.rsqrt(spread + 1e-05) * gain).astype(jnp.bfloat16)


def edges_kernel(pair_ref, mask_ref, gain_ref, w_ref, out_ref, scr):
    group, cols, width = pair_ref.shape
    gain = gain_ref[0:1, :]
    wt = w_ref[:, : 4 * width].T

    def some(t, carry):
        x = pair_ref[pl.ds(t * EDGE_ROWS, EDGE_ROWS)].reshape(EDGE_ROWS * cols, width)
        mixed = dot_nt(wt, norm_lanes(x, gain))
        m = jnp.concatenate(
            [mask_ref[pl.ds(t * EDGE_ROWS + r, 1), :] for r in range(EDGE_ROWS)], axis=1
        ).astype(jnp.float32)
        left = m * sigmoid(mixed[width : 2 * width]) * mixed[:width]
        right = m * sigmoid(mixed[3 * width :]) * mixed[2 * width : 3 * width]
        for e, edge in enumerate((left, right)):
            for r in range(EDGE_ROWS):
                for s in range(cols // 128):
                    at = r * cols + s * 128
                    scr[e, s, pl.ds(t * EDGE_ROWS + r, width, stride=group), :] = edge[:, at : at + 128]
        return carry

    lax.fori_loop(0, group // EDGE_ROWS, some, 0, unroll=EDGE_UNROLL)
    for e in range(2):
        for s in range(cols // 128):
            out_ref[:, e, :, s * 128 : (s + 1) * 128] = (
                scr[e, s].reshape(width, group, 128).astype(jnp.bfloat16)
            )


EDGE_UNROLL = 1
EDGE_ROWS = 8


def edges(pair, mask, gains, w, group=8):
    rows, cols, width = pair.shape
    return pl.pallas_call(
        edges_kernel,
        grid=(rows // group,),
        out_shape=jax.ShapeDtypeStruct((width, 2, rows, cols), jnp.bfloat16),
        in_specs=[
            pl.BlockSpec((group, cols, width), lambda i: (i, 0, 0)),
            pl.BlockSpec((group, cols), lambda i: (i, 0)),
            VMEM,
            VMEM,
        ],
        out_specs=pl.BlockSpec((width, 2, group, cols), lambda i: (0, 0, i, 0)),
        scratch_shapes=[pltpu.VMEM((2, cols // 128, width * group, 128), jnp.float32)],
        compiler_params=PARAMS,
    )(pair, mask, gains, w)


def gate_kernel(pair_ref, gain_ref, w_ref, out_ref):
    group, cols, width = pair_ref.shape
    normed = norm_lanes(pair_ref[...].reshape(group * cols, width), gain_ref[0:1, :])
    gates = sigmoid(dot_nn(normed, w_ref[:, 4 * width :])).astype(jnp.bfloat16)
    out_ref[...] = gates.reshape(group, cols, width)


def gate(pair, gains, w, group=8):
    rows, cols, width = pair.shape
    block = pl.BlockSpec((group, cols, width), lambda i: (i, 0, 0))
    return pl.pallas_call(
        gate_kernel,
        grid=(rows // group,),
        out_shape=jax.ShapeDtypeStruct(pair.shape, jnp.bfloat16),
        in_specs=[block, VMEM, VMEM],
        out_specs=block,
        compiler_params=PARAMS,
        cost_estimate=pl.CostEstimate(
            flops=6 * rows * cols * width * width,
            bytes_accessed=4 * rows * cols * width,
            transcendentals=rows * cols * width,
        ),
    )(pair, gains, w)


PRODUCT_ROWS = 512


def product_kernel(lr_ref, out_ref):
    blocks, halves, _, rows, cols = lr_ref.shape
    step = PRODUCT_ROWS // rows

    def tile(t, carry):
        acc = None
        for h in range(halves):
            left = lr_ref[pl.ds(t * step, step), h, 0].reshape(step * rows, cols)
            right = lr_ref[:, h, 1].reshape(blocks * rows, cols)
            part = dot_nt(left, right)
            acc = part if acc is None else acc + part
        for h in range(halves):
            out_ref[pl.ds(t * step, step), h] = (
                acc[:, h * cols : (h + 1) * cols].reshape(step, rows, cols).astype(jnp.bfloat16)
            )
        return carry

    lax.fori_loop(0, blocks // step, tile, 0)


def product(lr):
    blocks, halves, _, rows, cols = lr.shape
    return pl.pallas_call(
        product_kernel,
        out_shape=jax.ShapeDtypeStruct((blocks, halves, rows, cols), jnp.bfloat16),
        in_specs=[VMEM],
        out_specs=VMEM,
        compiler_params=PARAMS,
    )(lr)


OUT_ROWS = 8


def output_kernel(prod_ref, pair_ref, gate_ref, mask_ref, gain_ref, gcol_ref, wo_ref, wb_ref, after_ref, norm_ref, bias_ref, scr):
    width, rows, cols = prod_ref.shape
    heads = bias_ref.shape[1]
    for s in range(cols // 128):
        for c in range(0, width, 16):
            part = prod_ref[c : c + 16, :, s * 128 : (s + 1) * 128].astype(jnp.float32)
            scr[s, c * rows : (c + 16) * rows, :] = part.reshape(16 * rows, 128)

    def some(t, carry):
        i = t * OUT_ROWS
        x = jnp.concatenate(
            [
                scr[s, pl.ds(i + r, width, stride=rows), :]
                for r in range(OUT_ROWS)
                for s in range(cols // 128)
            ],
            axis=1,
        )
        normed = norm_sublanes(x.astype(jnp.bfloat16), gcol_ref[...])
        update = dot_tn(normed, wo_ref[...])
        here = pl.ds(i, OUT_ROWS)
        flat = (OUT_ROWS * cols, width)
        p = pair_ref[here].reshape(flat).astype(jnp.float32)
        after = p + gate_ref[here].reshape(flat).astype(jnp.float32) * update
        after = after.astype(jnp.bfloat16)
        after_ref[here] = after.reshape(OUT_ROWS, cols, width)
        a = norm_lanes(after, gain_ref[2:3, :])
        norm_ref[here] = a.reshape(OUT_ROWS, cols, width)
        bias = (dot_nt(wb_ref[...], a) * LOG2E).astype(jnp.bfloat16)
        for r in range(OUT_ROWS):
            bias_ref[i + r] = bias[:heads, r * cols : (r + 1) * cols]
        return carry

    lax.fori_loop(0, rows // OUT_ROWS, some, 0)
    used = rows * cols // width
    norm_ref[rows, :used, :] = mask_ref[...]
    norm_ref[rows, used:, :] = jnp.zeros((cols - used, width), jnp.bfloat16)


def tri_output(prod, pair, gates, mask_flat, gains, gcol, wo, wb, heads, chunk):
    width, rows, cols = prod.shape
    rows //= CHUNKS
    block = pl.BlockSpec((rows, cols, width), lambda i: (chunk, 0, 0))
    return pl.pallas_call(
        output_kernel,
        grid=(1,),
        out_shape=(
            jax.ShapeDtypeStruct((rows, cols, width), jnp.bfloat16),
            jax.ShapeDtypeStruct((rows + 1, cols, width), jnp.bfloat16),
            jax.ShapeDtypeStruct((rows, heads, cols), jnp.bfloat16),
        ),
        in_specs=[
            pl.BlockSpec((width, rows, cols), lambda i: (0, chunk, 0)),
            block,
            block,
            pl.BlockSpec((rows * cols // width, width), lambda i: (chunk, 0)),
        ]
        + [VMEM] * 4,
        out_specs=(VMEM,) * 3,
        scratch_shapes=[pltpu.VMEM((cols // 128, width * rows, 128), jnp.float32)],
        compiler_params=PARAMS,
    )(prod, pair, gates, mask_flat, gains, gcol, wo, wb)


def project_kernel(own, n, n_top, w_ref, *refs):
    refs = list(refs)
    take = lambda k: [refs.pop(0) for _ in range(k)]
    xs, last = take(n), n_top > 0
    (e_ref, q_in) = take(2) if last else (None, None)
    tops_in = take(n_top)
    q_ref, g_ref = take(2) if own else (None, None)
    k_ref, v_ref, m_ref = refs
    width = w_ref.shape[0]
    group, cols, _ = xs[0].shape
    tops = [functools.reduce(jnp.maximum, [t[r, 0:1, :] for t in tops_in]) if last else None for r in range(group)]
    for b, x_ref in enumerate(xs):
        a = x_ref[...].reshape(group * cols, width)
        at = slice(b * cols, (b + 1) * cols)
        if own:
            mixed = dot_nn(a, w_ref[...])
            scale = LOG2E * HEAD_DIM**-0.5
            q_ref[...] = (mixed[:, :width] * scale).astype(jnp.bfloat16).reshape(q_ref.shape)
            g_ref[...] = sigmoid(mixed[:, 3 * width :]).astype(jnp.bfloat16).reshape(g_ref.shape)
            kv = mixed[:, width : 3 * width].astype(jnp.bfloat16)
        else:
            kv = dot_nn(a, w_ref[:, width : 3 * width]).astype(jnp.bfloat16)
        k_ref[:, at, :] = kv[:, :width].reshape(group, cols, width)
        v_ref[:, at, :] = kv[:, width:].reshape(group, cols, width)
        for r in range(group):
            m = jnp.max(jnp.abs(kv[r * cols : (r + 1) * cols, :width]), axis=0, keepdims=True)
            m = m.astype(jnp.float32)
            tops[r] = m if tops[r] is None else jnp.maximum(tops[r], m)
    if last:
        sized = [
            (jnp.abs(q_in[r]).astype(jnp.float32) * tops[r]).astype(jnp.bfloat16)
            for r in range(group)
        ]
        reach = dot_nn(jnp.concatenate(sized, axis=0), e_ref[...])
        tops = [
            jnp.max(reach[r * cols : (r + 1) * cols], axis=0, keepdims=True) for r in range(group)
        ]
    for r in range(group):
        m_ref[r] = jnp.broadcast_to(tops[r], m_ref.shape[1:])


HEAD_DIM = 32
AHEAD = 1


def project(blocks, w, own=False, q=None, tops=(), group=8):
    rows, cols, width = blocks[0].shape
    rows -= 1
    n = len(blocks)
    one = lambda c: pl.BlockSpec((group, c, width), lambda i: (i, 0, 0))
    shape = lambda c: jax.ShapeDtypeStruct((rows, c, width), jnp.bfloat16)
    extra, specs = [], []
    if tops:
        lanes = jnp.arange(width) // HEAD_DIM
        extra = [(lanes[:, None] == lanes[None, :]).astype(jnp.bfloat16), q, *tops]
        specs = [VMEM, one(cols)] + [one(8)] * len(tops)
    return pl.pallas_call(
        functools.partial(project_kernel, own, n, len(tops)),
        grid=(rows // group,),
        out_shape=[shape(cols)] * (2 * own)
        + [shape(n * cols), shape(n * cols), jax.ShapeDtypeStruct((rows, 8, width), jnp.float32)],
        in_specs=[VMEM] + [one(cols)] * n + specs,
        out_specs=[one(cols)] * (2 * own) + [one(n * cols), one(n * cols), one(8)],
        compiler_params=PARAMS,
        cost_estimate=pl.CostEstimate(
            flops=8 * n * rows * cols * width * width,
            bytes_accessed=8 * n * rows * cols * width,
            transcendentals=rows * cols * width,
        ),
    )(w, *blocks, *extra)


def attention_kernel(halves, pieces, me_ref, bias_a_ref, bias_b_ref, wo_ref, reach_ref, *refs):
    q_ref, g_ref, x_ref = refs[:3]
    k_refs, v_refs = refs[3 : 3 + pieces], refs[3 + pieces : 3 + 2 * pieces]
    masks = refs[3 + 2 * pieces : 3 + 2 * pieces + halves]
    out_ref, flags, mrow, vs, b32, gated = refs[-6:]
    i = pl.program_id(0)
    group, cols, width = q_ref.shape
    _, outer, heads, sub, _ = bias_a_ref.shape
    lane = lax.broadcasted_iota(jnp.int32, (1, width), 1)
    me = me_ref[0]
    where = [lax.rem(me + s, halves) for s in (0, halves - 1, 1, 2)]
    step = cols // 128
    count = mrow.shape[1] // step

    @pl.when(i == 0)
    def _():
        top = jnp.zeros((sub, cols), jnp.float32)
        for s, w in enumerate(where):

            def put(t, top, s=s, w=w):
                for p, piece in enumerate((bias_a_ref, bias_b_ref)):
                    core = me_ref[1] if p == 0 else 1 - me_ref[1]
                    j = pl.ds(pl.multiple_of((2 * t + core) * sub, sub), sub)
                    for h in range(heads):
                        b = piece[w, t, h].astype(jnp.float32)
                        b32[h, j, s * cols : (s + 1) * cols] = b
                        top = jnp.maximum(top, jnp.abs(b))
                return top

            top = lax.fori_loop(0, outer, put, top)
        bound = jnp.max(reach_ref[...]) * 1.02 + jnp.max(top)
        flags[0] = (bound < SAFE).astype(jnp.int32)
        for s in range(halves):
            mrow[s] = masks[s][0, : mrow.shape[1], :].astype(jnp.float32)
        least = None
        seen = jnp.max(mrow[...], axis=0)
        for r in range(count):
            u = jnp.max(seen[r * step : (r + 1) * step], keepdims=True)
            least = u if least is None else jnp.minimum(least, u)
        flags[1] = (jnp.max(least) > 0.0).astype(jnp.int32)
        vs[:, :, width:] = jnp.ones((group, vs.shape[1], width), jnp.bfloat16)

    def mask_line(r):
        at = (i * group + r) * step
        return jnp.concatenate(
            [mrow[s, pl.ds(at + t, 1), :] for s in range(halves) for t in range(step)], axis=1
        )

    def finish(r, attended):
        gated[r] = (attended * g_ref[r].astype(jnp.float32)).astype(jnp.bfloat16)

    def attend(shift):
        def score(r, h):
            q = q_ref[r]
            on = jnp.broadcast_to(lane // (width // heads) == h, q.shape)
            qm = jnp.where(on, q, jnp.zeros_like(q))
            scores = jnp.concatenate([dot_nt(qm, k[r]) for k in k_refs], axis=1)
            return scores + b32[h] + jnp.where(mask_line(r) > 0.0, 0.0, NEG)

        order = [(r, h) for r in range(group) for h in range(heads)]
        ahead = [score(*order[t]) for t in range(AHEAD)]
        for t, (r, h) in enumerate(order):
            if t + AHEAD < len(order):
                ahead.append(score(*order[t + AHEAD]))
            scores = ahead.pop(0)
            if h == 0:
                at = 0
                for v in v_refs:
                    vs[r, at : at + v.shape[1], :width] = v[r]
                    at += v.shape[1]
                num = jnp.zeros((cols, width), jnp.float32)
                den = jnp.ones((cols, width), jnp.float32)
            if shift:
                scores = scores - jnp.max(scores, axis=-1, keepdims=True)
            weights = jnp.exp2(scores).astype(jnp.bfloat16)
            both = dot_nn(weights, vs[r])
            on = lane // (width // heads) == h
            num = jnp.where(on, both[:, :width], num)
            den = jnp.where(on, both[:, width:], den)
            if h == heads - 1:
                finish(r, num / den)

    @pl.when(flags[0] > 0)
    def _():
        attend(False)

    @pl.when(flags[0] == 0)
    def _():
        attend(True)

    @pl.when(flags[1] == 0)
    def _():
        for r in range(group):
            used = jnp.max(mask_line(r), keepdims=True) > 0.0
            mean = jnp.mean(vs[r, :, :width].astype(jnp.float32), axis=0, keepdims=True)
            plain = mean * g_ref[r].astype(jnp.float32)
            gated[r] = jnp.where(used, gated[r].astype(jnp.float32), plain).astype(jnp.bfloat16)

    flat = (group * cols, width)
    out = dot_nn(gated[...].reshape(flat), wo_ref[...])
    out = x_ref[...].reshape(flat).astype(jnp.float32) + out
    out_ref[...] = out.astype(jnp.bfloat16).reshape(out_ref.shape)


def attention(me, bias, wo, reach, q, g, x, keys, values, blocks, chunk, filled, group=4):
    halves, _, heads, _, _ = bias[0].shape
    rows, cols, width = q.shape
    one = lambda c: pl.BlockSpec((group, c, width), lambda i: (i, 0, 0))
    last = pl.BlockSpec((1, cols, width), lambda i: (rows, 0, 0))
    pieces = len(keys)
    return pl.pallas_call(
        functools.partial(attention_kernel, halves, pieces),
        grid=(rows // group,),
        out_shape=jax.ShapeDtypeStruct((CHUNKS * rows, cols, width), jnp.bfloat16),
        in_specs=[SMEM, VMEM, VMEM, VMEM, VMEM]
        + [one(cols)] * 3
        + [one(k.shape[1]) for k in keys] * 2
        + [last] * halves
        + [pl.BlockSpec(memory_space=pl.ANY)] * len(filled),
        out_specs=pl.BlockSpec((group, cols, width), lambda i: (chunk * (rows // group) + i, 0, 0)),
        input_output_aliases={8 + 2 * pieces + halves: 0} if filled else {},
        scratch_shapes=[
            pltpu.SMEM((2,), jnp.int32),
            pltpu.VMEM((halves, rows * cols // 128, 128), jnp.float32),
            pltpu.VMEM((group, halves * cols, 2 * width), jnp.bfloat16),
            pltpu.VMEM((heads, cols, halves * cols), jnp.float32),
            pltpu.VMEM((group, cols, width), jnp.bfloat16),
        ],
        compiler_params=PARAMS,
        cost_estimate=pl.CostEstimate(
            flops=8 * rows * 4 * cols * halves * cols * width * 2,
            bytes_accessed=8 * rows * cols * width * halves,
            transcendentals=rows * 4 * cols * cols * halves,
        ),
    )(me, *bias, wo, reach, q, g, x, *keys, *values, *blocks, *filled)


def shards(sizes, pair, pair_mask, gains, w_tri, w_tri_out, w_att, w_bias, w_att_out):
    n_rows, halves = sizes
    rows, cols, width = pair.shape
    heads = w_bias.shape[1]
    lr = edges(pair, pair_mask, gains, w_tri)
    lr = lax.all_to_all(lr, AXES, split_axis=0, concat_axis=0, tiled=True)
    gates = gate(pair, gains, w_tri)
    prod = product(lr.reshape(n_rows, halves, 2, rows, cols))
    back = lax.all_to_all(
        prod.reshape(width, rows, cols), AXES, split_axis=0, concat_axis=0, tiled=True
    )
    wb = jnp.pad(w_bias.T, ((0, 8 - heads), (0, 0)))
    mask_flat = pair_mask.astype(jnp.bfloat16).reshape(rows * cols // width, width)
    up = [(y, (y + 1) % halves) for y in range(halves)]
    down = [(y, (y - 1) % halves) for y in range(halves)]
    after, blocks, bias = [], [], []
    for c in range(CHUNKS):
        x, own, b = tri_output(
            back, pair, gates, mask_flat, gains, gains[1][:, None], w_tri_out, wb, heads, c
        )
        prev = lax.ppermute(own, "half", up)
        next_ = lax.ppermute(own, "half", down)
        far = lax.ppermute(prev, "half", up) if c % 2 == 0 else lax.ppermute(next_, "half", down)
        after.append(x)
        blocks.append((own, prev, next_, far))
        bias.append(b)
    inner = n_rows // halves
    swap = [
        ((z * inner + k) * halves + y, (y * inner + k) * halves + z)
        for z in range(halves)
        for k in range(inner)
        for y in range(halves)
    ]
    bias = jnp.swapaxes(jnp.concatenate(bias, axis=0), 0, 1)
    bias = lax.ppermute(bias, AXES, swap)
    first = [project((b[0],), w_att, own=True) for b in blocks]
    bias, first, near = lax.optimization_barrier((bias, first, blocks[0][1:3]))
    blocks[0] = (blocks[0][0], *near, blocks[0][3])
    half_rows = n_rows // 2
    bias = jnp.broadcast_to(bias[None], (half_rows,) + bias.shape)
    cores = [[2 * t + core for t in range(half_rows)] for core in range(2)]
    bias = lax.all_to_all(
        bias, "rows", split_axis=0, concat_axis=0, axis_index_groups=cores, tiled=True
    )
    near = project(blocks[0][1:3], w_att)
    bias, near = lax.optimization_barrier((bias, near))
    other = lax.ppermute(bias, "rows", [(r, r ^ 1) for r in range(n_rows)])
    bias = [v.reshape(halves, inner // 2, heads, rows, cols) for v in (bias, other)]
    *bias, next_ = lax.optimization_barrier((*bias, blocks[1][2]))
    blocks[1] = (*blocks[1][:2], next_, blocks[1][3])

    me = jnp.stack([lax.axis_index("half"), lax.axis_index("rows") & 1]).astype(jnp.int32)
    q, g, k, v, top = first[0]
    far = project((blocks[0][3],), w_att, q=q, tops=(top, near[2]))
    out = attention(
        me, bias, w_att_out, far[2], q, g, after[0], (k, near[0], far[0]), (v, near[1], far[1]), blocks[0], 0, []
    )
    rest, out = lax.optimization_barrier((blocks[1][1:], out))
    q, g, k, v, top = first[1]
    far = project(rest, w_att, q=q, tops=(top,))
    return attention(
        me, bias, w_att_out, far[2], q, g, after[1], (k, far[0]), (v, far[1]), (blocks[1][0], *rest), 1, [out]
    )


def solution(mesh):
    sizes = (mesh.shape["rows"], mesh.shape["half"])
    in_specs = (P("rows", "half", None), P("rows", "half"), P(), P(), P(), P(), P(), P())
    out_specs = P("rows", "half", None)
    return jax.shard_map(
        functools.partial(shards, sizes),
        mesh=mesh,
        in_specs=in_specs,
        out_specs=out_specs,
        check_vma=False,
    )
```

```python
import functools

import jax
import jax.numpy as jnp
from jax import lax
from jax.experimental import pallas as pl
from jax.experimental.pallas import tpu as pltpu
from jax.sharding import PartitionSpec as P

LOG2E = 1.4426950408889634
NEG = -1e30
SAFE = 100.0
AXES = ("rows", "half")
VMEM = pl.BlockSpec(memory_space=pltpu.VMEM)
SMEM = pl.BlockSpec(memory_space=pltpu.SMEM)
PARAMS = pltpu.CompilerParams(vmem_limit_bytes=62 << 20)
CHUNKS = 2


def dot_nn(a, b):
    return lax.dot_general(a, b, (((1,), (0,)), ((), ())), preferred_element_type=jnp.float32)


def dot_nt(a, b):
    return lax.dot_general(a, b, (((1,), (1,)), ((), ())), preferred_element_type=jnp.float32)


def dot_tn(a, b):
    return lax.dot_general(a, b, (((0,), (0,)), ((), ())), preferred_element_type=jnp.float32)


def sigmoid(x):
    return 0.5 * jnp.tanh(0.5 * x) + 0.5


def norm_lanes(x, gain):
    x = x.astype(jnp.float32)
    center = x - jnp.mean(x, axis=-1, keepdims=True)
    spread = jnp.mean(center * center, axis=-1, keepdims=True)
    return (center * lax.rsqrt(spread + 1e-05) * gain).astype(jnp.bfloat16)


def norm_sublanes(x, gain):
    x = x.astype(jnp.float32)
    center = x - jnp.mean(x, axis=0, keepdims=True)
    spread = jnp.mean(center * center, axis=0, keepdims=True)
    return (center * lax.rsqrt(spread + 1e-05) * gain).astype(jnp.bfloat16)


def edges_kernel(pair_ref, mask_ref, gain_ref, w_ref, out_ref, scr, wt_ref):
    group, cols, width = pair_ref.shape
    gain = gain_ref[0:1, :]
    @pl.when(pl.program_id(0) == 0)
    def _():
        wt_ref[...] = w_ref[:, : 4 * width].T

    wt = wt_ref[...]

    def some(t, carry):
        x = pair_ref[pl.ds(t * EDGE_ROWS, EDGE_ROWS)].reshape(EDGE_ROWS * cols, width)
        mixed = dot_nt(wt, norm_lanes(x, gain))
        m = jnp.concatenate(
            [mask_ref[pl.ds(t * EDGE_ROWS + r, 1), :] for r in range(EDGE_ROWS)], axis=1
        ).astype(jnp.float32)
        left = m * sigmoid(mixed[width : 2 * width]) * mixed[:width]
        right = m * sigmoid(mixed[3 * width :]) * mixed[2 * width : 3 * width]
        for e, edge in enumerate((left, right)):
            for r in range(EDGE_ROWS):
                for s in range(cols // 128):
                    at = r * cols + s * 128
                    scr[e, s, pl.ds(t * EDGE_ROWS + r, width, stride=group), :] = edge[:, at : at + 128]
        return carry

    lax.fori_loop(0, group // EDGE_ROWS, some, 0, unroll=EDGE_UNROLL)
    for e in range(2):
        for s in range(cols // 128):
            out_ref[:, e, :, s * 128 : (s + 1) * 128] = (
                scr[e, s].reshape(width, group, 128).astype(jnp.bfloat16)
            )


EDGE_UNROLL = 1
EDGE_ROWS = 8


def edges(pair, mask, gains, w, group=8):
    rows, cols, width = pair.shape
    return pl.pallas_call(
        edges_kernel,
        grid=(rows // group,),
        out_shape=jax.ShapeDtypeStruct((width, 2, rows, cols), jnp.bfloat16),
        in_specs=[
            pl.BlockSpec((group, cols, width), lambda i: (i, 0, 0)),
            pl.BlockSpec((group, cols), lambda i: (i, 0)),
            VMEM,
            VMEM,
        ],
        out_specs=pl.BlockSpec((width, 2, group, cols), lambda i: (0, 0, i, 0)),
        scratch_shapes=[
            pltpu.VMEM((2, cols // 128, width * group, 128), jnp.float32),
            pltpu.VMEM((4 * width, width), jnp.bfloat16),
        ],
        compiler_params=PARAMS,
    )(pair, mask, gains, w)


def gate_kernel(pair_ref, gain_ref, w_ref, out_ref):
    group, cols, width = pair_ref.shape
    normed = norm_lanes(pair_ref[...].reshape(group * cols, width), gain_ref[0:1, :])
    gates = sigmoid(dot_nn(normed, w_ref[:, 4 * width :])).astype(jnp.bfloat16)
    out_ref[...] = gates.reshape(group, cols, width)


def gate(pair, gains, w, group=8):
    rows, cols, width = pair.shape
    block = pl.BlockSpec((group, cols, width), lambda i: (i, 0, 0))
    return pl.pallas_call(
        gate_kernel,
        grid=(rows // group,),
        out_shape=jax.ShapeDtypeStruct(pair.shape, jnp.bfloat16),
        in_specs=[block, VMEM, VMEM],
        out_specs=block,
        compiler_params=PARAMS,
        cost_estimate=pl.CostEstimate(
            flops=6 * rows * cols * width * width,
            bytes_accessed=4 * rows * cols * width,
            transcendentals=rows * cols * width,
        ),
    )(pair, gains, w)


def product_kernel(left_ref, right_ref, out_ref):
    step, halves, _, rows, cols = left_ref.shape
    acc = None
    for h in range(halves):
        left = left_ref[:, h, 0].reshape(step * rows, cols)
        right = right_ref[:, h, 0].reshape(-1, cols)
        part = dot_nt(left, right)
        acc = part if acc is None else acc + part
    for h in range(halves):
        out_ref[:, h] = (
            acc[:, h * cols : (h + 1) * cols].reshape(step, rows, cols).astype(jnp.bfloat16)
        )


def product(lr, tiles=2):
    blocks, halves, _, rows, cols = lr.shape
    step = blocks // tiles
    return pl.pallas_call(
        product_kernel,
        grid=(tiles,),
        out_shape=jax.ShapeDtypeStruct((blocks, halves, rows, cols), jnp.bfloat16),
        in_specs=[
            pl.BlockSpec((step, halves, 1, rows, cols), lambda i: (i, 0, 0, 0, 0)),
            pl.BlockSpec((blocks, halves, 1, rows, cols), lambda i: (0, 0, 1, 0, 0)),
        ],
        out_specs=pl.BlockSpec((step, halves, rows, cols), lambda i: (i, 0, 0, 0)),
        compiler_params=PARAMS,
    )(lr, lr)


OUT_ROWS = 8


def output_kernel(prod_ref, pair_ref, gate_ref, mask_ref, gain_ref, gcol_ref, wo_ref, wb_ref, after_ref, norm_ref, bias_ref, scr):
    width, rows, cols = prod_ref.shape
    heads = bias_ref.shape[1]
    for s in range(cols // 128):
        for c in range(0, width, 16):
            part = prod_ref[c : c + 16, :, s * 128 : (s + 1) * 128].astype(jnp.float32)
            scr[s, c * rows : (c + 16) * rows, :] = part.reshape(16 * rows, 128)

    def some(t, carry):
        i = t * OUT_ROWS
        x = jnp.concatenate(
            [
                scr[s, pl.ds(i + r, width, stride=rows), :]
                for r in range(OUT_ROWS)
                for s in range(cols // 128)
            ],
            axis=1,
        )
        normed = norm_sublanes(x.astype(jnp.bfloat16), gcol_ref[...])
        update = dot_tn(normed, wo_ref[...])
        here = pl.ds(i, OUT_ROWS)
        flat = (OUT_ROWS * cols, width)
        p = pair_ref[here].reshape(flat).astype(jnp.float32)
        after = p + gate_ref[here].reshape(flat).astype(jnp.float32) * update
        after = after.astype(jnp.bfloat16)
        after_ref[here] = after.reshape(OUT_ROWS, cols, width)
        a = norm_lanes(after, gain_ref[2:3, :])
        norm_ref[here] = a.reshape(OUT_ROWS, cols, width)
        bias = (dot_nt(wb_ref[...], a) * LOG2E).astype(jnp.bfloat16)
        for r in range(OUT_ROWS):
            bias_ref[i + r] = bias[:heads, r * cols : (r + 1) * cols]
        return carry

    lax.fori_loop(0, rows // OUT_ROWS, some, 0)
    used = rows * cols // width
    norm_ref[rows, :used, :] = mask_ref[...]
    norm_ref[rows, used:, :] = jnp.zeros((cols - used, width), jnp.bfloat16)


def tri_output(prod, pair, gates, mask_flat, gains, gcol, wo, wb, heads, chunk):
    width, rows, cols = prod.shape
    rows //= CHUNKS
    block = pl.BlockSpec((rows, cols, width), lambda i: (chunk, 0, 0))
    return pl.pallas_call(
        output_kernel,
        grid=(1,),
        out_shape=(
            jax.ShapeDtypeStruct((rows, cols, width), jnp.bfloat16),
            jax.ShapeDtypeStruct((rows + 1, cols, width), jnp.bfloat16),
            jax.ShapeDtypeStruct((rows, heads, cols), jnp.bfloat16),
        ),
        in_specs=[
            pl.BlockSpec((width, rows, cols), lambda i: (0, chunk, 0)),
            block,
            block,
            pl.BlockSpec((rows * cols // width, width), lambda i: (chunk, 0)),
        ]
        + [VMEM] * 4,
        out_specs=(VMEM,) * 3,
        scratch_shapes=[pltpu.VMEM((cols // 128, width * rows, 128), jnp.float32)],
        compiler_params=PARAMS,
    )(prod, pair, gates, mask_flat, gains, gcol, wo, wb)


def project_kernel(own, n, w_ref, *refs):
    xs, refs = refs[:n], refs[n:]
    if own:
        e_ref, q_ref, g_ref, m_ref, *refs = refs
    k_ref, v_ref = refs
    width = w_ref.shape[0]
    group, cols, _ = xs[0].shape
    for b, x_ref in enumerate(xs):
        a = x_ref[...].reshape(group * cols, width)
        at = slice(b * cols, (b + 1) * cols)
        if own:
            mixed = dot_nn(a, w_ref[...])
            scale = LOG2E * HEAD_DIM**-0.5
            q = (mixed[:, :width] * scale).astype(jnp.bfloat16)
            q_ref[...] = q.reshape(q_ref.shape)
            g_ref[...] = sigmoid(mixed[:, 3 * width :]).astype(jnp.bfloat16).reshape(g_ref.shape)
            kv = mixed[:, width : 3 * width].astype(jnp.bfloat16)
            norms = dot_nn(q * q, e_ref[...])
            for r in range(group):
                m = jnp.max(norms[r * cols : (r + 1) * cols], axis=0, keepdims=True)
                m_ref[r] = jnp.broadcast_to(m, m_ref.shape[1:])
        else:
            kv = dot_nn(a, w_ref[:, width : 3 * width]).astype(jnp.bfloat16)
        k_ref[:, at, :] = kv[:, :width].reshape(group, cols, width)
        v_ref[:, at, :] = kv[:, width:].reshape(group, cols, width)


HEAD_DIM = 32
AHEAD = 1


def project(blocks, w, own=False, group=8):
    rows, cols, width = blocks[0].shape
    rows -= 1
    n = len(blocks)
    one = lambda c: pl.BlockSpec((group, c, width), lambda i: (i, 0, 0))
    shape = lambda c: jax.ShapeDtypeStruct((rows, c, width), jnp.bfloat16)
    extra, shapes, specs = [], [], []
    if own:
        lanes = jnp.arange(width) // HEAD_DIM
        extra = [(lanes[:, None] == lanes[None, :]).astype(jnp.bfloat16)]
        shapes = [shape(cols), shape(cols), jax.ShapeDtypeStruct((rows, 8, width), jnp.float32)]
        specs = [one(cols), one(cols), one(8)]
    return pl.pallas_call(
        functools.partial(project_kernel, own, n),
        grid=(rows // group,),
        out_shape=shapes + [shape(n * cols), shape(n * cols)],
        in_specs=[VMEM] + [one(cols)] * n + [VMEM] * len(extra),
        out_specs=specs + [one(n * cols), one(n * cols)],
        compiler_params=PARAMS,
        cost_estimate=pl.CostEstimate(
            flops=8 * n * rows * cols * width * width,
            bytes_accessed=8 * n * rows * cols * width,
            transcendentals=rows * cols * width,
        ),
    )(w, *blocks, *extra)


def key_norms(gain, w_keys):
    width = w_keys.shape[0]
    parts = (gain[:, None] * w_keys.astype(jnp.float32)).reshape(width, -1, HEAD_DIM)
    gram = jnp.einsum("chd,che->hde", parts, parts, precision=lax.Precision.HIGHEST)
    top = jnp.max(jnp.sum(jnp.abs(gram), axis=2), axis=1)
    return jnp.repeat(1.05 * jnp.sqrt(width * top), HEAD_DIM)[None, :]


def attention_kernel(halves, pieces, raw, me_ref, bias_a_ref, bias_b_ref, wo_ref, reach_ref, cap_ref, wa_ref, *refs):
    q_ref, g_ref, x_ref = refs[:3]
    k_refs, v_refs = refs[3 : 3 + pieces], refs[3 + pieces : 3 + 2 * pieces]
    refs = refs[3 + 2 * pieces :]
    raws, masks = refs[:raw], refs[raw : raw + halves]
    out_ref, flags, mrow, ks, vs, b32, gated = refs[-7:]
    i = pl.program_id(0)
    group, cols, width = q_ref.shape
    _, outer, heads, sub, _ = bias_a_ref.shape
    lane = lax.broadcasted_iota(jnp.int32, (1, width), 1)
    me = me_ref[0]
    where = [lax.rem(me + s, halves) for s in (0, halves - 1, 1, 2)]
    step = cols // 128
    count = mrow.shape[1] // step

    @pl.when(i == 0)
    def _():
        top = jnp.zeros((sub, cols), jnp.float32)
        for s, w in enumerate(where):

            def put(t, top, s=s, w=w):
                for p, piece in enumerate((bias_a_ref, bias_b_ref)):
                    core = me_ref[1] if p == 0 else 1 - me_ref[1]
                    j = pl.ds(pl.multiple_of((2 * t + core) * sub, sub), sub)
                    for h in range(heads):
                        b = piece[w, t, h].astype(jnp.float32)
                        b32[h, j, s * cols : (s + 1) * cols] = b
                        top = jnp.maximum(top, jnp.abs(b))
                return top

            top = lax.fori_loop(0, outer, put, top)
        norms = jnp.max(reach_ref[...], axis=0)
        bound = jnp.max(jnp.sqrt(norms) * cap_ref[...]) * 1.02 + jnp.max(top)
        flags[0] = (bound < SAFE).astype(jnp.int32)
        for s in range(halves):
            mrow[s] = masks[s][0, : mrow.shape[1], :].astype(jnp.float32)
        least = None
        seen = jnp.max(mrow[...], axis=0)
        for r in range(count):
            u = jnp.max(seen[r * step : (r + 1) * step], keepdims=True)
            least = u if least is None else jnp.minimum(least, u)
        flags[1] = (jnp.max(least) > 0.0).astype(jnp.int32)
        vs[:, :, width:] = jnp.ones((group, vs.shape[1], width), jnp.bfloat16)

    def mask_line(r):
        at = (i * group + r) * step
        return jnp.concatenate(
            [mrow[s, pl.ds(at + t, 1), :] for s in range(halves) for t in range(step)], axis=1
        )

    def finish(r, attended):
        gated[r] = (attended * g_ref[r].astype(jnp.float32)).astype(jnp.bfloat16)

    def attend(shift):
        def score(r, h):
            q = q_ref[r]
            on = jnp.broadcast_to(lane // (width // heads) == h, q.shape)
            qm = jnp.where(on, q, jnp.zeros_like(q))
            keys = [k[r] for k in k_refs] + [ks[r]]
            scores = jnp.concatenate([dot_nt(qm, k) for k in keys], axis=1)
            return scores + b32[h] + jnp.where(mask_line(r) > 0.0, 0.0, NEG)

        done = sum(v.shape[1] for v in v_refs)
        for n, x in enumerate(raws):
            kv = dot_nn(x[...].reshape(group * cols, width), wa_ref[:, width : 3 * width])
            kv = kv.astype(jnp.bfloat16)
            ks[:, n * cols : (n + 1) * cols, :] = kv[:, :width].reshape(group, cols, width)
            at = done + n * cols
            vs[:, at : at + cols, :width] = kv[:, width:].reshape(group, cols, width)
        order = [(r, h) for r in range(group) for h in range(heads)]
        ahead = [score(*order[t]) for t in range(AHEAD)]
        for t, (r, h) in enumerate(order):
            if t + AHEAD < len(order):
                ahead.append(score(*order[t + AHEAD]))
            scores = ahead.pop(0)
            if h == 0:
                at = 0
                for v in v_refs:
                    vs[r, at : at + v.shape[1], :width] = v[r]
                    at += v.shape[1]
                num = jnp.zeros((cols, width), jnp.float32)
                den = jnp.ones((cols, width), jnp.float32)
            if shift:
                scores = scores - jnp.max(scores, axis=-1, keepdims=True)
            weights = jnp.exp2(scores).astype(jnp.bfloat16)
            both = dot_nn(weights, vs[r])
            on = lane // (width // heads) == h
            num = jnp.where(on, both[:, :width], num)
            den = jnp.where(on, both[:, width:], den)
            if h == heads - 1:
                finish(r, num / den)

    @pl.when(flags[0] > 0)
    def _():
        attend(False)

    @pl.when(flags[0] == 0)
    def _():
        attend(True)

    @pl.when(flags[1] == 0)
    def _():
        for r in range(group):
            used = jnp.max(mask_line(r), keepdims=True) > 0.0
            mean = jnp.mean(vs[r, :, :width].astype(jnp.float32), axis=0, keepdims=True)
            plain = mean * g_ref[r].astype(jnp.float32)
            gated[r] = jnp.where(used, gated[r].astype(jnp.float32), plain).astype(jnp.bfloat16)

    flat = (group * cols, width)
    out = dot_nn(gated[...].reshape(flat), wo_ref[...])
    out = x_ref[...].reshape(flat).astype(jnp.float32) + out
    out_ref[...] = out.astype(jnp.bfloat16).reshape(out_ref.shape)


def attention(me, bias, wo, reach, cap, w, q, g, x, keys, values, raws, blocks, chunk, filled, group=4):
    halves, _, heads, _, _ = bias[0].shape
    rows, cols, width = q.shape
    one = lambda c: pl.BlockSpec((group, c, width), lambda i: (i, 0, 0))
    last = pl.BlockSpec((1, cols, width), lambda i: (rows, 0, 0))
    pieces = len(keys)
    return pl.pallas_call(
        functools.partial(attention_kernel, halves, pieces, len(raws)),
        grid=(rows // group,),
        out_shape=jax.ShapeDtypeStruct((CHUNKS * rows, cols, width), jnp.bfloat16),
        in_specs=[SMEM] + [VMEM] * 6
        + [one(cols)] * 3
        + [one(k.shape[1]) for k in keys] * 2
        + [one(cols)] * len(raws)
        + [last] * halves
        + [pl.BlockSpec(memory_space=pl.ANY)] * len(filled),
        out_specs=pl.BlockSpec((group, cols, width), lambda i: (chunk * (rows // group) + i, 0, 0)),
        input_output_aliases={10 + 2 * pieces + len(raws) + halves: 0} if filled else {},
        scratch_shapes=[
            pltpu.SMEM((2,), jnp.int32),
            pltpu.VMEM((halves, rows * cols // 128, 128), jnp.float32),
            pltpu.VMEM((group, len(raws) * cols, width), jnp.bfloat16),
            pltpu.VMEM((group, halves * cols, 2 * width), jnp.bfloat16),
            pltpu.VMEM((heads, cols, halves * cols), jnp.float32),
            pltpu.VMEM((group, cols, width), jnp.bfloat16),
        ],
        compiler_params=PARAMS,
        cost_estimate=pl.CostEstimate(
            flops=8 * rows * 4 * cols * halves * cols * width * 2,
            bytes_accessed=8 * rows * cols * width * halves,
            transcendentals=rows * 4 * cols * cols * halves,
        ),
    )(me, *bias, wo, reach, cap, w, q, g, x, *keys, *values, *raws, *blocks, *filled)


def shards(sizes, pair, pair_mask, gains, w_tri, w_tri_out, w_att, w_bias, w_att_out):
    n_rows, halves = sizes
    rows, cols, width = pair.shape
    heads = w_bias.shape[1]
    lr = edges(pair, pair_mask, gains, w_tri)
    lr = lax.all_to_all(lr, AXES, split_axis=0, concat_axis=0, tiled=True)
    gates = gate(pair, gains, w_tri)
    cap = key_norms(gains[2], w_att[:, width : 2 * width])
    prod = product(lr.reshape(n_rows, halves, 2, rows, cols))
    back = lax.all_to_all(
        prod.reshape(width, rows, cols), AXES, split_axis=0, concat_axis=0, tiled=True
    )
    wb = jnp.pad(w_bias.T, ((0, 8 - heads), (0, 0)))
    mask_flat = pair_mask.astype(jnp.bfloat16).reshape(rows * cols // width, width)
    up = [(y, (y + 1) % halves) for y in range(halves)]
    down = [(y, (y - 1) % halves) for y in range(halves)]
    after, blocks, bias = [], [], []
    for c in range(CHUNKS):
        x, own, b = tri_output(
            back, pair, gates, mask_flat, gains, gains[1][:, None], w_tri_out, wb, heads, c
        )
        prev = lax.ppermute(own, "half", up)
        next_ = lax.ppermute(own, "half", down)
        far = lax.ppermute(prev, "half", up) if c % 2 == 0 else lax.ppermute(next_, "half", down)
        after.append(x)
        blocks.append((own, prev, next_, far))
        bias.append(b)
    inner = n_rows // halves
    swap = [
        ((z * inner + k) * halves + y, (y * inner + k) * halves + z)
        for z in range(halves)
        for k in range(inner)
        for y in range(halves)
    ]
    bias = jnp.swapaxes(jnp.concatenate(bias, axis=0), 0, 1)
    bias = lax.ppermute(bias, AXES, swap)
    first = [project((b[0],), w_att, own=True) for b in blocks]
    bias, first, near = lax.optimization_barrier((bias, first, blocks[0][1:3]))
    blocks[0] = (blocks[0][0], *near, blocks[0][3])
    half_rows = n_rows // 2
    bias = jnp.broadcast_to(bias[None], (half_rows,) + bias.shape)
    cores = [[2 * t + core for t in range(half_rows)] for core in range(2)]
    bias = lax.all_to_all(
        bias, "rows", split_axis=0, concat_axis=0, axis_index_groups=cores, tiled=True
    )
    near = project(blocks[0][1:3], w_att)
    bias, near = lax.optimization_barrier((bias, near))
    other = lax.ppermute(bias, "rows", [(r, r ^ 1) for r in range(n_rows)])
    bias = [v.reshape(halves, inner // 2, heads, rows, cols) for v in (bias, other)]
    *bias, next_ = lax.optimization_barrier((*bias, blocks[1][2]))
    blocks[1] = (*blocks[1][:2], next_, blocks[1][3])

    me = jnp.stack([lax.axis_index("half"), lax.axis_index("rows") & 1]).astype(jnp.int32)
    q, g, top, k, v = first[0]
    out = attention(
        me, bias, w_att_out, top, cap, w_att, q, g, after[0], (k, near[0]), (v, near[1]), blocks[0][3:], blocks[0], 0, []
    )
    rest, out = lax.optimization_barrier((blocks[1][1:], out))
    q, g, top, k, v = first[1]
    return attention(
        me, bias, w_att_out, top, cap, w_att, q, g, after[1], (k,), (v,), rest, (blocks[1][0], *rest), 1, [out]
    )


def solution(mesh):
    sizes = (mesh.shape["rows"], mesh.shape["half"])
    in_specs = (P("rows", "half", None), P("rows", "half"), P(), P(), P(), P(), P(), P())
    out_specs = P("rows", "half", None)
    return jax.shard_map(
        functools.partial(shards, sizes),
        mesh=mesh,
        in_specs=in_specs,
        out_specs=out_specs,
        check_vma=False,
    )
```

```python
import functools

import jax
import jax.numpy as jnp
import numpy as np
from jax import lax
from jax.experimental import pallas as pl
from jax.experimental.pallas import tpu as pltpu
from jax.sharding import PartitionSpec as P

LOG2E = 1.4426950408889634
NEG = -1e30
SAFE = 100.0
AXES = ("rows", "half")
VMEM = pl.BlockSpec(memory_space=pltpu.VMEM)
SMEM = pl.BlockSpec(memory_space=pltpu.SMEM)
PARAMS = pltpu.CompilerParams(vmem_limit_bytes=62 << 20)
CHUNKS = 2


def dot_nn(a, b):
    return lax.dot_general(a, b, (((1,), (0,)), ((), ())), preferred_element_type=jnp.float32)


def dot_nt(a, b):
    return lax.dot_general(a, b, (((1,), (1,)), ((), ())), preferred_element_type=jnp.float32)


def dot_tn(a, b):
    return lax.dot_general(a, b, (((0,), (0,)), ((), ())), preferred_element_type=jnp.float32)


def sigmoid(x):
    return 0.5 * jnp.tanh(0.5 * x) + 0.5


def norm_lanes(x, gain):
    x = x.astype(jnp.float32)
    center = x - jnp.mean(x, axis=-1, keepdims=True)
    spread = jnp.mean(center * center, axis=-1, keepdims=True)
    return (center * lax.rsqrt(spread + 1e-05) * gain).astype(jnp.bfloat16)


def norm_sublanes(x, gain):
    x = x.astype(jnp.float32)
    center = x - jnp.mean(x, axis=0, keepdims=True)
    spread = jnp.mean(center * center, axis=0, keepdims=True)
    return (center * lax.rsqrt(spread + 1e-05) * gain).astype(jnp.bfloat16)


def edges_kernel(pair_ref, mask_ref, gain_ref, w_ref, out_ref, scr, wt_ref):
    group, cols, width = pair_ref.shape
    gain = gain_ref[0:1, :]
    @pl.when(pl.program_id(0) == 0)
    def _():
        wt_ref[...] = w_ref[:, : 4 * width].T

    wt = wt_ref[...]

    def some(t, carry):
        x = pair_ref[pl.ds(t * EDGE_ROWS, EDGE_ROWS)].reshape(EDGE_ROWS * cols, width)
        mixed = dot_nt(wt, norm_lanes(x, gain))
        m = jnp.concatenate(
            [mask_ref[pl.ds(t * EDGE_ROWS + r, 1), :] for r in range(EDGE_ROWS)], axis=1
        ).astype(jnp.float32)
        left = m * sigmoid(mixed[width : 2 * width]) * mixed[:width]
        right = m * sigmoid(mixed[3 * width :]) * mixed[2 * width : 3 * width]
        for e, edge in enumerate((left, right)):
            for r in range(EDGE_ROWS):
                for s in range(cols // 128):
                    at = r * cols + s * 128
                    scr[e, s, pl.ds(t * EDGE_ROWS + r, width, stride=group), :] = edge[:, at : at + 128]
        return carry

    lax.fori_loop(0, group // EDGE_ROWS, some, 0, unroll=EDGE_UNROLL)
    for e in range(2):
        for s in range(cols // 128):
            out_ref[:, e, :, s * 128 : (s + 1) * 128] = (
                scr[e, s].reshape(width, group, 128).astype(jnp.bfloat16)
            )


EDGE_UNROLL = 1
EDGE_ROWS = 8


def edges(pair, mask, gains, w, group=8):
    rows, cols, width = pair.shape
    return pl.pallas_call(
        edges_kernel,
        grid=(rows // group,),
        out_shape=jax.ShapeDtypeStruct((width, 2, rows, cols), jnp.bfloat16),
        in_specs=[
            pl.BlockSpec((group, cols, width), lambda i: (i, 0, 0)),
            pl.BlockSpec((group, cols), lambda i: (i, 0)),
            VMEM,
            VMEM,
        ],
        out_specs=pl.BlockSpec((width, 2, group, cols), lambda i: (0, 0, i, 0)),
        scratch_shapes=[
            pltpu.VMEM((2, cols // 128, width * group, 128), jnp.float32),
            pltpu.VMEM((4 * width, width), jnp.bfloat16),
        ],
        compiler_params=PARAMS,
    )(pair, mask, gains, w)


def gate_kernel(pair_ref, gain_ref, w_ref, out_ref):
    group, cols, width = pair_ref.shape
    normed = norm_lanes(pair_ref[...].reshape(group * cols, width), gain_ref[0:1, :])
    gates = sigmoid(dot_nn(normed, w_ref[:, 4 * width :])).astype(jnp.bfloat16)
    out_ref[...] = gates.reshape(group, cols, width)


def gate(pair, gains, w, group=8):
    rows, cols, width = pair.shape
    block = pl.BlockSpec((group, cols, width), lambda i: (i, 0, 0))
    return pl.pallas_call(
        gate_kernel,
        grid=(rows // group,),
        out_shape=jax.ShapeDtypeStruct(pair.shape, jnp.bfloat16),
        in_specs=[block, VMEM, VMEM],
        out_specs=block,
        compiler_params=PARAMS,
        cost_estimate=pl.CostEstimate(
            flops=6 * rows * cols * width * width,
            bytes_accessed=4 * rows * cols * width,
            transcendentals=rows * cols * width,
        ),
    )(pair, gains, w)


def product_kernel(left_ref, right_ref, out_ref):
    step, halves, _, rows, cols = left_ref.shape
    acc = None
    for h in range(halves):
        left = left_ref[:, h, 0].reshape(step * rows, cols)
        right = right_ref[:, h, 0].reshape(-1, cols)
        part = dot_nt(left, right)
        acc = part if acc is None else acc + part
    for h in range(halves):
        out_ref[:, h] = (
            acc[:, h * cols : (h + 1) * cols].reshape(step, rows, cols).astype(jnp.bfloat16)
        )


def product(lr, tiles=2):
    blocks, halves, _, rows, cols = lr.shape
    step = blocks // tiles
    return pl.pallas_call(
        product_kernel,
        grid=(tiles,),
        out_shape=jax.ShapeDtypeStruct((blocks, halves, rows, cols), jnp.bfloat16),
        in_specs=[
            pl.BlockSpec((step, halves, 1, rows, cols), lambda i: (i, 0, 0, 0, 0)),
            pl.BlockSpec((blocks, halves, 1, rows, cols), lambda i: (0, 0, 1, 0, 0)),
        ],
        out_specs=pl.BlockSpec((step, halves, rows, cols), lambda i: (i, 0, 0, 0)),
        compiler_params=PARAMS,
    )(lr, lr)


OUT_ROWS = 16


def output_kernel(prod_ref, pair_ref, gate_ref, mask_ref, gain_ref, gcol_ref, wo_ref, wb_ref, after_ref, norm_ref, bias_ref, scr):
    width, rows, cols = prod_ref.shape
    heads = bias_ref.shape[1]
    for s in range(cols // 128):
        for c in range(0, width, 16):
            part = prod_ref[c : c + 16, :, s * 128 : (s + 1) * 128].astype(jnp.float32)
            scr[s, c * rows : (c + 16) * rows, :] = part.reshape(16 * rows, 128)

    def some(t, carry):
        i = t * OUT_ROWS
        x = jnp.concatenate(
            [
                scr[s, pl.ds(i + r, width, stride=rows), :]
                for r in range(OUT_ROWS)
                for s in range(cols // 128)
            ],
            axis=1,
        )
        normed = norm_sublanes(x.astype(jnp.bfloat16), gcol_ref[...])
        update = dot_tn(normed, wo_ref[...])
        here = pl.ds(i, OUT_ROWS)
        flat = (OUT_ROWS * cols, width)
        p = pair_ref[here].reshape(flat).astype(jnp.float32)
        after = p + gate_ref[here].reshape(flat).astype(jnp.float32) * update
        after = after.astype(jnp.bfloat16)
        after_ref[here] = after.reshape(OUT_ROWS, cols, width)
        a = norm_lanes(after, gain_ref[2:3, :])
        norm_ref[here] = a.reshape(OUT_ROWS, cols, width)
        bias = (dot_nt(wb_ref[...], a) * LOG2E).astype(jnp.bfloat16)
        for r in range(OUT_ROWS):
            bias_ref[i + r] = bias[:heads, r * cols : (r + 1) * cols]
        return carry

    lax.fori_loop(0, rows // OUT_ROWS, some, 0)
    used = rows * cols // width
    norm_ref[rows, :used, :] = mask_ref[...]
    norm_ref[rows, used:, :] = jnp.zeros((cols - used, width), jnp.bfloat16)


def tri_output(prod, pair, gates, mask_flat, gains, gcol, wo, wb, heads, chunk):
    width, rows, cols = prod.shape
    rows //= CHUNKS
    block = pl.BlockSpec((rows, cols, width), lambda i: (chunk, 0, 0))
    return pl.pallas_call(
        output_kernel,
        grid=(1,),
        out_shape=(
            jax.ShapeDtypeStruct((rows, cols, width), jnp.bfloat16),
            jax.ShapeDtypeStruct((rows + 1, cols, width), jnp.bfloat16),
            jax.ShapeDtypeStruct((rows, heads, cols), jnp.bfloat16),
        ),
        in_specs=[
            pl.BlockSpec((width, rows, cols), lambda i: (0, chunk, 0)),
            block,
            block,
            pl.BlockSpec((rows * cols // width, width), lambda i: (chunk, 0)),
        ]
        + [VMEM] * 4,
        out_specs=(VMEM,) * 3,
        scratch_shapes=[pltpu.VMEM((cols // 128, width * rows, 128), jnp.float32)],
        compiler_params=PARAMS,
    )(prod, pair, gates, mask_flat, gains, gcol, wo, wb)


def project_kernel(own, n, w_ref, *refs):
    xs, refs = refs[:n], refs[n:]
    if own:
        e_ref, q_ref, g_ref, m_ref, *refs = refs
    k_ref, v_ref = refs
    width = w_ref.shape[0]
    group, cols, _ = xs[0].shape
    for b, x_ref in enumerate(xs):
        a = x_ref[...].reshape(group * cols, width)
        at = slice(b * cols, (b + 1) * cols)
        if own:
            mixed = dot_nn(a, w_ref[...])
            scale = LOG2E * HEAD_DIM**-0.5
            q = (mixed[:, :width] * scale).astype(jnp.bfloat16)
            q_ref[...] = q.reshape(q_ref.shape)
            g_ref[...] = sigmoid(mixed[:, 3 * width :]).astype(jnp.bfloat16).reshape(g_ref.shape)
            kv = mixed[:, width : 3 * width].astype(jnp.bfloat16)
            norms = dot_nn(q * q, e_ref[...])
            for r in range(group):
                m = jnp.max(norms[r * cols : (r + 1) * cols], axis=0, keepdims=True)
                m_ref[r] = jnp.broadcast_to(m, m_ref.shape[1:])
        else:
            kv = dot_nn(a, w_ref[:, width : 3 * width]).astype(jnp.bfloat16)
        k_ref[:, at, :] = kv[:, :width].reshape(group, cols, width)
        v_ref[:, at, :] = kv[:, width:].reshape(group, cols, width)


HEAD_DIM = 32
AHEAD = 1


def project(blocks, w, own=False, group=8):
    rows, cols, width = blocks[0].shape
    rows -= 1
    n = len(blocks)
    one = lambda c: pl.BlockSpec((group, c, width), lambda i: (i, 0, 0))
    shape = lambda c: jax.ShapeDtypeStruct((rows, c, width), jnp.bfloat16)
    extra, shapes, specs = [], [], []
    if own:
        lanes = np.arange(width) // HEAD_DIM
        extra = [jnp.asarray(lanes[:, None] == lanes[None, :], jnp.bfloat16)]
        shapes = [shape(cols), shape(cols), jax.ShapeDtypeStruct((rows, 8, width), jnp.float32)]
        specs = [one(cols), one(cols), one(8)]
    return pl.pallas_call(
        functools.partial(project_kernel, own, n),
        grid=(rows // group,),
        out_shape=shapes + [shape(n * cols), shape(n * cols)],
        in_specs=[VMEM] + [one(cols)] * n + [VMEM] * len(extra),
        out_specs=specs + [one(n * cols), one(n * cols)],
        compiler_params=PARAMS,
        cost_estimate=pl.CostEstimate(
            flops=8 * n * rows * cols * width * width,
            bytes_accessed=8 * n * rows * cols * width,
            transcendentals=rows * cols * width,
        ),
    )(w, *blocks, *extra)


def key_norms(gain, w_keys):
    width = w_keys.shape[0]
    parts = (gain[:, None] * w_keys.astype(jnp.float32)).reshape(width, -1, HEAD_DIM)
    gram = jnp.einsum("chd,che->hde", parts, parts, precision=lax.Precision.HIGHEST)
    top = jnp.max(jnp.sum(jnp.abs(gram), axis=2), axis=1)
    return jnp.repeat(1.05 * jnp.sqrt(width * top), HEAD_DIM)[None, :]


def attention_kernel(halves, pieces, raw, me_ref, bias_a_ref, bias_b_ref, wo_ref, reach_ref, cap_ref, wa_ref, *refs):
    q_ref, g_ref, x_ref = refs[:3]
    k_refs, v_refs = refs[3 : 3 + pieces], refs[3 + pieces : 3 + 2 * pieces]
    refs = refs[3 + 2 * pieces :]
    raws, masks = refs[:raw], refs[raw : raw + halves]
    out_ref, flags, mrow, ks, vs, b32, gated = refs[-7:]
    i = pl.program_id(0)
    group, cols, width = q_ref.shape
    _, outer, heads, sub, _ = bias_a_ref.shape
    lane = lax.broadcasted_iota(jnp.int32, (1, width), 1)
    me = me_ref[0]
    where = [lax.rem(me + s, halves) for s in (0, halves - 1, 1, 2)]
    step = cols // 128
    count = mrow.shape[1] // step

    @pl.when(i == 0)
    def _():
        top = jnp.zeros((sub, cols), jnp.float32)
        for s, w in enumerate(where):

            def put(t, top, s=s, w=w):
                for p, piece in enumerate((bias_a_ref, bias_b_ref)):
                    core = me_ref[1] if p == 0 else 1 - me_ref[1]
                    j = pl.ds(pl.multiple_of((2 * t + core) * sub, sub), sub)
                    for h in range(heads):
                        b = piece[w, t, h].astype(jnp.float32)
                        b32[h, j, s * cols : (s + 1) * cols] = b
                        top = jnp.maximum(top, jnp.abs(b))
                return top

            top = lax.fori_loop(0, outer, put, top)
        norms = jnp.max(reach_ref[...], axis=0)
        bound = jnp.max(jnp.sqrt(norms) * cap_ref[...]) * 1.02 + jnp.max(top)
        flags[0] = (bound < SAFE).astype(jnp.int32)
        for s in range(halves):
            mrow[s] = masks[s][0, : mrow.shape[1], :].astype(jnp.float32)
        least = None
        seen = jnp.max(mrow[...], axis=0)
        for r in range(count):
            u = jnp.max(seen[r * step : (r + 1) * step], keepdims=True)
            least = u if least is None else jnp.minimum(least, u)
        flags[1] = (jnp.max(least) > 0.0).astype(jnp.int32)
        vs[:, :, width:] = jnp.ones((group, vs.shape[1], width), jnp.bfloat16)

    def mask_line(r):
        at = (i * group + r) * step
        return jnp.concatenate(
            [mrow[s, pl.ds(at + t, 1), :] for s in range(halves) for t in range(step)], axis=1
        )

    def finish(r, attended):
        gated[r] = (attended * g_ref[r].astype(jnp.float32)).astype(jnp.bfloat16)

    def attend(shift):
        def score(r, h):
            q = q_ref[r]
            on = jnp.broadcast_to(lane // (width // heads) == h, q.shape)
            qm = jnp.where(on, q, jnp.zeros_like(q))
            keys = [k[r] for k in k_refs] + [ks[r]]
            scores = jnp.concatenate([dot_nt(qm, k) for k in keys], axis=1)
            return scores + b32[h] + jnp.where(mask_line(r) > 0.0, 0.0, NEG)

        done = sum(v.shape[1] for v in v_refs)
        for n, x in enumerate(raws):
            kv = dot_nn(x[...].reshape(group * cols, width), wa_ref[:, width : 3 * width])
            kv = kv.astype(jnp.bfloat16)
            ks[:, n * cols : (n + 1) * cols, :] = kv[:, :width].reshape(group, cols, width)
            at = done + n * cols
            vs[:, at : at + cols, :width] = kv[:, width:].reshape(group, cols, width)
        order = [(r, h) for r in range(group) for h in range(heads)]
        ahead = [score(*order[t]) for t in range(AHEAD)]
        for t, (r, h) in enumerate(order):
            if t + AHEAD < len(order):
                ahead.append(score(*order[t + AHEAD]))
            scores = ahead.pop(0)
            if h == 0:
                at = 0
                for v in v_refs:
                    vs[r, at : at + v.shape[1], :width] = v[r]
                    at += v.shape[1]
                num = jnp.zeros((cols, width), jnp.float32)
                den = jnp.ones((cols, width), jnp.float32)
            if shift:
                scores = scores - jnp.max(scores, axis=-1, keepdims=True)
            weights = jnp.exp2(scores).astype(jnp.bfloat16)
            both = dot_nn(weights, vs[r])
            on = lane // (width // heads) == h
            num = jnp.where(on, both[:, :width], num)
            den = jnp.where(on, both[:, width:], den)
            if h == heads - 1:
                finish(r, num / den)

    @pl.when(flags[0] > 0)
    def _():
        attend(False)

    @pl.when(flags[0] == 0)
    def _():
        attend(True)

    @pl.when(flags[1] == 0)
    def _():
        for r in range(group):
            used = jnp.max(mask_line(r), keepdims=True) > 0.0
            mean = jnp.mean(vs[r, :, :width].astype(jnp.float32), axis=0, keepdims=True)
            plain = mean * g_ref[r].astype(jnp.float32)
            gated[r] = jnp.where(used, gated[r].astype(jnp.float32), plain).astype(jnp.bfloat16)

    flat = (group * cols, width)
    out = dot_nn(gated[...].reshape(flat), wo_ref[...])
    out = x_ref[...].reshape(flat).astype(jnp.float32) + out
    out_ref[...] = out.astype(jnp.bfloat16).reshape(out_ref.shape)


def attention(me, bias, wo, reach, cap, w, q, g, x, keys, values, raws, blocks, chunk, filled, group=4):
    halves, _, heads, _, _ = bias[0].shape
    rows, cols, width = q.shape
    one = lambda c: pl.BlockSpec((group, c, width), lambda i: (i, 0, 0))
    last = pl.BlockSpec((1, cols, width), lambda i: (rows, 0, 0))
    pieces = len(keys)
    return pl.pallas_call(
        functools.partial(attention_kernel, halves, pieces, len(raws)),
        grid=(rows // group,),
        out_shape=jax.ShapeDtypeStruct((CHUNKS * rows, cols, width), jnp.bfloat16),
        in_specs=[SMEM] + [VMEM] * 6
        + [one(cols)] * 3
        + [one(k.shape[1]) for k in keys] * 2
        + [one(cols)] * len(raws)
        + [last] * halves
        + [pl.BlockSpec(memory_space=pl.ANY)] * len(filled),
        out_specs=pl.BlockSpec((group, cols, width), lambda i: (chunk * (rows // group) + i, 0, 0)),
        input_output_aliases={10 + 2 * pieces + len(raws) + halves: 0} if filled else {},
        scratch_shapes=[
            pltpu.SMEM((2,), jnp.int32),
            pltpu.VMEM((halves, rows * cols // 128, 128), jnp.float32),
            pltpu.VMEM((group, len(raws) * cols, width), jnp.bfloat16),
            pltpu.VMEM((group, halves * cols, 2 * width), jnp.bfloat16),
            pltpu.VMEM((heads, cols, halves * cols), jnp.float32),
            pltpu.VMEM((group, cols, width), jnp.bfloat16),
        ],
        compiler_params=PARAMS,
        cost_estimate=pl.CostEstimate(
            flops=8 * rows * 4 * cols * halves * cols * width * 2,
            bytes_accessed=8 * rows * cols * width * halves,
            transcendentals=rows * 4 * cols * cols * halves,
        ),
    )(me, *bias, wo, reach, cap, w, q, g, x, *keys, *values, *raws, *blocks, *filled)


def shards(sizes, pair, pair_mask, gains, w_tri, w_tri_out, w_att, w_bias, w_att_out):
    n_rows, halves = sizes
    rows, cols, width = pair.shape
    heads = w_bias.shape[1]
    lr = edges(pair, pair_mask, gains, w_tri)
    lr = lax.all_to_all(lr, AXES, split_axis=0, concat_axis=0, tiled=True)
    gates = gate(pair, gains, w_tri)
    cap = key_norms(gains[2], w_att[:, width : 2 * width])
    prod = product(lr.reshape(n_rows, halves, 2, rows, cols))
    back = lax.all_to_all(
        prod.reshape(width, rows, cols), AXES, split_axis=0, concat_axis=0, tiled=True
    )
    wb = jnp.pad(w_bias.T, ((0, 8 - heads), (0, 0)))
    mask_flat = pair_mask.astype(jnp.bfloat16).reshape(rows * cols // width, width)
    up = [(y, (y + 1) % halves) for y in range(halves)]
    down = [(y, (y - 1) % halves) for y in range(halves)]
    after, blocks, bias = [], [], []
    for c in range(CHUNKS):
        x, own, b = tri_output(
            back, pair, gates, mask_flat, gains, gains[1][:, None], w_tri_out, wb, heads, c
        )
        prev = lax.ppermute(own, "half", up)
        next_ = lax.ppermute(own, "half", down)
        far = lax.ppermute(prev, "half", up) if c % 2 == 0 else lax.ppermute(next_, "half", down)
        after.append(x)
        blocks.append((own, prev, next_, far))
        bias.append(b)
    inner = n_rows // halves
    swap = [
        ((z * inner + k) * halves + y, (y * inner + k) * halves + z)
        for z in range(halves)
        for k in range(inner)
        for y in range(halves)
    ]
    bias = jnp.swapaxes(jnp.concatenate(bias, axis=0), 0, 1)
    bias = lax.ppermute(bias, AXES, swap)
    first = [project((b[0],), w_att, own=True) for b in blocks]
    bias, first, near = lax.optimization_barrier((bias, first, blocks[0][1:3]))
    blocks[0] = (blocks[0][0], *near, blocks[0][3])
    half_rows = n_rows // 2
    bias = jnp.broadcast_to(bias[None], (half_rows,) + bias.shape)
    cores = [[2 * t + core for t in range(half_rows)] for core in range(2)]
    bias = lax.all_to_all(
        bias, "rows", split_axis=0, concat_axis=0, axis_index_groups=cores, tiled=True
    )
    near = project(blocks[0][1:3], w_att)
    bias, near = lax.optimization_barrier((bias, near))
    other = lax.ppermute(bias, "rows", [(r, r ^ 1) for r in range(n_rows)])
    bias = [v.reshape(halves, inner // 2, heads, rows, cols) for v in (bias, other)]
    *bias, next_ = lax.optimization_barrier((*bias, blocks[1][2]))
    blocks[1] = (*blocks[1][:2], next_, blocks[1][3])

    me = jnp.stack([lax.axis_index("half"), lax.axis_index("rows") & 1]).astype(jnp.int32)
    q, g, top, k, v = first[0]
    out = attention(
        me, bias, w_att_out, top, cap, w_att, q, g, after[0], (k, near[0]), (v, near[1]), blocks[0][3:], blocks[0], 0, []
    )
    rest, out = lax.optimization_barrier((blocks[1][1:], out))
    q, g, top, k, v = first[1]
    return attention(
        me, bias, w_att_out, top, cap, w_att, q, g, after[1], (k,), (v,), rest, (blocks[1][0], *rest), 1, [out]
    )


def solution(mesh):
    sizes = (mesh.shape["rows"], mesh.shape["half"])
    in_specs = (P("rows", "half", None), P("rows", "half"), P(), P(), P(), P(), P(), P())
    out_specs = P("rows", "half", None)
    return jax.shard_map(
        functools.partial(shards, sizes),
        mesh=mesh,
        in_specs=in_specs,
        out_specs=out_specs,
        check_vma=False,
    )
```
